256 devices in a mesh: dom: 32 (over z_lo, y, core), rep: 8 (over x, z_hi).
Axes of the slice: x: 4, y: 4, z: 8 (z_hi: 2, z_lo: 4; z = z_hi * 4 + z_lo), core: 2. Of those that a mesh axis runs over, the one named last changes fastest.
Arguments:
- entity: float32 [65536, 256], P(('dom', 'rep'))
- entity_accum: float32 [65536], P(('dom', 'rep')), may hold values from 0.5 to 50
- relation: float32 [4, 256, 256], replicated, may hold values from -0.375 to 0.375
- relation_accum: float32 [4, 256], replicated, may hold values from 0.01 to 1
- src_index: int32 [1024000], P(('dom', 'rep')), may hold values from 0 to 2047
- dst_index: int32 [1024000], P(('dom', 'rep')), may hold values from 0 to 2047
- neg_index: int32 [1024, 1000], P(('dom', 'rep')), may hold values from 0 to 2047
- rel_id: int32 [1024], P(('dom', 'rep')), may hold values from 0 to 3
- counts: int32 [256], P(('dom', 'rep')), may hold values from 1000 to 4000, as said below
Outputs:
- entity_new: float32 [65536, 256], P(('dom', 'rep'))
- entity_accum_new: float32 [65536], P(('dom', 'rep'))
- relation_new: float32 [4, 256, 256], replicated
- relation_accum_new: float32 [4, 256], replicated
The draws below stay inside these ranges and needn't reach their ends.
Inputs may be any that keep to these rules, and one draw needn't show every extreme that they name: `counts`: one block of 4000 slots has all slots live in every draw.
All inputs are finite; a program needn't handle non-finite values.
Results may differ from the reference program's by a relative error of at most 0.0047.
Values may be sent and summed in bfloat16 or wider, within the bound.
No kernel may reach another device: no remote copies, remote signals or barrier semaphores. Data moves between devices by JAX's collectives and lax.ppermute only.
A program may use at most 128 MiB of HBM per device.

```python
import math
import jax
import jax.numpy as jnp
from jax import lax

D = 256
NEG = 1000
REL = 4
GROUPS_DEV = 4
P_ROWS = 2048
ENTITIES = 65536
E_DEV = 4000
EDGES = 1024000
GROUPS_ALL = 1024
N_DOM = 32
N_REP = 8
DEVICES = 256


def draw_entity(key, part):
    key = jax.random.fold_in(key, 1)
    first = jax.random.fold_in(key, 0)
    return 0.4 * jax.random.normal(first, (ENTITIES, D), jnp.float32)


def draw_entity_accum(key, part):
    key = jax.random.fold_in(key, 2)
    return jnp.exp(jax.random.uniform(key, (ENTITIES,), jnp.float32, math.log(0.5), math.log(50.0)))


def draw_counts(key, part):
    key = jax.random.fold_in(key, 5)
    first, second = jax.random.split(key)
    values = jax.random.randint(first, (DEVICES,), E_DEV // 4, E_DEV + 1, jnp.int32)
    chosen = jax.random.randint(second, (), 0, DEVICES, jnp.int32)
    return jnp.where(jnp.arange(DEVICES, dtype=jnp.int32) == chosen, E_DEV, values).astype(jnp.int32)


def place_ends(values, own_key, smallest, high):
    shape = values.shape
    place = [jax.random.randint(jax.random.fold_in(own_key, axis), (), 0, shape[axis]) for axis in range(len(shape))]
    values = values.at[tuple(place)].set(smallest)
    longest = shape.index(max(shape))
    place[longest] = (place[longest] + 1) % shape[longest]
    return values.at[tuple(place)].set(high)


def centred(rng, extent, width, bound, kind=jnp.bfloat16):
    values = width * jax.random.normal(rng, extent, jnp.float32)
    return jnp.clip(values, min=-bound, max=bound).astype(kind)


def setup_inputs(seed: int = 0) -> dict:
    keys = jax.random.split(jax.random.key(seed), 10)
    return {
        "entity": draw_entity(jax.random.fold_in(keys[9], 71), 0),
        "entity_accum": draw_entity_accum(jax.random.fold_in(keys[9], 71), 0),
        "relation": centred(keys[2], (REL, D, D), D ** -0.5, 0.375, jnp.float32),
        "relation_accum": jnp.clip(jnp.exp(jax.random.uniform(keys[3], (REL, D), jnp.float32, math.log(0.01), math.log(1.0))), 0.01, 1.0),
        "src_index": place_ends(jax.random.randint(keys[4], (EDGES,), 0, P_ROWS), jax.random.fold_in(keys[4], 1), 0, P_ROWS - 1).astype(jnp.int32),
        "dst_index": place_ends(jax.random.randint(keys[5], (EDGES,), 0, P_ROWS), jax.random.fold_in(keys[5], 1), 0, P_ROWS - 1).astype(jnp.int32),
        "neg_index": place_ends(jax.random.randint(keys[6], (GROUPS_ALL, NEG), 0, P_ROWS), jax.random.fold_in(keys[6], 1), 0, P_ROWS - 1).astype(jnp.int32),
        "rel_id": place_ends(jax.random.randint(keys[7], (GROUPS_ALL,), 0, REL), jax.random.fold_in(keys[7], 1), 0, REL - 1).astype(jnp.int32),
        "counts": draw_counts(jax.random.fold_in(keys[9], 71), 0),
    }


learn_rate = 0.1

def bucket_grads(src_block, dst_block, rel_b, src_idx, dst_idx, neg_idx, group_rel, count):
    groups = neg_idx.shape[0]
    srcs = src_block[src_idx].reshape(groups, -1, D)
    mats = rel_b[group_rel]
    q = jnp.einsum('cnd,cde->cne', srcs.astype(jnp.float32), mats.astype(jnp.float32)).astype(jnp.bfloat16)
    tgt = dst_block[dst_idx].reshape(q.shape)
    negs = dst_block[neg_idx]
    qf = q.astype(jnp.float32)
    pos = lax.optimization_barrier(jnp.sum(qf * tgt.astype(jnp.float32), -1))
    neg = jnp.einsum('cnd,cmd->cnm', qf, negs.astype(jnp.float32))
    top = jnp.maximum(pos, lax.optimization_barrier(jnp.max(neg, -1)))
    epos = jnp.exp(pos - top)
    eneg = jnp.exp(neg - top[..., None])
    total = epos + lax.optimization_barrier(jnp.sum(eneg, -1))
    slot = jnp.arange(src_idx.shape[0], dtype=jnp.int32).reshape(groups, -1)
    live = (slot < count).astype(jnp.float32)
    gpos = (epos / total - 1.0) * live
    gneg = (eneg / total[..., None] * live[..., None]).astype(jnp.bfloat16)
    gq = gpos[..., None] * tgt.astype(jnp.float32) + jnp.einsum('cnm,cmd->cnd', gneg.astype(jnp.float32), negs.astype(jnp.float32))
    gq = gq.astype(jnp.bfloat16)
    gqf = gq.astype(jnp.float32)
    grad_tgt = gpos[..., None] * qf
    grad_neg = jnp.einsum('cnm,cnd->cmd', gneg.astype(jnp.float32), qf)
    grad_src = jnp.einsum('cne,cde->cnd', gqf, mats.astype(jnp.float32))
    per_group = jnp.einsum('cnd,cne->cde', srcs.astype(jnp.float32), gqf)
    src_grad = jnp.zeros((src_block.shape[0], D), jnp.float32).at[src_idx].add(grad_src.reshape(-1, D))
    dst_grad = jnp.zeros((dst_block.shape[0], D), jnp.float32).at[dst_idx].add(grad_tgt.reshape(-1, D))
    dst_grad = dst_grad.at[neg_idx.reshape(-1)].add(grad_neg.reshape(-1, D))
    rel_grad = jnp.zeros((REL, D, D), jnp.float32).at[group_rel].add(per_group)
    return (src_grad, dst_grad, rel_grad)

def rowwise(param, accum, grad):
    fresh = accum + lax.optimization_barrier(jnp.mean(grad * grad, -1))
    return (param - learn_rate * grad / jnp.sqrt(fresh)[..., None], fresh)

def reference(entity, entity_accum, relation, relation_accum, src_index, dst_index, neg_index, rel_id, counts):
    ent_b = entity.astype(jnp.bfloat16)
    rel_b = relation.astype(jnp.bfloat16)
    slots = E_DEV

    def step(index, carry):
        grads, rgrad = carry
        index = jnp.asarray(index).astype(jnp.int32)
        part = index // N_REP
        nxt = (part + 1) % N_DOM
        src_block = lax.dynamic_slice_in_dim(ent_b, part * P_ROWS, P_ROWS, 0)
        dst_block = lax.dynamic_slice_in_dim(ent_b, nxt * P_ROWS, P_ROWS, 0)
        s_idx = lax.dynamic_slice_in_dim(src_index, index * slots, slots, 0)
        d_idx = lax.dynamic_slice_in_dim(dst_index, index * slots, slots, 0)
        n_idx = lax.dynamic_slice_in_dim(neg_index, index * GROUPS_DEV, GROUPS_DEV, 0)
        c_rel = lax.dynamic_slice_in_dim(rel_id, index * GROUPS_DEV, GROUPS_DEV, 0)
        count = counts[index]
        sg, dg, rg = bucket_grads(src_block, dst_block, rel_b, s_idx, d_idx, n_idx, c_rel, count)
        old = lax.dynamic_slice_in_dim(grads, part * P_ROWS, P_ROWS, 0)
        grads = lax.dynamic_update_slice_in_dim(grads, old + sg, part * P_ROWS, 0)
        old = lax.dynamic_slice_in_dim(grads, nxt * P_ROWS, P_ROWS, 0)
        grads = lax.dynamic_update_slice_in_dim(grads, old + dg, nxt * P_ROWS, 0)
        return (grads, rgrad + rg)
    start = (jnp.zeros((ENTITIES, D), jnp.float32), jnp.zeros((REL, D, D), jnp.float32))
    grads, rgrad = lax.fori_loop(0, N_DOM * N_REP, step, start)
    entity_new, entity_accum_new = rowwise(entity, entity_accum, grads)
    relation_new, relation_accum_new = rowwise(relation, relation_accum, rgrad)
    return (entity_new, entity_accum_new, relation_new, relation_accum_new)
```

```python
import functools
import jax
import jax.numpy as jnp
from jax import lax
from jax.experimental import pallas as pl
from jax.experimental.pallas import tpu as pltpu
from jax.sharding import PartitionSpec as P

learn_rate = 0.1
LOG2E = 1.4426950408889634
GROUPS = 4
SLOTS = 1000
PAD = 1024
ROWS = 2048
D = 256
BLK = 256
NBLK = ROWS // BLK
CH = 512
NCH = GROUPS * PAD // CH
PER = PAD // CH
bf16 = jnp.bfloat16
f32 = jnp.float32

NN = (((1,), (0,)), ((), ()))
NT = (((1,), (1,)), ((), ()))
MB = 1024 * 1024


def mm(a, b, dims=NN):
    return lax.dot_general(a, b, dims, preferred_element_type=f32)


def params():
    return pltpu.CompilerParams(
        dimension_semantics=("arbitrary",), vmem_limit_bytes=48 * MB
    )


def count_kernel(neg_ref, out_ref):
    rows = lax.broadcasted_iota(jnp.int32, (BLK, PAD), 0)

    def body(b, carry):
        hits = jnp.where(rows == neg_ref[0] - b * BLK, 1.0, 0.0)
        count = jnp.sum(hits, axis=1, keepdims=True)
        at = pl.ds(pl.multiple_of(b * BLK, BLK), BLK)
        out_ref[0, at, 0:1] = jnp.log2(count)
        out_ref[0, at, 1:2] = jnp.log2(count + 1.0)
        return carry

    lax.fori_loop(0, NBLK, body, 0)


def neg_weights(neg_pad):
    return pl.pallas_call(
        count_kernel,
        grid=(GROUPS,),
        in_specs=[pl.BlockSpec((1, 1, PAD), lambda g: (g, 0, 0))],
        out_specs=pl.BlockSpec((1, ROWS, 2), lambda g: (g, 0, 0)),
        out_shape=jax.ShapeDtypeStruct((GROUPS, ROWS, 2), f32),
        compiler_params=params(),
        name="neg_weights",
    )(neg_pad.reshape(GROUPS, 1, PAD))


def query_kernel(rel_ref, own_ref, idx_ref, mat_ref, s_ref, q_ref):
    cols = lax.broadcasted_iota(jnp.int32, (CH, BLK), 1)
    acc = jnp.zeros((CH, D), f32)
    for b in range(NBLK):
        hot = jnp.where(cols == idx_ref[...] - b * BLK, 1.0, 0.0).astype(bf16)
        acc = acc + mm(hot, own_ref[b * BLK : (b + 1) * BLK, :])
    rows = acc.astype(bf16)
    s_ref[...] = rows
    q_ref[...] = mm(mat_ref[0], rows, NT).astype(bf16)


def make_queries(own, src_col, rel_id, rel_t):
    return pl.pallas_call(
        query_kernel,
        grid_spec=pltpu.PrefetchScalarGridSpec(
            num_scalar_prefetch=1,
            grid=(NCH,),
            in_specs=[
                pl.BlockSpec((ROWS, D), lambda j, rel: (0, 0)),
                pl.BlockSpec((CH, 1), lambda j, rel: (j, 0)),
                pl.BlockSpec((1, D, D), lambda j, rel: (rel[j // PER], 0, 0)),
            ],
            out_specs=[
                pl.BlockSpec((CH, D), lambda j, rel: (j, 0)),
                pl.BlockSpec((D, CH), lambda j, rel: (0, j)),
            ],
        ),
        out_shape=[
            jax.ShapeDtypeStruct((GROUPS * PAD, D), bf16),
            jax.ShapeDtypeStruct((D, GROUPS * PAD), bf16),
        ],
        compiler_params=params(),
        name="queries",
    )(rel_id, own, src_col, rel_t)


def score_kernel(
    rel_ref, cnt_ref, nxt_ref, nxt_t_ref, q_ref, s_ref, dst_ref, wt_ref,
    gq_ref, dg_ref, rg_ref, sc, w, dacc,
):
    j = pl.program_id(0)
    kind = rel_ref[j // PER]

    @pl.when(j == 0)
    def _():
        dacc[...] = jnp.zeros_like(dacc)
        rg_ref[...] = jnp.zeros_like(rg_ref)

    dst = dst_ref[0]
    rows = lax.broadcasted_iota(jnp.int32, (BLK, CH), 0)
    top = jnp.full((8, CH), -jnp.inf, f32)
    hit = jnp.zeros((8, CH), f32)
    for b in range(NBLK):
        at = slice(b * BLK, (b + 1) * BLK)
        raw = mm(nxt_ref[at, :], q_ref[...])
        mask = rows == dst - b * BLK
        val = raw * LOG2E + jnp.where(mask, wt_ref[0, at, 1:2], wt_ref[0, at, 0:1])
        sc[at, :] = val
        top = jnp.maximum(top, jnp.max(val.reshape(BLK // 8, 8, CH), axis=0))
        hit = hit + jnp.sum(jnp.where(mask, val, 0.0).reshape(BLK // 8, 8, CH), axis=0)
    top = jnp.max(top, axis=0, keepdims=True)
    hit = jnp.sum(hit, axis=0, keepdims=True)
    tot = jnp.zeros((8, CH), f32)
    for b in range(NBLK):
        at = slice(b * BLK, (b + 1) * BLK)
        e = jnp.exp2(sc[at, :] - top)
        tot = tot + jnp.sum(e.reshape(BLK // 8, 8, CH), axis=0)
        w[at, :] = e.astype(bf16)
    tot = jnp.sum(tot, axis=0, keepdims=True)
    gain = (jnp.exp2(hit - top) - tot).astype(bf16)
    lane = lax.broadcasted_iota(jnp.int32, (1, CH), 1) + lax.rem(j, PER) * CH
    slot = (j // PER) * SLOTS + lane
    live = jnp.logical_and(lane < SLOTS, slot < cnt_ref[0])
    scale = jnp.where(live, 1.0 / tot, 0.0)
    for b in range(NBLK):
        at = slice(b * BLK, (b + 1) * BLK)
        mask = rows == dst - b * BLK
        w[at, :] = jnp.where(mask, gain.astype(f32), w[at, :].astype(f32)).astype(bf16)
    gq = (mm(nxt_t_ref[...], w[...]) * scale).astype(bf16)
    gq_ref[...] = gq
    rg_ref[kind] += mm(gq, s_ref[...])
    qs = (q_ref[...].astype(f32) * scale).astype(bf16)
    for b in range(NBLK):
        at = slice(b * BLK, (b + 1) * BLK)
        dacc[at, :] += mm(w[at, :], qs, NT)

    @pl.when(j == NCH - 1)
    def _():
        dg_ref[...] = dacc[...].astype(bf16)


def score_side(nxt, nxt_t, q, s, dst_rows, weights, rel_id, counts, kinds):
    return pl.pallas_call(
        score_kernel,
        grid_spec=pltpu.PrefetchScalarGridSpec(
            num_scalar_prefetch=2,
            grid=(NCH,),
            in_specs=[
                pl.BlockSpec((ROWS, D), lambda j, rel, cnt: (0, 0)),
                pl.BlockSpec((D, ROWS), lambda j, rel, cnt: (0, 0)),
                pl.BlockSpec((D, CH), lambda j, rel, cnt: (0, j)),
                pl.BlockSpec((CH, D), lambda j, rel, cnt: (j, 0)),
                pl.BlockSpec((1, 1, CH), lambda j, rel, cnt: (j, 0, 0)),
                pl.BlockSpec((1, ROWS, 2), lambda j, rel, cnt: (j // PER, 0, 0)),
            ],
            out_specs=[
                pl.BlockSpec((D, CH), lambda j, rel, cnt: (0, j)),
                pl.BlockSpec((ROWS, D), lambda j, rel, cnt: (0, 0)),
                pl.BlockSpec((kinds, D, D), lambda j, rel, cnt: (0, 0, 0)),
            ],
            scratch_shapes=[
                pltpu.VMEM((ROWS, CH), f32),
                pltpu.VMEM((ROWS, CH), bf16),
                pltpu.VMEM((ROWS, D), f32),
            ],
        ),
        out_shape=[
            jax.ShapeDtypeStruct((D, GROUPS * PAD), bf16),
            jax.ShapeDtypeStruct((ROWS, D), bf16),
            jax.ShapeDtypeStruct((kinds, D, D), f32),
        ],
        compiler_params=params(),
        name="scores",
    )(rel_id, counts, nxt, nxt_t, q, s, dst_rows, weights)


def source_kernel(rel_ref, gq_ref, src_ref, mat_ref, out_ref, acc):
    j = pl.program_id(0)

    @pl.when(j == 0)
    def _():
        acc[...] = jnp.zeros_like(acc)

    grad = mm(mat_ref[0], gq_ref[...]).astype(bf16)
    rows = lax.broadcasted_iota(jnp.int32, (BLK, CH), 0)
    for b in range(NBLK):
        at = slice(b * BLK, (b + 1) * BLK)
        hot = jnp.where(rows == src_ref[0] - b * BLK, 1.0, 0.0).astype(bf16)
        acc[at, :] += mm(hot, grad, NT)

    @pl.when(j == NCH - 1)
    def _():
        out_ref[...] = acc[...].astype(bf16)


def source_side(gq, src_rows, rel_id, rel_b):
    return pl.pallas_call(
        source_kernel,
        grid_spec=pltpu.PrefetchScalarGridSpec(
            num_scalar_prefetch=1,
            grid=(NCH,),
            in_specs=[
                pl.BlockSpec((D, CH), lambda j, rel: (0, j)),
                pl.BlockSpec((1, 1, CH), lambda j, rel: (j, 0, 0)),
                pl.BlockSpec((1, D, D), lambda j, rel: (rel[j // PER], 0, 0)),
            ],
            out_specs=pl.BlockSpec((ROWS, D), lambda j, rel: (0, 0)),
            scratch_shapes=[pltpu.VMEM((ROWS, D), f32)],
        ),
        out_shape=jax.ShapeDtypeStruct((ROWS, D), bf16),
        compiler_params=params(),
        name="source_grads",
    )(rel_id, gq, src_rows, rel_b)


def rowwise(param, accum, grad):
    fresh = accum + jnp.mean(grad * grad, -1)
    return (param - learn_rate * grad / jnp.sqrt(fresh)[..., None], fresh)


def shift_dom(block, by):
    size = lax.axis_size("dom")
    return lax.ppermute(block, "dom", [(i, (i + by) % size) for i in range(size)])


def swap_z(block):
    return lax.ppermute(block, "rep", [(i, i ^ 1) for i in range(8)])


def shift_x(block, by):
    return lax.ppermute(block, "rep", [(i, (i + 2 * by) % 8) for i in range(8)])


def gather_part(shard):
    rep = lax.axis_index("rep")
    z, x = rep % 2, rep // 2
    other = swap_z(shard)
    pair = jnp.where(z == 0, jnp.concatenate([shard, other]), jnp.concatenate([other, shard]))
    parts = jnp.stack([pair] + [shift_x(pair, -k) for k in (1, 2, 3)])
    order = (jnp.arange(4) - x) % 4
    return parts[order].reshape(-1, shard.shape[-1])


def reduce_part(grad):
    rep = lax.axis_index("rep")
    z = rep % 2
    pieces = grad.reshape(4, 512, D)
    got = lax.all_to_all(pieces, "rep", 0, 0, axis_index_groups=[[0, 2, 4, 6], [1, 3, 5, 7]])
    total = jnp.sum(got.astype(f32), 0).reshape(2, 256, D)
    mine = lax.dynamic_index_in_dim(total, z, 0, False)
    give = lax.dynamic_index_in_dim(total, 1 - z, 0, False)
    return mine + swap_z(give.astype(bf16)).astype(f32)


def reduce_relation(rel_t):
    kinds = rel_t.shape[0]
    part = rel_t.transpose(0, 2, 1).reshape(32, -1, D).astype(bf16)
    got = lax.all_to_all(part, "dom", 0, 0)
    mine = jnp.sum(got.astype(f32), 0)
    every = lax.all_to_all(jnp.broadcast_to(mine, (8,) + mine.shape), "rep", 0, 0)
    total = jnp.sum(every, 0)
    full = lax.all_to_all(jnp.broadcast_to(total, (32,) + total.shape), "dom", 0, 0)
    return full.reshape(kinds, D, D)


def pad_slots(index, fill):
    return jnp.pad(index.reshape(GROUPS, SLOTS), ((0, 0), (0, PAD - SLOTS)), constant_values=fill)


def on_device(
    entity, entity_accum, relation, relation_accum, src_index, dst_index, neg_index, rel_id, counts
):
    ent_b = entity.astype(bf16)
    rel_b = relation.astype(bf16)
    rel_t = rel_b.transpose(0, 2, 1)
    shifted = shift_dom(ent_b, -1)
    own = gather_part(ent_b)
    nxt = gather_part(shifted)
    src_pad = pad_slots(src_index, -1)
    dst_pad = pad_slots(dst_index, -1)
    weights = neg_weights(pad_slots(neg_index, -1))
    s, q = make_queries(own, src_pad.reshape(-1, 1), rel_id, rel_t)
    gq, dst_grad, rel_grad = score_side(
        nxt, nxt.T, q, s, dst_pad.reshape(NCH, 1, CH), weights, rel_id, counts, relation.shape[0]
    )
    moved = shift_dom(dst_grad, 1)
    src_grad = source_side(gq, src_pad.reshape(NCH, 1, CH), rel_id, rel_b)
    both = (src_grad.astype(f32) + moved.astype(f32)).astype(bf16)
    grads = reduce_part(both)
    rel_total = reduce_relation(rel_grad)
    entity_new, entity_accum_new = rowwise(entity, entity_accum, grads)
    relation_new, relation_accum_new = rowwise(relation, relation_accum, rel_total)
    return (entity_new, entity_accum_new, relation_new, relation_accum_new)


def solution(mesh):
    placed = (
        P(("dom", "rep"), None),
        P(("dom", "rep")),
        P(),
        P(),
        P(("dom", "rep")),
        P(("dom", "rep")),
        P(("dom", "rep"), None),
        P(("dom", "rep")),
        P(("dom", "rep")),
    )
    return jax.shard_map(
        on_device,
        mesh=mesh,
        in_specs=placed,
        out_specs=(P(("dom", "rep"), None), P(("dom", "rep")), P(), P()),
        check_vma=False,
    )
```

```python
import functools
import jax
import jax.numpy as jnp
from jax import lax
from jax.experimental import pallas as pl
from jax.experimental.pallas import tpu as pltpu
from jax.sharding import PartitionSpec as P

learn_rate = 0.1
LOG2E = 1.4426950408889634
GROUPS = 4
SLOTS = 1000
PAD = 1024
ROWS = 2048
D = 256
BLK = 256
NBLK = ROWS // BLK
CH = 512
NCH = GROUPS * PAD // CH
PER = PAD // CH
bf16 = jnp.bfloat16
f32 = jnp.float32

NN = (((1,), (0,)), ((), ()))
NT = (((1,), (1,)), ((), ()))
MB = 1024 * 1024


def mm(a, b, dims=NN):
    return lax.dot_general(a, b, dims, preferred_element_type=f32)


def params():
    return pltpu.CompilerParams(
        dimension_semantics=("arbitrary",), vmem_limit_bytes=48 * MB
    )


PARTS = 4
PART = ROWS // PARTS


def block_of(parts, b):
    first = b * BLK % PART
    return parts[b * BLK // PART][first : first + BLK, :]


def count_kernel(neg_ref, after_ref, out_ref):
    rows = lax.broadcasted_iota(jnp.int32, (BLK, PAD), 0)

    def body(b, carry):
        hits = jnp.where(rows == neg_ref[0] - b * BLK, 1.0, 0.0)
        count = jnp.sum(hits, axis=1, keepdims=True)
        at = pl.ds(pl.multiple_of(b * BLK, BLK), BLK)
        out_ref[0, at, 0:1] = jnp.log2(count)
        out_ref[0, at, 1:2] = jnp.log2(count + 1.0)
        return carry

    lax.fori_loop(0, NBLK, body, 0)


def neg_weights(neg_pad, after):
    return pl.pallas_call(
        count_kernel,
        grid=(GROUPS,),
        in_specs=[
            pl.BlockSpec((1, 1, PAD), lambda g: (g, 0, 0)),
            pl.BlockSpec(memory_space=pl.ANY),
        ],
        out_specs=pl.BlockSpec((1, ROWS, 2), lambda g: (g, 0, 0)),
        out_shape=jax.ShapeDtypeStruct((GROUPS, ROWS, 2), f32),
        compiler_params=params(),
        name="neg_weights",
    )(neg_pad.reshape(GROUPS, 1, PAD), after)


def one_hot(rows, index, first):
    return jnp.where(rows == (index - first).astype(jnp.int16), bf16(1), bf16(0))


def query_kernel(rel_ref, *refs):
    own = refs[:PARTS]
    idx_ref, mat_ref, s_ref, q_ref = refs[PARTS:]
    column = jnp.broadcast_to(idx_ref[0].astype(f32), (128, CH)).T
    column = column.astype(jnp.int32).astype(jnp.int16)
    cols = lax.broadcasted_iota(jnp.int32, (CH, 128), 1).astype(jnp.int16)
    acc = None
    for b in range(NBLK):
        hot = jnp.concatenate(
            [
                jnp.where(cols + jnp.int16(first) == column, bf16(1), bf16(0))
                for first in (b * BLK, b * BLK + 128)
            ],
            axis=1,
        )
        part = mm(hot, block_of(own, b))
        acc = part if acc is None else acc + part
    rows = acc.astype(bf16)
    s_ref[...] = rows
    q_ref[...] = mm(mat_ref[0], rows, NT).astype(bf16)


def make_queries(own, src_rows, rel_id, rel_t):
    return pl.pallas_call(
        query_kernel,
        grid_spec=pltpu.PrefetchScalarGridSpec(
            num_scalar_prefetch=1,
            grid=(NCH,),
            in_specs=[
                *[pl.BlockSpec((PART, D), lambda j, rel: (0, 0))] * PARTS,
                pl.BlockSpec((1, 1, CH), lambda j, rel: (j, 0, 0)),
                pl.BlockSpec((1, D, D), lambda j, rel: (rel[j // PER], 0, 0)),
            ],
            out_specs=[
                pl.BlockSpec((CH, D), lambda j, rel: (j, 0)),
                pl.BlockSpec((D, CH), lambda j, rel: (0, j)),
            ],
        ),
        out_shape=[
            jax.ShapeDtypeStruct((GROUPS * PAD, D), bf16),
            jax.ShapeDtypeStruct((D, GROUPS * PAD), bf16),
        ],
        compiler_params=params(),
        name="queries",
    )(rel_id, *own, src_rows, rel_t)


SUB = 32


def score_kernel(rel_ref, cnt_ref, *refs):
    nxt = refs[:PARTS]
    q_ref, s_ref, dst_ref, wt_ref, gq_ref = refs[PARTS : PARTS + 5]
    dg = refs[PARTS + 5 : 2 * PARTS + 5]
    rg_ref, sc, nxt_t_ref, w0, w1, qs0, qs1, sl0, sl1, dacc = refs[2 * PARTS + 5 :]
    g = pl.program_id(0)
    rows = lax.broadcasted_iota(jnp.int32, (SUB, CH), 0)
    rows16 = lax.broadcasted_iota(jnp.int32, (BLK, CH), 0).astype(jnp.int16)

    @pl.when(g == 0)
    def _():
        dacc[...] = jnp.zeros_like(dacc)
        rg_ref[...] = jnp.zeros_like(rg_ref)
        w1[...] = jnp.zeros_like(w1)
        for b in range(NBLK):
            nxt_t_ref[:, b * BLK : (b + 1) * BLK] = block_of(nxt, b).T
        qs1[...] = jnp.zeros_like(qs1)
        sl1[...] = jnp.zeros_like(sl1)

    def spread(b, w, qs):
        at = slice(b * BLK, (b + 1) * BLK)
        dacc[at, :] += mm(w[at, :], qs[...], NT)

    def finish(acc, sl, chunk, s_at):
        gq = (acc * sl[0:1, :]).astype(bf16)
        gq_ref[:, pl.ds(pl.multiple_of(chunk * CH, CH), CH)] = gq
        rg_ref[rel_ref[chunk // PER]] += mm(gq, s_ref[pl.ds(pl.multiple_of(s_at, CH), CH), :])

    def stage(half, w, qs, sl, w_old, qs_old, sl_old, chunk_old):
        here = slice(half * CH, (half + 1) * CH)
        q = q_ref[:, here]
        dst = dst_ref[0, 0:1, here]
        top = jnp.full((8, CH), -jnp.inf, f32)
        hit = jnp.zeros((8, CH), f32)
        for b in range(NBLK):
            raw = mm(block_of(nxt, b), q)
            for i in range(BLK // SUB):
                at = slice(b * BLK + i * SUB, b * BLK + (i + 1) * SUB)
                mask = rows == dst - (b * BLK + i * SUB)
                val = raw[i * SUB : (i + 1) * SUB] * LOG2E + jnp.where(
                    mask, wt_ref[0, at, 1:2], wt_ref[0, at, 0:1]
                )
                sc[at, :] = val
                top = jnp.maximum(top, jnp.max(val.reshape(SUB // 8, 8, CH), axis=0))
                hit = hit + jnp.sum(jnp.where(mask, val, 0.0).reshape(SUB // 8, 8, CH), axis=0)
            spread(b, w_old, qs_old)
        top = jnp.max(top, axis=0, keepdims=True)
        hit = jnp.sum(hit, axis=0, keepdims=True)
        tot = jnp.zeros((8, CH), f32)
        acc = None
        for b in range(NBLK):
            for i in range(BLK // SUB):
                at = slice(b * BLK + i * SUB, b * BLK + (i + 1) * SUB)
                e = jnp.exp2(sc[at, :] - top)
                tot = tot + jnp.sum(e.reshape(SUB // 8, 8, CH), axis=0)
                w[at, :] = e.astype(bf16)
            at = slice(b * BLK, (b + 1) * BLK)
            part = mm(nxt_t_ref[:, at], w_old[at, :])
            acc = part if acc is None else acc + part
        finish(acc, sl_old, chunk_old, chunk_old * CH)
        tot = jnp.sum(tot, axis=0, keepdims=True)
        gain = (jnp.exp2(hit - top) - tot).astype(bf16)
        lane = lax.broadcasted_iota(jnp.int32, (1, CH), 1) + half * CH
        live = jnp.logical_and(lane < SLOTS, g * SLOTS + lane < cnt_ref[0])
        scale = jnp.where(live, 1.0 / tot, 0.0)
        sl[...] = jnp.broadcast_to(scale, (8, CH))
        qs[...] = (q.astype(f32) * scale).astype(bf16)
        for b in range(NBLK):
            at = slice(b * BLK, (b + 1) * BLK)
            mask = rows16 == (dst - b * BLK).astype(jnp.int16)
            w[at, :] = jnp.where(mask, gain, w[at, :])

    stage(0, w0, qs0, sl0, w1, qs1, sl1, jnp.maximum(2 * g - 1, 0))
    stage(1, w1, qs1, sl1, w0, qs0, sl0, 2 * g)

    @pl.when(g == GROUPS - 1)
    def _():
        for b in range(NBLK):
            spread(b, w1, qs1)
        finish(mm(nxt_t_ref[...], w1[...]), sl1, 2 * g + 1, (2 * g + 1) * CH)
        for p in range(PARTS):
            dg[p][...] = dacc[p * PART : (p + 1) * PART, :].astype(bf16)


def score_side(nxt, q, s, dst_rows, weights, rel_id, counts, kinds):
    return pl.pallas_call(
        score_kernel,
        grid_spec=pltpu.PrefetchScalarGridSpec(
            num_scalar_prefetch=2,
            grid=(GROUPS,),
            in_specs=[
                *[pl.BlockSpec((PART, D), lambda j, rel, cnt: (0, 0))] * PARTS,
                pl.BlockSpec((D, PAD), lambda j, rel, cnt: (0, j)),
                pl.BlockSpec((GROUPS * PAD, D), lambda j, rel, cnt: (0, 0)),
                pl.BlockSpec((1, 1, PAD), lambda j, rel, cnt: (j, 0, 0)),
                pl.BlockSpec((1, ROWS, 2), lambda j, rel, cnt: (j, 0, 0)),
            ],
            out_specs=[
                pl.BlockSpec((D, GROUPS * PAD), lambda j, rel, cnt: (0, 0)),
                *[pl.BlockSpec((PART, D), lambda j, rel, cnt: (0, 0))] * PARTS,
                pl.BlockSpec((kinds, D, D), lambda j, rel, cnt: (0, 0, 0)),
            ],
            scratch_shapes=[
                pltpu.VMEM((ROWS, CH), f32),
                pltpu.VMEM((D, ROWS), bf16),
                pltpu.VMEM((ROWS, CH), bf16),
                pltpu.VMEM((ROWS, CH), bf16),
                pltpu.VMEM((D, CH), bf16),
                pltpu.VMEM((D, CH), bf16),
                pltpu.VMEM((8, CH), f32),
                pltpu.VMEM((8, CH), f32),
                pltpu.VMEM((ROWS, D), f32),
            ],
        ),
        out_shape=[
            jax.ShapeDtypeStruct((D, GROUPS * PAD), bf16),
            *[jax.ShapeDtypeStruct((PART, D), bf16)] * PARTS,
            jax.ShapeDtypeStruct((kinds, D, D), f32),
        ],
        compiler_params=params(),
        name="scores",
    )(rel_id, counts, *nxt, q, s, dst_rows, weights)


def source_kernel(rel_ref, gq_ref, src_ref, mat_ref, *refs):
    out, acc = refs[:PARTS], refs[PARTS]
    g = pl.program_id(0)

    @pl.when(g == 0)
    def _():
        acc[...] = jnp.zeros_like(acc)

    grad = mm(mat_ref[0], gq_ref[...]).astype(bf16)
    rows = lax.broadcasted_iota(jnp.int32, (BLK, PAD), 0).astype(jnp.int16)
    for b in range(NBLK):
        at = slice(b * BLK, (b + 1) * BLK)
        acc[at, :] += mm(one_hot(rows, src_ref[0], b * BLK), grad, NT)

    @pl.when(g == GROUPS - 1)
    def _():
        for p in range(PARTS):
            out[p][...] = acc[p * PART : (p + 1) * PART, :].astype(bf16)


def source_side(gq, src_rows, rel_id, rel_b):
    return pl.pallas_call(
        source_kernel,
        grid_spec=pltpu.PrefetchScalarGridSpec(
            num_scalar_prefetch=1,
            grid=(GROUPS,),
            in_specs=[
                pl.BlockSpec((D, PAD), lambda j, rel: (0, j)),
                pl.BlockSpec((1, 1, PAD), lambda j, rel: (j, 0, 0)),
                pl.BlockSpec((1, D, D), lambda j, rel: (rel[j], 0, 0)),
            ],
            out_specs=[pl.BlockSpec((PART, D), lambda j, rel: (0, 0))] * PARTS,
            scratch_shapes=[pltpu.VMEM((ROWS, D), f32)],
        ),
        out_shape=[jax.ShapeDtypeStruct((PART, D), bf16)] * PARTS,
        compiler_params=params(),
        name="source_grads",
    )(rel_id, gq, src_rows, rel_b)


def rowwise(param, accum, grad):
    fresh = accum + jnp.mean(grad * grad, -1)
    return (param - learn_rate * grad / jnp.sqrt(fresh)[..., None], fresh)


def shift_dom(block, by):
    size = lax.axis_size("dom")
    return lax.ppermute(block, "dom", [(i, (i + by) % size) for i in range(size)])


def swap_z(block):
    return lax.ppermute(block, "rep", [(i, i ^ 1) for i in range(8)])


def shift_x(block, by):
    return lax.ppermute(block, "rep", [(i, (i + 2 * by) % 8) for i in range(8)])


def spread_x(pair):
    return [pair] + [shift_x(pair, -k) for k in (1, 2, 3)]


def collect_x(blocks):
    got = [blocks[0]] + [shift_x(blocks[k], k) for k in (1, 2, 3)]
    return sum(block.astype(f32) for block in got)


def turned(index):
    rep = lax.axis_index("rep")
    return ((index - PART * (rep // 2)) % ROWS) ^ (256 * (rep % 2))


def reduce_relation(rel_t):
    kinds = rel_t.shape[0]
    part = rel_t.astype(bf16).transpose(0, 2, 1).reshape(32, -1, D)
    got = lax.all_to_all(part, "dom", 0, 0)
    mine = jnp.sum(got.astype(f32), 0)
    every = lax.all_to_all(jnp.broadcast_to(mine, (8,) + mine.shape), "rep", 0, 0)
    total = jnp.sum(every, 0).astype(bf16)
    full = lax.all_to_all(jnp.broadcast_to(total, (32,) + total.shape), "dom", 0, 0)
    return full.reshape(kinds, D, D).astype(f32)


def pad_slots(index, fill):
    return jnp.pad(index.reshape(GROUPS, SLOTS), ((0, 0), (0, PAD - SLOTS)), constant_values=fill)


def source_stage(own, src_pad, rel_id, rel_t):
    return make_queries(own, src_pad.reshape(NCH, 1, CH), rel_id, rel_t)


def target_stage(nxt, q, s, dst_pad, weights, rel_id, counts, kinds):
    out = score_side(nxt, q, s, dst_pad.reshape(GROUPS, 1, PAD), weights, rel_id, counts, kinds)
    return out[0], out[1 : PARTS + 1], out[PARTS + 1]


def local_grads(own, nxt, relation, src_index, dst_index, neg_index, rel_id, counts):
    own, nxt, rel_b = own.astype(bf16), nxt.astype(bf16), relation.astype(bf16)
    src_pad = pad_slots(src_index, -1)
    weights = neg_weights(pad_slots(neg_index, -1), own)
    own = [own[k * PART : (k + 1) * PART] for k in range(PARTS)]
    nxt = [nxt[k * PART : (k + 1) * PART] for k in range(PARTS)]
    s, q = source_stage(own, src_pad, rel_id, rel_b.transpose(0, 2, 1))
    gq, dst_grad, rel_grad = target_stage(
        nxt, q, s, pad_slots(dst_index, -1), weights, rel_id, counts, relation.shape[0]
    )
    src_grad = source_side(gq, src_pad.reshape(GROUPS, 1, PAD), rel_id, rel_b)
    return jnp.concatenate(src_grad), jnp.concatenate(dst_grad), rel_grad.transpose(0, 2, 1)


def on_device(
    entity, entity_accum, relation, relation_accum, src_index, dst_index, neg_index, rel_id, counts
):
    ent_b = entity.astype(bf16)
    rel_b = relation.astype(bf16)
    src_pad = pad_slots(turned(src_index), -1)
    dst_pad = pad_slots(turned(dst_index), -1)
    neg_pad = pad_slots(turned(neg_index), -1)
    other = swap_z(ent_b)
    shifted = shift_dom(ent_b, -1)
    own = spread_x(jnp.concatenate([ent_b, other]))
    nxt = spread_x(jnp.concatenate([shifted, swap_z(shifted)]))
    weights = neg_weights(neg_pad, other)
    s, q = source_stage(own, src_pad, rel_id, rel_b.transpose(0, 2, 1))
    gq, dst_grad, rel_grad = target_stage(
        nxt, q, s, dst_pad, weights, rel_id, counts, relation.shape[0]
    )
    rel_total = reduce_relation(rel_grad)
    moved = shift_dom(collect_x(dst_grad).astype(bf16), 1)
    src_grad = source_side(gq, src_pad.reshape(GROUPS, 1, PAD), rel_id, rel_b)
    total = collect_x(src_grad) + moved.astype(f32)
    grads = total[:256] + swap_z(total[256:].astype(bf16)).astype(f32)
    entity_new, entity_accum_new = rowwise(entity, entity_accum, grads)
    relation_new, relation_accum_new = rowwise(relation, relation_accum, rel_total)
    return (entity_new, entity_accum_new, relation_new, relation_accum_new)


def solution(mesh):
    placed = (
        P(("dom", "rep"), None),
        P(("dom", "rep")),
        P(),
        P(),
        P(("dom", "rep")),
        P(("dom", "rep")),
        P(("dom", "rep"), None),
        P(("dom", "rep")),
        P(("dom", "rep")),
    )
    return jax.shard_map(
        on_device,
        mesh=mesh,
        in_specs=placed,
        out_specs=(P(("dom", "rep"), None), P(("dom", "rep")), P(), P()),
        check_vma=False,
    )
```

```python
import functools
import jax
import jax.numpy as jnp
from jax import lax
from jax.experimental import pallas as pl
from jax.experimental.pallas import tpu as pltpu
from jax.sharding import PartitionSpec as P

learn_rate = 0.1
LOG2E = 1.4426950408889634
GROUPS = 4
SLOTS = 1000
PAD = 1024
ROWS = 2048
D = 256
BLK = 256
NBLK = ROWS // BLK
CH = 512
NCH = GROUPS * PAD // CH
PER = PAD // CH
bf16 = jnp.bfloat16
f32 = jnp.float32

NN = (((1,), (0,)), ((), ()))
NT = (((1,), (1,)), ((), ()))
MB = 1024 * 1024


def mm(a, b, dims=NN):
    return lax.dot_general(a, b, dims, preferred_element_type=f32)


def params():
    return pltpu.CompilerParams(
        dimension_semantics=("arbitrary",), vmem_limit_bytes=48 * MB
    )


def one_hot(rows, index, first):
    return jnp.where(rows == (index - first).astype(jnp.int16), bf16(1), bf16(0))


PARTS = 4
PART = ROWS // PARTS


def block_of(parts, b):
    first = b * BLK % PART
    return parts[b * BLK // PART][first : first + BLK, :]


def count_kernel(neg_ref, after_ref, out_ref):
    rows = lax.broadcasted_iota(jnp.int32, (BLK, 128), 0).astype(jnp.int16)
    for b in range(NBLK):
        hits = None
        for c in range(0, PAD, 128):
            hot = one_hot(rows, neg_ref[0, :, c : c + 128], b * BLK)
            hits = hot if hits is None else hits + hot
        count = jnp.sum(hits.astype(f32), axis=1, keepdims=True)
        at = slice(b * BLK, (b + 1) * BLK)
        out_ref[0, at, 0:1] = jnp.log2(count)
        out_ref[0, at, 1:2] = jnp.log2(count + 1.0)


def neg_weights(neg_pad, after):
    return pl.pallas_call(
        count_kernel,
        grid=(GROUPS,),
        in_specs=[
            pl.BlockSpec((1, 1, PAD), lambda g: (g, 0, 0)),
            pl.BlockSpec(memory_space=pl.ANY),
        ],
        out_specs=pl.BlockSpec((1, ROWS, 2), lambda g: (g, 0, 0)),
        out_shape=jax.ShapeDtypeStruct((GROUPS, ROWS, 2), f32),
        compiler_params=params(),
        name="neg_weights",
    )(neg_pad.reshape(GROUPS, 1, PAD), after)


def query_kernel(rel_ref, *refs):
    own = refs[:PARTS]
    idx_ref, mat_ref, s_ref, q_ref = refs[PARTS:]
    column = jnp.broadcast_to(idx_ref[0].astype(f32), (128, CH)).T
    column = column.astype(jnp.int32).astype(jnp.int16)
    cols = lax.broadcasted_iota(jnp.int32, (CH, 128), 1).astype(jnp.int16)
    acc = None
    for b in range(NBLK):
        hot = jnp.concatenate(
            [
                jnp.where(cols + jnp.int16(first) == column, bf16(1), bf16(0))
                for first in (b * BLK, b * BLK + 128)
            ],
            axis=1,
        )
        part = mm(hot, block_of(own, b))
        acc = part if acc is None else acc + part
    rows = acc.astype(bf16)
    s_ref[...] = rows
    q_ref[...] = mm(mat_ref[0].astype(bf16).T, rows, NT).astype(bf16)


def make_queries(own, src_rows, rel_id, relation):
    return pl.pallas_call(
        query_kernel,
        grid_spec=pltpu.PrefetchScalarGridSpec(
            num_scalar_prefetch=1,
            grid=(NCH,),
            in_specs=[
                *[pl.BlockSpec((PART, D), lambda j, rel: (0, 0))] * PARTS,
                pl.BlockSpec((1, 1, CH), lambda j, rel: (j, 0, 0)),
                pl.BlockSpec((1, D, D), lambda j, rel: (rel[j // PER], 0, 0)),
            ],
            out_specs=[
                pl.BlockSpec((CH, D), lambda j, rel: (j, 0)),
                pl.BlockSpec((D, CH), lambda j, rel: (0, j)),
            ],
        ),
        out_shape=[
            jax.ShapeDtypeStruct((GROUPS * PAD, D), bf16),
            jax.ShapeDtypeStruct((D, GROUPS * PAD), bf16),
        ],
        compiler_params=params(),
        name="queries",
    )(rel_id, *own, src_rows, relation)


SUB = 32


def score_kernel(cnt_ref, *refs):
    nxt = refs[:PARTS]
    q_ref, dst_ref, wt_ref, gq_ref = refs[PARTS : PARTS + 4]
    dg = refs[PARTS + 4 : 2 * PARTS + 4]
    sc, nxt_t_ref, w0, w1, qs0, qs1, sl0, sl1, dacc = refs[2 * PARTS + 4 :]
    g = pl.program_id(0)
    rows = lax.broadcasted_iota(jnp.int32, (SUB, CH), 0)
    rows16 = lax.broadcasted_iota(jnp.int32, (BLK, CH), 0).astype(jnp.int16)

    @pl.when(g == 0)
    def _():
        dacc[...] = jnp.zeros_like(dacc)
        w1[...] = jnp.zeros_like(w1)
        for b in range(NBLK):
            nxt_t_ref[:, b * BLK : (b + 1) * BLK] = block_of(nxt, b).T
        qs1[...] = jnp.zeros_like(qs1)
        sl1[...] = jnp.zeros_like(sl1)

    def spread(b, w, qs):
        at = slice(b * BLK, (b + 1) * BLK)
        dacc[at, :] += mm(w[at, :], qs[...], NT)

    def finish(acc, sl, chunk):
        gq = (acc * sl[0:1, :]).astype(bf16)
        gq_ref[:, pl.ds(pl.multiple_of(chunk * CH, CH), CH)] = gq

    def stage(half, w, qs, sl, w_old, qs_old, sl_old, chunk_old):
        here = slice(half * CH, (half + 1) * CH)
        q = q_ref[:, here]
        dst = dst_ref[0, 0:1, here]
        top = jnp.full((8, CH), -jnp.inf, f32)
        hit = jnp.zeros((8, CH), f32)
        for b in range(NBLK):
            raw = mm(block_of(nxt, b), q)
            for i in range(BLK // SUB):
                at = slice(b * BLK + i * SUB, b * BLK + (i + 1) * SUB)
                mask = rows == dst - (b * BLK + i * SUB)
                val = raw[i * SUB : (i + 1) * SUB] * LOG2E + jnp.where(
                    mask, wt_ref[0, at, 1:2], wt_ref[0, at, 0:1]
                )
                sc[at, :] = val
                top = jnp.maximum(top, jnp.max(val.reshape(SUB // 8, 8, CH), axis=0))
                hit = hit + jnp.sum(jnp.where(mask, val, 0.0).reshape(SUB // 8, 8, CH), axis=0)
            spread(b, w_old, qs_old)
        top = jnp.max(top, axis=0, keepdims=True)
        hit = jnp.sum(hit, axis=0, keepdims=True)
        tot = jnp.zeros((8, CH), f32)
        acc = None
        for b in range(NBLK):
            for i in range(BLK // SUB):
                at = slice(b * BLK + i * SUB, b * BLK + (i + 1) * SUB)
                e = jnp.exp2(sc[at, :] - top)
                tot = tot + jnp.sum(e.reshape(SUB // 8, 8, CH), axis=0)
                w[at, :] = e.astype(bf16)
            at = slice(b * BLK, (b + 1) * BLK)
            part = mm(nxt_t_ref[:, at], w_old[at, :])
            acc = part if acc is None else acc + part
        finish(acc, sl_old, chunk_old)
        tot = jnp.sum(tot, axis=0, keepdims=True)
        gain = (jnp.exp2(hit - top) - tot).astype(bf16)
        lane = lax.broadcasted_iota(jnp.int32, (1, CH), 1) + half * CH
        live = jnp.logical_and(lane < SLOTS, g * SLOTS + lane < cnt_ref[0])
        scale = jnp.where(live, 1.0 / tot, 0.0)
        sl[...] = jnp.broadcast_to(scale, (8, CH))
        qs[...] = (q.astype(f32) * scale).astype(bf16)
        for b in range(NBLK):
            at = slice(b * BLK, (b + 1) * BLK)
            mask = rows16 == (dst - b * BLK).astype(jnp.int16)
            w[at, :] = jnp.where(mask, gain, w[at, :])

    stage(0, w0, qs0, sl0, w1, qs1, sl1, jnp.maximum(2 * g - 1, 0))
    stage(1, w1, qs1, sl1, w0, qs0, sl0, 2 * g)

    @pl.when(g == GROUPS - 1)
    def _():
        for b in range(NBLK):
            spread(b, w1, qs1)
        finish(mm(nxt_t_ref[...], w1[...]), sl1, 2 * g + 1)
        for p in range(PARTS):
            dg[p][...] = dacc[p * PART : (p + 1) * PART, :].astype(bf16)


def score_side(nxt, q, dst_rows, weights, counts):
    return pl.pallas_call(
        score_kernel,
        grid_spec=pltpu.PrefetchScalarGridSpec(
            num_scalar_prefetch=1,
            grid=(GROUPS,),
            in_specs=[
                *[pl.BlockSpec((PART, D), lambda j, cnt: (0, 0))] * PARTS,
                pl.BlockSpec((D, PAD), lambda j, cnt: (0, j)),
                pl.BlockSpec((1, 1, PAD), lambda j, cnt: (j, 0, 0)),
                pl.BlockSpec((1, ROWS, 2), lambda j, cnt: (j, 0, 0)),
            ],
            out_specs=[
                pl.BlockSpec((D, GROUPS * PAD), lambda j, cnt: (0, 0)),
                *[pl.BlockSpec((PART, D), lambda j, cnt: (0, 0))] * PARTS,
            ],
            scratch_shapes=[
                pltpu.VMEM((ROWS, CH), f32),
                pltpu.VMEM((D, ROWS), bf16),
                pltpu.VMEM((ROWS, CH), bf16),
                pltpu.VMEM((ROWS, CH), bf16),
                pltpu.VMEM((D, CH), bf16),
                pltpu.VMEM((D, CH), bf16),
                pltpu.VMEM((8, CH), f32),
                pltpu.VMEM((8, CH), f32),
                pltpu.VMEM((ROWS, D), f32),
            ],
        ),
        out_shape=[
            jax.ShapeDtypeStruct((D, GROUPS * PAD), bf16),
            *[jax.ShapeDtypeStruct((PART, D), bf16)] * PARTS,
        ],
        compiler_params=params(),
        name="scores",
    )(counts, *nxt, q, dst_rows, weights)


def source_kernel(rel_ref, gq_ref, s_ref, src_ref, mat_ref, *refs):
    out, rg_ref, acc, racc = refs[:PARTS], *refs[PARTS:]
    g = pl.program_id(0)

    @pl.when(g == 0)
    def _():
        acc[...] = jnp.zeros_like(acc)
        racc[...] = jnp.zeros_like(racc)

    racc[rel_ref[g]] += mm(gq_ref[...], s_ref[...])
    grad = mm(mat_ref[0].astype(bf16), gq_ref[...]).astype(bf16)
    rows = lax.broadcasted_iota(jnp.int32, (BLK, PAD), 0).astype(jnp.int16)
    for b in range(NBLK):
        at = slice(b * BLK, (b + 1) * BLK)
        acc[at, :] += mm(one_hot(rows, src_ref[0], b * BLK), grad, NT)

    @pl.when(g == GROUPS - 1)
    def _():
        for p in range(PARTS):
            out[p][...] = acc[p * PART : (p + 1) * PART, :].astype(bf16)
        for k in range(racc.shape[0]):
            rg_ref[k] = racc[k].T.astype(bf16)


def source_side(gq, s, src_rows, rel_id, relation):
    kinds = relation.shape[0]
    return pl.pallas_call(
        source_kernel,
        grid_spec=pltpu.PrefetchScalarGridSpec(
            num_scalar_prefetch=1,
            grid=(GROUPS,),
            in_specs=[
                pl.BlockSpec((D, PAD), lambda j, rel: (0, j)),
                pl.BlockSpec((PAD, D), lambda j, rel: (j, 0)),
                pl.BlockSpec((1, 1, PAD), lambda j, rel: (j, 0, 0)),
                pl.BlockSpec((1, D, D), lambda j, rel: (rel[j], 0, 0)),
            ],
            out_specs=[
                *[pl.BlockSpec((PART, D), lambda j, rel: (0, 0))] * PARTS,
                pl.BlockSpec((kinds, D, D), lambda j, rel: (0, 0, 0)),
            ],
            scratch_shapes=[pltpu.VMEM((ROWS, D), f32), pltpu.VMEM((kinds, D, D), f32)],
        ),
        out_shape=[
            *[jax.ShapeDtypeStruct((PART, D), bf16)] * PARTS,
            jax.ShapeDtypeStruct((kinds, D, D), bf16),
        ],
        compiler_params=params(),
        name="source_grads",
    )(rel_id, gq, s, src_rows, relation)


def rowwise(param, accum, grad):
    fresh = accum + jnp.mean(grad * grad, -1)
    return (param - learn_rate * grad / jnp.sqrt(fresh)[..., None], fresh)


def shift_dom(block, by):
    size = lax.axis_size("dom")
    return lax.ppermute(block, "dom", [(i, (i + by) % size) for i in range(size)])


def swap_z(block):
    return lax.ppermute(block, "rep", [(i, i ^ 1) for i in range(8)])


def shift_x(block, by):
    return lax.ppermute(block, "rep", [(i, (i + 2 * by) % 8) for i in range(8)])


def spread_x(pair):
    return [pair] + [shift_x(pair, -k) for k in (1, 2, 3)]


def collect_x(blocks):
    got = [blocks[0]] + [shift_x(blocks[k], k) for k in (1, 2, 3)]
    return sum(block.astype(f32) for block in got)


def turned(index):
    rep = lax.axis_index("rep")
    return ((index - PART * (rep // 2)) % ROWS) ^ (256 * (rep % 2))


def spread_dom(block, stride, count):
    size = lax.axis_size("dom")

    def route(k):
        step = [((i // stride % count + k) % count - i // stride % count) * stride for i in range(size)]
        return [(i + step[i], i) for i in range(size)]

    return jnp.concatenate([block] + [lax.ppermute(block, "dom", route(k)) for k in range(1, count)])


def reduce_relation(grad):
    kinds = grad.shape[0]
    got = lax.all_to_all(grad.reshape(32, -1, D), "dom", 0, 0)
    mine = jnp.sum(got.astype(f32), 0).astype(bf16)
    every = lax.all_to_all(jnp.broadcast_to(mine, (8,) + mine.shape), "rep", 0, 0)
    total = jnp.sum(every.astype(f32), 0)
    full = spread_dom(spread_dom(spread_dom(total, 8, 4), 2, 4), 1, 2)
    me = lax.axis_index("dom")
    i = jnp.arange(32)
    z, y, core = (i // 8 - me // 8) % 4, (i // 2 - me // 2) % 4, (i - me) % 2
    order = core * 16 + y * 4 + z
    return full.reshape(32, -1, D)[order].reshape(kinds, D, D)


def pad_slots(index, fill):
    return jnp.pad(index.reshape(GROUPS, SLOTS), ((0, 0), (0, PAD - SLOTS)), constant_values=fill)


def source_stage(own, src_pad, rel_id, relation):
    return make_queries(own, src_pad.reshape(NCH, 1, CH), rel_id, relation)


def target_stage(nxt, q, dst_pad, weights, counts):
    out = score_side(nxt, q, dst_pad.reshape(GROUPS, 1, PAD), weights, counts)
    return out[0], out[1:]


def back_stage(gq, s, src_pad, rel_id, relation):
    out = source_side(gq, s, src_pad.reshape(GROUPS, 1, PAD), rel_id, relation)
    return out[:PARTS], out[PARTS]


def local_grads(own, nxt, relation, src_index, dst_index, neg_index, rel_id, counts):
    own, nxt = own.astype(bf16), nxt.astype(bf16)
    src_pad = pad_slots(src_index, -1)
    weights = neg_weights(pad_slots(neg_index, -1), own)
    own = [own[k * PART : (k + 1) * PART] for k in range(PARTS)]
    nxt = [nxt[k * PART : (k + 1) * PART] for k in range(PARTS)]
    s, q = source_stage(own, src_pad, rel_id, relation)
    gq, dst_grad = target_stage(nxt, q, pad_slots(dst_index, -1), weights, counts)
    src_grad, rel_grad = back_stage(gq, s, src_pad, rel_id, relation)
    return jnp.concatenate(src_grad), jnp.concatenate(dst_grad), rel_grad


def on_device(
    entity, entity_accum, relation, relation_accum, src_index, dst_index, neg_index, rel_id, counts
):
    ent_b = entity.astype(bf16)
    src_pad = pad_slots(turned(src_index), -1)
    dst_pad = pad_slots(turned(dst_index), -1)
    neg_pad = pad_slots(turned(neg_index), -1)
    other = swap_z(ent_b)
    shifted = shift_dom(ent_b, -1)
    own = spread_x(jnp.concatenate([ent_b, other]))
    nxt = spread_x(jnp.concatenate([shifted, swap_z(shifted)]))
    weights = neg_weights(neg_pad, other)
    s, q = source_stage(own, src_pad, rel_id, relation)
    gq, dst_grad = target_stage(nxt, q, dst_pad, weights, counts)
    moved = shift_dom(collect_x(dst_grad).astype(bf16), 1)
    src_grad, rel_grad = back_stage(gq, s, src_pad, rel_id, relation)
    rel_total = reduce_relation(rel_grad)
    total = collect_x(src_grad) + moved.astype(f32)
    grads = total[:256] + swap_z(total[256:].astype(bf16)).astype(f32)
    entity_new, entity_accum_new = rowwise(entity, entity_accum, grads)
    relation_new, relation_accum_new = rowwise(relation, relation_accum, rel_total)
    return (entity_new, entity_accum_new, relation_new, relation_accum_new)


def solution(mesh):
    placed = (
        P(("dom", "rep"), None),
        P(("dom", "rep")),
        P(),
        P(),
        P(("dom", "rep")),
        P(("dom", "rep")),
        P(("dom", "rep"), None),
        P(("dom", "rep")),
        P(("dom", "rep")),
    )
    return jax.shard_map(
        on_device,
        mesh=mesh,
        in_specs=placed,
        out_specs=(P(("dom", "rep"), None), P(("dom", "rep")), P(), P()),
        check_vma=False,
    )
```

```python
import functools
import jax
import jax.numpy as jnp
from jax import lax
from jax.experimental import pallas as pl
from jax.experimental.pallas import tpu as pltpu
from jax.sharding import PartitionSpec as P

learn_rate = 0.1
LOG2E = 1.4426950408889634
GROUPS = 4
SLOTS = 1000
PAD = 1024
ROWS = 2048
D = 256
BLK = 256
NBLK = ROWS // BLK
CH = 512
NCH = GROUPS * PAD // CH
PER = PAD // CH
bf16 = jnp.bfloat16
f32 = jnp.float32

NN = (((1,), (0,)), ((), ()))
NT = (((1,), (1,)), ((), ()))
MB = 1024 * 1024


def mm(a, b, dims=NN):
    return lax.dot_general(a, b, dims, preferred_element_type=f32)


def cost(us):
    return pl.CostEstimate(flops=int(us * 5e8), bytes_accessed=int(us * 3.5e6), transcendentals=0)


def params():
    return pltpu.CompilerParams(
        dimension_semantics=("arbitrary",), vmem_limit_bytes=48 * MB
    )


def one_hot(rows, index, first):
    return jnp.where(rows == (index - first).astype(jnp.int16), bf16(1), bf16(0))


PARTS = 4
PART = ROWS // PARTS


def block_of(parts, b):
    first = b * BLK % PART
    return parts[b * BLK // PART][first : first + BLK, :]


def count_kernel(neg_ref, after_ref, out_ref):
    rows = lax.broadcasted_iota(jnp.int32, (BLK, 128), 0).astype(jnp.int16)
    for b in range(NBLK):
        hits = None
        for c in range(0, PAD, 128):
            hot = one_hot(rows, neg_ref[0, :, c : c + 128], b * BLK)
            hits = hot if hits is None else hits + hot
        count = jnp.sum(hits.astype(f32), axis=1, keepdims=True)
        at = slice(b * BLK, (b + 1) * BLK)
        out_ref[0, at, 0:1] = jnp.log2(count)
        out_ref[0, at, 1:2] = jnp.log2(count + 1.0)


def neg_weights(neg_pad, after):
    return pl.pallas_call(
        count_kernel,
        grid=(GROUPS,),
        in_specs=[
            pl.BlockSpec((1, 1, PAD), lambda g: (g, 0, 0)),
            pl.BlockSpec(memory_space=pl.ANY),
        ],
        out_specs=pl.BlockSpec((1, ROWS, 2), lambda g: (g, 0, 0)),
        out_shape=jax.ShapeDtypeStruct((GROUPS, ROWS, 2), f32),
        compiler_params=params(),
        cost_estimate=cost(3),
        name="neg_weights",
    )(neg_pad.reshape(GROUPS, 1, PAD), after)


def query_kernel(rel_ref, *refs):
    own = refs[:PARTS]
    idx_ref, mat_ref, s_ref, q_ref = refs[PARTS:]
    column = jnp.broadcast_to(idx_ref[0].astype(f32), (128, CH)).T
    column = column.astype(jnp.int32).astype(jnp.int16)
    cols = lax.broadcasted_iota(jnp.int32, (CH, 128), 1).astype(jnp.int16)
    acc = None
    for b in range(NBLK):
        hot = jnp.concatenate(
            [
                jnp.where(cols + jnp.int16(first) == column, bf16(1), bf16(0))
                for first in (b * BLK, b * BLK + 128)
            ],
            axis=1,
        )
        part = mm(hot, block_of(own, b))
        acc = part if acc is None else acc + part
    rows = acc.astype(bf16)
    s_ref[...] = rows
    q_ref[...] = mm(mat_ref[0].astype(bf16).T, rows, NT).astype(bf16)


def make_queries(own, src_rows, rel_id, relation):
    return pl.pallas_call(
        query_kernel,
        grid_spec=pltpu.PrefetchScalarGridSpec(
            num_scalar_prefetch=1,
            grid=(NCH,),
            in_specs=[
                *[pl.BlockSpec((PART, D), lambda j, rel: (0, 0))] * PARTS,
                pl.BlockSpec((1, 1, CH), lambda j, rel: (j, 0, 0)),
                pl.BlockSpec((1, D, D), lambda j, rel: (rel[j // PER], 0, 0)),
            ],
            out_specs=[
                pl.BlockSpec((CH, D), lambda j, rel: (j, 0)),
                pl.BlockSpec((D, CH), lambda j, rel: (0, j)),
            ],
        ),
        out_shape=[
            jax.ShapeDtypeStruct((GROUPS * PAD, D), bf16),
            jax.ShapeDtypeStruct((D, GROUPS * PAD), bf16),
        ],
        compiler_params=params(),
        cost_estimate=cost(9),
        name="queries",
    )(rel_id, *own, src_rows, relation)


SUB = 32


def score_kernel(cnt_ref, *refs):
    nxt = refs[:PARTS]
    q_ref, dst_ref, wt_ref, gq_ref = refs[PARTS : PARTS + 4]
    dg = refs[PARTS + 4 : 2 * PARTS + 4]
    sc, nxt_t_ref, w0, w1, qs0, qs1, sl0, sl1, dacc = refs[2 * PARTS + 4 :]
    g = pl.program_id(0)
    rows = lax.broadcasted_iota(jnp.int32, (SUB, CH), 0)
    rows16 = lax.broadcasted_iota(jnp.int32, (BLK, CH), 0).astype(jnp.int16)

    @pl.when(g == 0)
    def _():
        dacc[...] = jnp.zeros_like(dacc)
        w1[...] = jnp.zeros_like(w1)
        for b in range(NBLK):
            nxt_t_ref[:, b * BLK : (b + 1) * BLK] = block_of(nxt, b).T
        qs1[...] = jnp.zeros_like(qs1)
        sl1[...] = jnp.zeros_like(sl1)

    def spread(b, w, qs):
        at = slice(b * BLK, (b + 1) * BLK)
        dacc[at, :] += mm(w[at, :], qs[...], NT)

    def finish(acc, sl, chunk):
        gq = (acc * sl[0:1, :]).astype(bf16)
        gq_ref[:, pl.ds(pl.multiple_of(chunk * CH, CH), CH)] = gq

    def stage(half, w, qs, sl, w_old, qs_old, sl_old, chunk_old):
        here = slice(half * CH, (half + 1) * CH)
        q = q_ref[:, here]
        dst = dst_ref[0, 0:1, here]
        top = jnp.full((8, CH), -jnp.inf, f32)
        hit = jnp.zeros((8, CH), f32)
        for b in range(NBLK):
            raw = mm(block_of(nxt, b), q)
            for i in range(BLK // SUB):
                at = slice(b * BLK + i * SUB, b * BLK + (i + 1) * SUB)
                mask = rows == dst - (b * BLK + i * SUB)
                val = raw[i * SUB : (i + 1) * SUB] * LOG2E + jnp.where(
                    mask, wt_ref[0, at, 1:2], wt_ref[0, at, 0:1]
                )
                sc[at, :] = val
                top = jnp.maximum(top, jnp.max(val.reshape(SUB // 8, 8, CH), axis=0))
                hit = hit + jnp.sum(jnp.where(mask, val, 0.0).reshape(SUB // 8, 8, CH), axis=0)
            spread(b, w_old, qs_old)
        top = jnp.max(top, axis=0, keepdims=True)
        hit = jnp.sum(hit, axis=0, keepdims=True)
        tot = jnp.zeros((8, CH), f32)
        acc = None
        for b in range(NBLK):
            for i in range(BLK // SUB):
                at = slice(b * BLK + i * SUB, b * BLK + (i + 1) * SUB)
                e = jnp.exp2(sc[at, :] - top)
                tot = tot + jnp.sum(e.reshape(SUB // 8, 8, CH), axis=0)
                w[at, :] = e.astype(bf16)
            at = slice(b * BLK, (b + 1) * BLK)
            part = mm(nxt_t_ref[:, at], w_old[at, :])
            acc = part if acc is None else acc + part
        finish(acc, sl_old, chunk_old)
        tot = jnp.sum(tot, axis=0, keepdims=True)
        gain = (jnp.exp2(hit - top) - tot).astype(bf16)
        lane = lax.broadcasted_iota(jnp.int32, (1, CH), 1) + half * CH
        live = jnp.logical_and(lane < SLOTS, g * SLOTS + lane < cnt_ref[0])
        scale = jnp.where(live, 1.0 / tot, 0.0)
        sl[...] = jnp.broadcast_to(scale, (8, CH))
        qs[...] = (q.astype(f32) * scale).astype(bf16)
        for b in range(NBLK):
            at = slice(b * BLK, (b + 1) * BLK)
            mask = rows16 == (dst - b * BLK).astype(jnp.int16)
            w[at, :] = jnp.where(mask, gain, w[at, :])

    stage(0, w0, qs0, sl0, w1, qs1, sl1, jnp.maximum(2 * g - 1, 0))
    stage(1, w1, qs1, sl1, w0, qs0, sl0, 2 * g)

    @pl.when(g == GROUPS - 1)
    def _():
        for b in range(NBLK):
            spread(b, w1, qs1)
        finish(mm(nxt_t_ref[...], w1[...]), sl1, 2 * g + 1)
        for p in range(PARTS):
            dg[p][...] = dacc[p * PART : (p + 1) * PART, :].astype(bf16)


def score_side(nxt, q, dst_rows, weights, counts):
    return pl.pallas_call(
        score_kernel,
        grid_spec=pltpu.PrefetchScalarGridSpec(
            num_scalar_prefetch=1,
            grid=(GROUPS,),
            in_specs=[
                *[pl.BlockSpec((PART, D), lambda j, cnt: (0, 0))] * PARTS,
                pl.BlockSpec((D, PAD), lambda j, cnt: (0, j)),
                pl.BlockSpec((1, 1, PAD), lambda j, cnt: (j, 0, 0)),
                pl.BlockSpec((1, ROWS, 2), lambda j, cnt: (j, 0, 0)),
            ],
            out_specs=[
                pl.BlockSpec((D, GROUPS * PAD), lambda j, cnt: (0, 0)),
                *[pl.BlockSpec((PART, D), lambda j, cnt: (0, 0))] * PARTS,
            ],
            scratch_shapes=[
                pltpu.VMEM((ROWS, CH), f32),
                pltpu.VMEM((D, ROWS), bf16),
                pltpu.VMEM((ROWS, CH), bf16),
                pltpu.VMEM((ROWS, CH), bf16),
                pltpu.VMEM((D, CH), bf16),
                pltpu.VMEM((D, CH), bf16),
                pltpu.VMEM((8, CH), f32),
                pltpu.VMEM((8, CH), f32),
                pltpu.VMEM((ROWS, D), f32),
            ],
        ),
        out_shape=[
            jax.ShapeDtypeStruct((D, GROUPS * PAD), bf16),
            *[jax.ShapeDtypeStruct((PART, D), bf16)] * PARTS,
        ],
        compiler_params=params(),
        cost_estimate=cost(28),
        name="scores",
    )(counts, *nxt, q, dst_rows, weights)


def operator_kernel(rel_ref, gq_ref, s_ref, out_ref, acc):
    g = pl.program_id(0)

    @pl.when(g == 0)
    def _():
        acc[...] = jnp.zeros_like(acc)

    acc[rel_ref[g]] += mm(gq_ref[...], s_ref[...])

    @pl.when(g == GROUPS - 1)
    def _():
        for k in range(acc.shape[0]):
            out_ref[k] = acc[k].T.astype(bf16)


def operator_side(gq, s, rel_id, kinds):
    return pl.pallas_call(
        operator_kernel,
        grid_spec=pltpu.PrefetchScalarGridSpec(
            num_scalar_prefetch=1,
            grid=(GROUPS,),
            in_specs=[
                pl.BlockSpec((D, PAD), lambda j, rel: (0, j)),
                pl.BlockSpec((PAD, D), lambda j, rel: (j, 0)),
            ],
            out_specs=pl.BlockSpec((kinds, D, D), lambda j, rel: (0, 0, 0)),
            scratch_shapes=[pltpu.VMEM((kinds, D, D), f32)],
        ),
        out_shape=jax.ShapeDtypeStruct((kinds, D, D), bf16),
        compiler_params=params(),
        cost_estimate=cost(2),
        name="operator_grads",
    )(rel_id, gq, s)


def source_kernel(rel_ref, gq_ref, src_ref, mat_ref, *refs):
    out, acc = refs[:PARTS], refs[PARTS]
    g = pl.program_id(0)

    @pl.when(g == 0)
    def _():
        acc[...] = jnp.zeros_like(acc)

    grad = mm(mat_ref[0].astype(bf16), gq_ref[...]).astype(bf16)
    rows = lax.broadcasted_iota(jnp.int32, (BLK, PAD), 0).astype(jnp.int16)
    for b in range(NBLK):
        at = slice(b * BLK, (b + 1) * BLK)
        acc[at, :] += mm(one_hot(rows, src_ref[0], b * BLK), grad, NT)

    @pl.when(g == GROUPS - 1)
    def _():
        for p in range(PARTS):
            out[p][...] = acc[p * PART : (p + 1) * PART, :].astype(bf16)


def source_side(gq, src_rows, rel_id, relation):
    return pl.pallas_call(
        source_kernel,
        grid_spec=pltpu.PrefetchScalarGridSpec(
            num_scalar_prefetch=1,
            grid=(GROUPS,),
            in_specs=[
                pl.BlockSpec((D, PAD), lambda j, rel: (0, j)),
                pl.BlockSpec((1, 1, PAD), lambda j, rel: (j, 0, 0)),
                pl.BlockSpec((1, D, D), lambda j, rel: (rel[j], 0, 0)),
            ],
            out_specs=[pl.BlockSpec((PART, D), lambda j, rel: (0, 0))] * PARTS,
            scratch_shapes=[pltpu.VMEM((ROWS, D), f32)],
        ),
        out_shape=[jax.ShapeDtypeStruct((PART, D), bf16)] * PARTS,
        compiler_params=params(),
        cost_estimate=cost(8),
        name="source_grads",
    )(rel_id, gq, src_rows, relation)


def rowwise(param, accum, grad):
    fresh = accum + jnp.mean(grad * grad, -1)
    return (param - learn_rate * grad / jnp.sqrt(fresh)[..., None], fresh)


def shift_dom(block, by):
    size = lax.axis_size("dom")
    return lax.ppermute(block, "dom", [(i, (i + by) % size) for i in range(size)])


def swap_z(block):
    return lax.ppermute(block, "rep", [(i, i ^ 1) for i in range(8)])


def shift_x(block, by):
    return lax.ppermute(block, "rep", [(i, (i + 2 * by) % 8) for i in range(8)])


def spread_x(pair):
    return [pair] + [shift_x(pair, -k) for k in (1, 2, 3)]


def collect_x(blocks):
    got = [blocks[0]] + [shift_x(blocks[k], k) for k in (1, 2, 3)]
    return sum(block.astype(f32) for block in got)


def turned(index):
    rep = lax.axis_index("rep")
    return ((index - PART * (rep // 2)) % ROWS) ^ (256 * (rep % 2))


def reduce_relation(grad):
    kinds = grad.shape[0]
    got = lax.all_to_all(grad.reshape(32, -1, D), "dom", 0, 0)
    mine = jnp.sum(got.astype(f32), 0).astype(bf16)
    every = lax.all_to_all(jnp.broadcast_to(mine, (8,) + mine.shape), "rep", 0, 0)
    total = jnp.sum(every.astype(f32), 0)
    cores = [[2 * i + c for i in range(16)] for c in range(2)]
    half = lax.all_to_all(
        jnp.broadcast_to(total, (16,) + total.shape), "dom", 0, 0, axis_index_groups=cores
    )
    other = lax.ppermute(half, "dom", [(i, i ^ 1) for i in range(32)])
    second = lax.axis_index("dom") % 2 == 1
    pairs = [jnp.where(second, other, half), jnp.where(second, half, other)]
    return jnp.stack(pairs, 1).reshape(kinds, D, D)


def pad_slots(index, fill):
    return jnp.pad(index.reshape(GROUPS, SLOTS), ((0, 0), (0, PAD - SLOTS)), constant_values=fill)


def source_stage(own, src_pad, rel_id, relation):
    return make_queries(own, src_pad.reshape(NCH, 1, CH), rel_id, relation)


def target_stage(nxt, q, s, dst_pad, weights, rel_id, counts, kinds):
    out = score_side(nxt, q, dst_pad.reshape(GROUPS, 1, PAD), weights, counts)
    return out[0], out[1:], operator_side(out[0], s, rel_id, kinds)


def back_stage(gq, src_pad, rel_id, relation):
    return source_side(gq, src_pad.reshape(GROUPS, 1, PAD), rel_id, relation)


def local_grads(own, nxt, relation, src_index, dst_index, neg_index, rel_id, counts):
    own, nxt = own.astype(bf16), nxt.astype(bf16)
    src_pad = pad_slots(src_index, -1)
    weights = neg_weights(pad_slots(neg_index, -1), own)
    own = [own[k * PART : (k + 1) * PART] for k in range(PARTS)]
    nxt = [nxt[k * PART : (k + 1) * PART] for k in range(PARTS)]
    s, q = source_stage(own, src_pad, rel_id, relation)
    gq, dst_grad, rel_grad = target_stage(
        nxt, q, s, pad_slots(dst_index, -1), weights, rel_id, counts, relation.shape[0]
    )
    src_grad = back_stage(gq, src_pad, rel_id, relation)
    return jnp.concatenate(src_grad), jnp.concatenate(dst_grad), rel_grad


def on_device(
    entity, entity_accum, relation, relation_accum, src_index, dst_index, neg_index, rel_id, counts
):
    ent_b = entity.astype(bf16)
    src_pad = pad_slots(turned(src_index), -1)
    dst_pad = pad_slots(turned(dst_index), -1)
    neg_pad = pad_slots(turned(neg_index), -1)
    other = swap_z(ent_b)
    own = spread_x(jnp.concatenate([ent_b, other]))
    nxt = [shift_dom(block, -1) for block in own]
    weights = neg_weights(neg_pad, other)
    s, q = source_stage(own, src_pad, rel_id, relation)
    gq, dst_grad, rel_grad = target_stage(
        nxt, q, s, dst_pad, weights, rel_id, counts, relation.shape[0]
    )
    rel_total = reduce_relation(rel_grad)
    moved = shift_dom(collect_x(dst_grad).astype(bf16), 1)
    src_grad = back_stage(gq, src_pad, rel_id, relation)
    total = collect_x(src_grad) + moved.astype(f32)
    grads = total[:256] + swap_z(total[256:].astype(bf16)).astype(f32)
    entity_new, entity_accum_new = rowwise(entity, entity_accum, grads)
    relation_new, relation_accum_new = rowwise(relation, relation_accum, rel_total)
    return (entity_new, entity_accum_new, relation_new, relation_accum_new)


def solution(mesh):
    placed = (
        P(("dom", "rep"), None),
        P(("dom", "rep")),
        P(),
        P(),
        P(("dom", "rep")),
        P(("dom", "rep")),
        P(("dom", "rep"), None),
        P(("dom", "rep")),
        P(("dom", "rep")),
    )
    return jax.shard_map(
        on_device,
        mesh=mesh,
        in_specs=placed,
        out_specs=(P(("dom", "rep"), None), P(("dom", "rep")), P(), P()),
        check_vma=False,
    )
```

```python
import functools
import jax
import jax.numpy as jnp
from jax import lax
from jax.experimental import pallas as pl
from jax.experimental.pallas import tpu as pltpu
from jax.sharding import PartitionSpec as P

learn_rate = 0.1
LOG2E = 1.4426950408889634
GROUPS = 4
SLOTS = 1000
PAD = 1024
ROWS = 2048
D = 256
BLK = 256
NBLK = ROWS // BLK
CH = 512
NCH = GROUPS * PAD // CH
PER = PAD // CH
bf16 = jnp.bfloat16
f32 = jnp.float32

NN = (((1,), (0,)), ((), ()))
NT = (((1,), (1,)), ((), ()))
MB = 1024 * 1024


def mm(a, b, dims=NN):
    return lax.dot_general(a, b, dims, preferred_element_type=f32)


def cost(us):
    return pl.CostEstimate(flops=int(us * 5e8), bytes_accessed=int(us * 3.5e6), transcendentals=0)


def params():
    return pltpu.CompilerParams(
        dimension_semantics=("arbitrary",), vmem_limit_bytes=48 * MB
    )


def one_hot(rows, index, first):
    return jnp.where(rows == (index - first).astype(jnp.int16), bf16(1), bf16(0))


PARTS = 4
PART = ROWS // PARTS


def block_of(parts, b):
    first = b * BLK % PART
    return parts[b * BLK // PART][first : first + BLK, :]


def count_kernel(neg_ref, out_ref):
    rows = lax.broadcasted_iota(jnp.int32, (BLK, 128), 0).astype(jnp.int16)
    for b in range(NBLK):
        hits = None
        for c in range(0, PAD, 128):
            hot = one_hot(rows, neg_ref[0, :, c : c + 128], b * BLK)
            hits = hot if hits is None else hits + hot
        count = jnp.sum(hits.astype(f32), axis=1, keepdims=True)
        at = slice(b * BLK, (b + 1) * BLK)
        out_ref[0, at, 0:1] = jnp.log2(count)
        out_ref[0, at, 1:2] = jnp.log2(count + 1.0)


def neg_weights(neg_pad):
    return pl.pallas_call(
        count_kernel,
        grid=(GROUPS,),
        in_specs=[pl.BlockSpec((1, 1, PAD), lambda g: (g, 0, 0))],
        out_specs=pl.BlockSpec((1, ROWS, 2), lambda g: (g, 0, 0)),
        out_shape=jax.ShapeDtypeStruct((GROUPS, ROWS, 2), f32),
        compiler_params=params(),
        cost_estimate=cost(3),
        name="neg_weights",
    )(neg_pad.reshape(GROUPS, 1, PAD))


def query_kernel(rel_ref, *refs):
    own = refs[:PARTS]
    idx_ref, mat_ref, s_ref, q_ref = refs[PARTS:]
    column = jnp.broadcast_to(idx_ref[0].astype(f32), (128, CH)).T
    column = column.astype(jnp.int32).astype(jnp.int16)
    cols = lax.broadcasted_iota(jnp.int32, (CH, 128), 1).astype(jnp.int16)
    acc = None
    for b in range(NBLK):
        hot = jnp.concatenate(
            [
                jnp.where(cols + jnp.int16(first) == column, bf16(1), bf16(0))
                for first in (b * BLK, b * BLK + 128)
            ],
            axis=1,
        )
        part = mm(hot, block_of(own, b))
        acc = part if acc is None else acc + part
    rows = acc.astype(bf16)
    s_ref[...] = rows
    q_ref[...] = mm(mat_ref[0].astype(bf16).T, rows, NT).astype(bf16)


def make_queries(own, src_rows, rel_id, relation):
    return pl.pallas_call(
        query_kernel,
        grid_spec=pltpu.PrefetchScalarGridSpec(
            num_scalar_prefetch=1,
            grid=(NCH,),
            in_specs=[
                *[pl.BlockSpec((PART, D), lambda j, rel: (0, 0))] * PARTS,
                pl.BlockSpec((1, 1, CH), lambda j, rel: (j, 0, 0)),
                pl.BlockSpec((1, D, D), lambda j, rel: (rel[j // PER], 0, 0)),
            ],
            out_specs=[
                pl.BlockSpec((CH, D), lambda j, rel: (j, 0)),
                pl.BlockSpec((D, CH), lambda j, rel: (0, j)),
            ],
        ),
        out_shape=[
            jax.ShapeDtypeStruct((GROUPS * PAD, D), bf16),
            jax.ShapeDtypeStruct((D, GROUPS * PAD), bf16),
        ],
        compiler_params=params(),
        cost_estimate=cost(9),
        name="queries",
    )(rel_id, *own, src_rows, relation)


SUB = 32


def score_kernel(cnt_ref, *refs):
    nxt = refs[:PARTS]
    q_ref, dst_ref, wt_ref, gq_ref = refs[PARTS : PARTS + 4]
    dg = refs[PARTS + 4 : 2 * PARTS + 4]
    sc, nxt_t_ref, w0, w1, qs0, qs1, sl0, sl1, dacc = refs[2 * PARTS + 4 :]
    g = pl.program_id(0)
    rows = lax.broadcasted_iota(jnp.int32, (SUB, CH), 0)
    rows16 = lax.broadcasted_iota(jnp.int32, (BLK, CH), 0).astype(jnp.int16)

    @pl.when(g == 0)
    def _():
        dacc[...] = jnp.zeros_like(dacc)
        w1[...] = jnp.zeros_like(w1)
        for b in range(NBLK):
            nxt_t_ref[:, b * BLK : (b + 1) * BLK] = block_of(nxt, b).T
        qs1[...] = jnp.zeros_like(qs1)
        sl1[...] = jnp.zeros_like(sl1)

    def spread(b, w, qs):
        at = slice(b * BLK, (b + 1) * BLK)
        dacc[at, :] += mm(w[at, :], qs[...], NT)

    def finish(acc, sl, chunk):
        gq = (acc * sl[0:1, :]).astype(bf16)
        gq_ref[:, pl.ds(pl.multiple_of(chunk * CH, CH), CH)] = gq

    def stage(half, w, qs, sl, w_old, qs_old, sl_old, chunk_old):
        here = slice(half * CH, (half + 1) * CH)
        q = q_ref[:, here]
        dst = dst_ref[0, 0:1, here]
        top = jnp.full((8, CH), -jnp.inf, f32)
        hit = jnp.zeros((8, CH), f32)
        for b in range(NBLK):
            raw = mm(block_of(nxt, b), q)
            for i in range(BLK // SUB):
                at = slice(b * BLK + i * SUB, b * BLK + (i + 1) * SUB)
                mask = rows == dst - (b * BLK + i * SUB)
                val = raw[i * SUB : (i + 1) * SUB] * LOG2E + jnp.where(
                    mask, wt_ref[0, at, 1:2], wt_ref[0, at, 0:1]
                )
                sc[at, :] = val
                top = jnp.maximum(top, jnp.max(val.reshape(SUB // 8, 8, CH), axis=0))
                hit = hit + jnp.sum(jnp.where(mask, val, 0.0).reshape(SUB // 8, 8, CH), axis=0)
            spread(b, w_old, qs_old)
        top = jnp.max(top, axis=0, keepdims=True)
        hit = jnp.sum(hit, axis=0, keepdims=True)
        tot = jnp.zeros((8, CH), f32)
        acc = None
        for b in range(NBLK):
            for i in range(BLK // SUB):
                at = slice(b * BLK + i * SUB, b * BLK + (i + 1) * SUB)
                e = jnp.exp2(sc[at, :] - top)
                tot = tot + jnp.sum(e.reshape(SUB // 8, 8, CH), axis=0)
                w[at, :] = e.astype(bf16)
            at = slice(b * BLK, (b + 1) * BLK)
            part = mm(nxt_t_ref[:, at], w_old[at, :])
            acc = part if acc is None else acc + part
        finish(acc, sl_old, chunk_old)
        tot = jnp.sum(tot, axis=0, keepdims=True)
        gain = (jnp.exp2(hit - top) - tot).astype(bf16)
        lane = lax.broadcasted_iota(jnp.int32, (1, CH), 1) + half * CH
        live = jnp.logical_and(lane < SLOTS, g * SLOTS + lane < cnt_ref[0])
        scale = jnp.where(live, 1.0 / tot, 0.0)
        sl[...] = jnp.broadcast_to(scale, (8, CH))
        qs[...] = (q.astype(f32) * scale).astype(bf16)
        for b in range(NBLK):
            at = slice(b * BLK, (b + 1) * BLK)
            mask = rows16 == (dst - b * BLK).astype(jnp.int16)
            w[at, :] = jnp.where(mask, gain, w[at, :])

    stage(0, w0, qs0, sl0, w1, qs1, sl1, jnp.maximum(2 * g - 1, 0))
    stage(1, w1, qs1, sl1, w0, qs0, sl0, 2 * g)

    @pl.when(g == GROUPS - 1)
    def _():
        for b in range(NBLK):
            spread(b, w1, qs1)
        finish(mm(nxt_t_ref[...], w1[...]), sl1, 2 * g + 1)
        for p in range(PARTS):
            dg[p][...] = dacc[p * PART : (p + 1) * PART, :].astype(bf16)


def score_side(nxt, q, dst_rows, weights, counts):
    return pl.pallas_call(
        score_kernel,
        grid_spec=pltpu.PrefetchScalarGridSpec(
            num_scalar_prefetch=1,
            grid=(GROUPS,),
            in_specs=[
                *[pl.BlockSpec((PART, D), lambda j, cnt: (0, 0))] * PARTS,
                pl.BlockSpec((D, PAD), lambda j, cnt: (0, j)),
                pl.BlockSpec((1, 1, PAD), lambda j, cnt: (j, 0, 0)),
                pl.BlockSpec((1, ROWS, 2), lambda j, cnt: (j, 0, 0)),
            ],
            out_specs=[
                pl.BlockSpec((D, GROUPS * PAD), lambda j, cnt: (0, 0)),
                *[pl.BlockSpec((PART, D), lambda j, cnt: (0, 0))] * PARTS,
            ],
            scratch_shapes=[
                pltpu.VMEM((ROWS, CH), f32),
                pltpu.VMEM((D, ROWS), bf16),
                pltpu.VMEM((ROWS, CH), bf16),
                pltpu.VMEM((ROWS, CH), bf16),
                pltpu.VMEM((D, CH), bf16),
                pltpu.VMEM((D, CH), bf16),
                pltpu.VMEM((8, CH), f32),
                pltpu.VMEM((8, CH), f32),
                pltpu.VMEM((ROWS, D), f32),
            ],
        ),
        out_shape=[
            jax.ShapeDtypeStruct((D, GROUPS * PAD), bf16),
            *[jax.ShapeDtypeStruct((PART, D), bf16)] * PARTS,
        ],
        compiler_params=params(),
        cost_estimate=cost(28),
        name="scores",
    )(counts, *nxt, q, dst_rows, weights)


def operator_kernel(rel_ref, gq_ref, s_ref, out_ref, acc):
    g = pl.program_id(0)

    @pl.when(g == 0)
    def _():
        acc[...] = jnp.zeros_like(acc)

    acc[rel_ref[g]] += mm(gq_ref[...], s_ref[...])

    @pl.when(g == GROUPS - 1)
    def _():
        for k in range(acc.shape[0]):
            out_ref[k] = acc[k].T.astype(bf16)


def operator_side(gq, s, rel_id, kinds):
    return pl.pallas_call(
        operator_kernel,
        grid_spec=pltpu.PrefetchScalarGridSpec(
            num_scalar_prefetch=1,
            grid=(GROUPS,),
            in_specs=[
                pl.BlockSpec((D, PAD), lambda j, rel: (0, j)),
                pl.BlockSpec((PAD, D), lambda j, rel: (j, 0)),
            ],
            out_specs=pl.BlockSpec((kinds, D, D), lambda j, rel: (0, 0, 0)),
            scratch_shapes=[pltpu.VMEM((kinds, D, D), f32)],
        ),
        out_shape=jax.ShapeDtypeStruct((kinds, D, D), bf16),
        compiler_params=params(),
        cost_estimate=cost(2),
        name="operator_grads",
    )(rel_id, gq, s)


def source_kernel(rel_ref, gq_ref, src_ref, mat_ref, *refs):
    out, acc = refs[:PARTS], refs[PARTS]
    g = pl.program_id(0)

    @pl.when(g == 0)
    def _():
        acc[...] = jnp.zeros_like(acc)

    grad = mm(mat_ref[0].astype(bf16), gq_ref[...]).astype(bf16)
    rows = lax.broadcasted_iota(jnp.int32, (BLK, PAD), 0).astype(jnp.int16)
    for b in range(NBLK):
        at = slice(b * BLK, (b + 1) * BLK)
        acc[at, :] += mm(one_hot(rows, src_ref[0], b * BLK), grad, NT)

    @pl.when(g == GROUPS - 1)
    def _():
        for p in range(PARTS):
            out[p][...] = acc[p * PART : (p + 1) * PART, :].astype(bf16)


def source_side(gq, src_rows, rel_id, relation):
    return pl.pallas_call(
        source_kernel,
        grid_spec=pltpu.PrefetchScalarGridSpec(
            num_scalar_prefetch=1,
            grid=(GROUPS,),
            in_specs=[
                pl.BlockSpec((D, PAD), lambda j, rel: (0, j)),
                pl.BlockSpec((1, 1, PAD), lambda j, rel: (j, 0, 0)),
                pl.BlockSpec((1, D, D), lambda j, rel: (rel[j], 0, 0)),
            ],
            out_specs=[pl.BlockSpec((PART, D), lambda j, rel: (0, 0))] * PARTS,
            scratch_shapes=[pltpu.VMEM((ROWS, D), f32)],
        ),
        out_shape=[jax.ShapeDtypeStruct((PART, D), bf16)] * PARTS,
        compiler_params=params(),
        cost_estimate=cost(8),
        name="source_grads",
    )(rel_id, gq, src_rows, relation)


def rowwise(param, accum, grad):
    fresh = accum + jnp.mean(grad * grad, -1)
    return (param - learn_rate * grad / jnp.sqrt(fresh)[..., None], fresh)


def shift_dom(block, by):
    size = lax.axis_size("dom")
    return lax.ppermute(block, "dom", [(i, (i + by) % size) for i in range(size)])


def swap_z(block):
    return lax.ppermute(block, "rep", [(i, i ^ 1) for i in range(8)])


def shift_x(block, by):
    return lax.ppermute(block, "rep", [(i, (i + 2 * by) % 8) for i in range(8)])


def spread_x(pair):
    return [pair] + [shift_x(pair, -k) for k in (1, 2, 3)]


def send_x(blocks):
    return [blocks[0]] + [shift_x(blocks[k], k) for k in (1, 2, 3)]


def add_up(blocks, after, dtype, copies=None):
    stacked = len(blocks) == 1
    shape = blocks[0].shape[1:] if stacked else blocks[0].shape
    whole = pl.BlockSpec(memory_space=pltpu.VMEM)

    def kernel(*refs):
        out = refs[-1]
        total = None
        if stacked:
            for i in range(blocks[0].shape[0]):
                part = refs[0][i].astype(f32)
                total = part if total is None else total + part
            total = total.astype(dtype)
        else:
            for ref in refs[: len(blocks)]:
                part = ref[...].astype(f32)
                total = part if total is None else total + part
            total = total.astype(dtype)
        if copies is None:
            out[...] = total
        else:
            for i in range(copies):
                out[i] = total

    return pl.pallas_call(
        kernel,
        in_specs=[whole] * len(blocks) + [pl.BlockSpec(memory_space=pl.ANY)],
        out_specs=whole,
        out_shape=jax.ShapeDtypeStruct(shape if copies is None else (copies,) + shape, dtype),
        compiler_params=pltpu.CompilerParams(vmem_limit_bytes=16 * MB),
        cost_estimate=cost(1),
        name="add_up",
    )(*blocks, after)


def turned(index):
    rep = lax.axis_index("rep")
    return ((index - PART * (rep // 2)) % ROWS) ^ (256 * (rep % 2))


def spread_total(shares, kinds):
    cores = [[2 * i + c for i in range(16)] for c in range(2)]
    half = lax.all_to_all(shares, "dom", 0, 0, axis_index_groups=cores)
    other = lax.ppermute(half, "dom", [(i, i ^ 1) for i in range(32)])
    second = lax.axis_index("dom") % 2 == 1
    pairs = [jnp.where(second, other, half), jnp.where(second, half, other)]
    return jnp.stack(pairs, 1).reshape(kinds, D, D)


def pad_slots(index, fill):
    return jnp.pad(index.reshape(GROUPS, SLOTS), ((0, 0), (0, PAD - SLOTS)), constant_values=fill)


def source_stage(own, src_pad, rel_id, relation):
    return make_queries(own, src_pad.reshape(NCH, 1, CH), rel_id, relation)


def target_stage(nxt, q, s, dst_pad, weights, rel_id, counts, kinds):
    out = score_side(nxt, q, dst_pad.reshape(GROUPS, 1, PAD), weights, counts)
    return out[0], out[1:], operator_side(out[0], s, rel_id, kinds)


def back_stage(gq, src_pad, rel_id, relation):
    return source_side(gq, src_pad.reshape(GROUPS, 1, PAD), rel_id, relation)


def local_grads(own, nxt, relation, src_index, dst_index, neg_index, rel_id, counts):
    own, nxt = own.astype(bf16), nxt.astype(bf16)
    src_pad = pad_slots(src_index, -1)
    weights = neg_weights(pad_slots(neg_index, -1))
    own = [own[k * PART : (k + 1) * PART] for k in range(PARTS)]
    nxt = [nxt[k * PART : (k + 1) * PART] for k in range(PARTS)]
    s, q = source_stage(own, src_pad, rel_id, relation)
    gq, dst_grad, rel_grad = target_stage(
        nxt, q, s, pad_slots(dst_index, -1), weights, rel_id, counts, relation.shape[0]
    )
    src_grad = back_stage(gq, src_pad, rel_id, relation)
    return jnp.concatenate(src_grad), jnp.concatenate(dst_grad), rel_grad


def on_device(
    entity, entity_accum, relation, relation_accum, src_index, dst_index, neg_index, rel_id, counts
):
    ent_b = entity.astype(bf16)
    src_pad = pad_slots(turned(src_index), -1)
    dst_pad = pad_slots(turned(dst_index), -1)
    neg_pad = pad_slots(turned(neg_index), -1)
    other = swap_z(ent_b)
    own = spread_x(jnp.concatenate([ent_b, other]))
    nxt = [shift_dom(block, -1) for block in own]
    weights = neg_weights(neg_pad)
    s, q = source_stage(own, src_pad, rel_id, relation)
    gq, dst_grad, rel_grad = target_stage(
        nxt, q, s, dst_pad, weights, rel_id, counts, relation.shape[0]
    )
    kinds = relation.shape[0]
    dst_blocks = send_x(dst_grad)
    got = lax.all_to_all(rel_grad.reshape(32, -1, D), "dom", 0, 0)
    src_grad = back_stage(gq, src_pad, rel_id, relation)
    src_blocks = send_x(src_grad)
    mine = add_up([got], src_grad[0], bf16, 8)
    every = lax.all_to_all(mine, "rep", 0, 0)
    dst_sum = add_up(dst_blocks, mine, bf16)
    moved = shift_dom(dst_sum, 1)
    shares = add_up([every], dst_sum, f32, 16)
    rel_total = spread_total(shares, kinds)
    total = sum(block.astype(f32) for block in src_blocks + [moved])
    grads = total[:256] + swap_z(total[256:].astype(bf16)).astype(f32)
    entity_new, entity_accum_new = rowwise(entity, entity_accum, grads)
    relation_new, relation_accum_new = rowwise(relation, relation_accum, rel_total)
    return (entity_new, entity_accum_new, relation_new, relation_accum_new)


def solution(mesh):
    placed = (
        P(("dom", "rep"), None),
        P(("dom", "rep")),
        P(),
        P(),
        P(("dom", "rep")),
        P(("dom", "rep")),
        P(("dom", "rep"), None),
        P(("dom", "rep")),
        P(("dom", "rep")),
    )
    return jax.shard_map(
        on_device,
        mesh=mesh,
        in_specs=placed,
        out_specs=(P(("dom", "rep"), None), P(("dom", "rep")), P(), P()),
        check_vma=False,
    )
```

```python
import functools
import jax
import jax.numpy as jnp
from jax import lax
from jax.experimental import pallas as pl
from jax.experimental.pallas import tpu as pltpu
from jax.sharding import PartitionSpec as P

learn_rate = 0.1
LOG2E = 1.4426950408889634
GROUPS = 4
SLOTS = 1000
PAD = 1024
ROWS = 2048
D = 256
BLK = 256
NBLK = ROWS // BLK
CH = 512
NCH = GROUPS * PAD // CH
PER = PAD // CH
bf16 = jnp.bfloat16
f32 = jnp.float32

NN = (((1,), (0,)), ((), ()))
NT = (((1,), (1,)), ((), ()))
MB = 1024 * 1024


def mm(a, b, dims=NN):
    return lax.dot_general(a, b, dims, preferred_element_type=f32)


def cost(us):
    return pl.CostEstimate(flops=int(us * 5e8), bytes_accessed=int(us * 3.5e6), transcendentals=0)


def params():
    return pltpu.CompilerParams(
        dimension_semantics=("arbitrary",), vmem_limit_bytes=48 * MB
    )


def one_hot(rows, index, first):
    return jnp.where(rows == (index - first).astype(jnp.int16), bf16(1), bf16(0))


PARTS = 4
PART = ROWS // PARTS


def block_of(parts, b):
    first = b * BLK % PART
    return parts[b * BLK // PART][first : first + BLK, :]


def count_kernel(neg_ref, out_ref):
    rows = lax.broadcasted_iota(jnp.int32, (BLK, 128), 0).astype(jnp.int16)
    for b in range(NBLK):
        hits = None
        for c in range(0, PAD, 128):
            hot = one_hot(rows, neg_ref[0, :, c : c + 128], b * BLK)
            hits = hot if hits is None else hits + hot
        count = jnp.sum(hits.astype(f32), axis=1, keepdims=True)
        lane = lax.broadcasted_iota(jnp.int32, (BLK, 8), 1)
        out_ref[0, :, b * BLK : (b + 1) * BLK] = jnp.where(lane == 0, count, count + 1.0).T
    out_ref[0] = jnp.log2(out_ref[0])


def neg_weights(neg_pad):
    return pl.pallas_call(
        count_kernel,
        grid=(GROUPS,),
        in_specs=[pl.BlockSpec((1, 1, PAD), lambda g: (g, 0, 0))],
        out_specs=pl.BlockSpec((1, 8, ROWS), lambda g: (g, 0, 0)),
        out_shape=jax.ShapeDtypeStruct((GROUPS, 8, ROWS), f32),
        compiler_params=params(),
        cost_estimate=cost(3),
        name="neg_weights",
    )(neg_pad.reshape(GROUPS, 1, PAD))


def query_kernel(rel_ref, *refs):
    own = refs[:PARTS]
    idx_ref, mat_ref, _, s_ref, q_ref = refs[PARTS:]
    column = jnp.broadcast_to(idx_ref[0].astype(f32), (128, CH)).T
    column = column.astype(jnp.int32).astype(jnp.int16)
    cols = lax.broadcasted_iota(jnp.int32, (CH, 128), 1).astype(jnp.int16)
    acc = None
    for b in range(NBLK):
        hot = jnp.concatenate(
            [
                jnp.where(cols + jnp.int16(first) == column, bf16(1), bf16(0))
                for first in (b * BLK, b * BLK + 128)
            ],
            axis=1,
        )
        part = mm(hot, block_of(own, b))
        acc = part if acc is None else acc + part
    rows = acc.astype(bf16)
    s_ref[...] = rows
    q_ref[...] = mm(mat_ref[0].astype(bf16).T, rows, NT).astype(bf16)


def make_queries(own, src_rows, rel_id, relation, after):
    return pl.pallas_call(
        query_kernel,
        grid_spec=pltpu.PrefetchScalarGridSpec(
            num_scalar_prefetch=1,
            grid=(NCH,),
            in_specs=[
                *[pl.BlockSpec((PART, D), lambda j, rel: (0, 0))] * PARTS,
                pl.BlockSpec((1, 1, CH), lambda j, rel: (j, 0, 0)),
                pl.BlockSpec((1, D, D), lambda j, rel: (rel[j // PER], 0, 0)),
                pl.BlockSpec(memory_space=pl.ANY),
            ],
            out_specs=[
                pl.BlockSpec((CH, D), lambda j, rel: (j, 0)),
                pl.BlockSpec((D, CH), lambda j, rel: (0, j)),
            ],
        ),
        out_shape=[
            jax.ShapeDtypeStruct((GROUPS * PAD, D), bf16),
            jax.ShapeDtypeStruct((D, GROUPS * PAD), bf16),
        ],
        compiler_params=params(),
        cost_estimate=cost(9),
        name="queries",
    )(rel_id, *own, src_rows, relation, after)


SUB = 32


def score_kernel(cnt_ref, *refs):
    nxt = refs[:PARTS]
    q_ref, dst_ref, wt_ref, gq_ref = refs[PARTS : PARTS + 4]
    dg = refs[PARTS + 4 : 2 * PARTS + 4]
    sc, nxt_t_ref, w0, w1, qs0, qs1, sl0, sl1, dacc, wcol = refs[2 * PARTS + 4 :]
    g = pl.program_id(0)
    rows = lax.broadcasted_iota(jnp.int32, (SUB, CH), 0)
    rows16 = lax.broadcasted_iota(jnp.int32, (BLK, CH), 0).astype(jnp.int16)

    @pl.when(g == 0)
    def _():
        dacc[...] = jnp.zeros_like(dacc)
        w1[...] = jnp.zeros_like(w1)
        for b in range(NBLK):
            nxt_t_ref[:, b * BLK : (b + 1) * BLK] = block_of(nxt, b).T
        qs1[...] = jnp.zeros_like(qs1)
        sl1[...] = jnp.zeros_like(sl1)

    for b in range(NBLK):
        at = slice(b * BLK, (b + 1) * BLK)
        wcol[at, :] = wt_ref[0, :, at].T

    def spread(b, w, qs):
        at = slice(b * BLK, (b + 1) * BLK)
        dacc[at, :] += mm(w[at, :], qs[...], NT)

    def finish(acc, sl, chunk):
        gq = (acc * sl[0:1, :]).astype(bf16)
        gq_ref[:, pl.ds(pl.multiple_of(chunk * CH, CH), CH)] = gq

    def stage(half, w, qs, sl, w_old, qs_old, sl_old, chunk_old):
        here = slice(half * CH, (half + 1) * CH)
        q = q_ref[:, here]
        dst = dst_ref[0, 0:1, here]
        top = jnp.full((8, CH), -jnp.inf, f32)
        hit = jnp.zeros((8, CH), f32)
        for b in range(NBLK):
            raw = mm(block_of(nxt, b), q)
            for i in range(BLK // SUB):
                at = slice(b * BLK + i * SUB, b * BLK + (i + 1) * SUB)
                mask = rows == dst - (b * BLK + i * SUB)
                val = raw[i * SUB : (i + 1) * SUB] * LOG2E + jnp.where(
                    mask, wcol[at, 1:2], wcol[at, 0:1]
                )
                sc[at, :] = val
                top = jnp.maximum(top, jnp.max(val.reshape(SUB // 8, 8, CH), axis=0))
                hit = hit + jnp.sum(jnp.where(mask, val, 0.0).reshape(SUB // 8, 8, CH), axis=0)
            spread(b, w_old, qs_old)
        top = jnp.max(top, axis=0, keepdims=True)
        hit = jnp.sum(hit, axis=0, keepdims=True)
        tot = jnp.zeros((8, CH), f32)
        acc = None
        for b in range(NBLK):
            for i in range(BLK // SUB):
                at = slice(b * BLK + i * SUB, b * BLK + (i + 1) * SUB)
                e = jnp.exp2(sc[at, :] - top)
                tot = tot + jnp.sum(e.reshape(SUB // 8, 8, CH), axis=0)
                w[at, :] = e.astype(bf16)
            at = slice(b * BLK, (b + 1) * BLK)
            part = mm(nxt_t_ref[:, at], w_old[at, :])
            acc = part if acc is None else acc + part
        finish(acc, sl_old, chunk_old)
        tot = jnp.sum(tot, axis=0, keepdims=True)
        gain = (jnp.exp2(hit - top) - tot).astype(bf16)
        lane = lax.broadcasted_iota(jnp.int32, (1, CH), 1) + half * CH
        live = jnp.logical_and(lane < SLOTS, g * SLOTS + lane < cnt_ref[0])
        scale = jnp.where(live, 1.0 / tot, 0.0)
        sl[...] = jnp.broadcast_to(scale, (8, CH))
        qs[...] = (q.astype(f32) * scale).astype(bf16)
        for b in range(NBLK):
            at = slice(b * BLK, (b + 1) * BLK)
            mask = rows16 == (dst - b * BLK).astype(jnp.int16)
            w[at, :] = jnp.where(mask, gain, w[at, :])

    stage(0, w0, qs0, sl0, w1, qs1, sl1, jnp.maximum(2 * g - 1, 0))
    stage(1, w1, qs1, sl1, w0, qs0, sl0, 2 * g)

    @pl.when(g == GROUPS - 1)
    def _():
        for b in range(NBLK):
            spread(b, w1, qs1)
        finish(mm(nxt_t_ref[...], w1[...]), sl1, 2 * g + 1)
        for p in range(PARTS):
            dg[p][...] = dacc[p * PART : (p + 1) * PART, :].astype(bf16)


def score_side(nxt, q, dst_rows, weights, counts):
    return pl.pallas_call(
        score_kernel,
        grid_spec=pltpu.PrefetchScalarGridSpec(
            num_scalar_prefetch=1,
            grid=(GROUPS,),
            in_specs=[
                *[pl.BlockSpec((PART, D), lambda j, cnt: (0, 0))] * PARTS,
                pl.BlockSpec((D, PAD), lambda j, cnt: (0, j)),
                pl.BlockSpec((1, 1, PAD), lambda j, cnt: (j, 0, 0)),
                pl.BlockSpec((1, 8, ROWS), lambda j, cnt: (j, 0, 0)),
            ],
            out_specs=[
                pl.BlockSpec((D, GROUPS * PAD), lambda j, cnt: (0, 0)),
                *[pl.BlockSpec((PART, D), lambda j, cnt: (0, 0))] * PARTS,
            ],
            scratch_shapes=[
                pltpu.VMEM((ROWS, CH), f32),
                pltpu.VMEM((D, ROWS), bf16),
                pltpu.VMEM((ROWS, CH), bf16),
                pltpu.VMEM((ROWS, CH), bf16),
                pltpu.VMEM((D, CH), bf16),
                pltpu.VMEM((D, CH), bf16),
                pltpu.VMEM((8, CH), f32),
                pltpu.VMEM((8, CH), f32),
                pltpu.VMEM((ROWS, D), f32),
                pltpu.VMEM((ROWS, 8), f32),
            ],
        ),
        out_shape=[
            jax.ShapeDtypeStruct((D, GROUPS * PAD), bf16),
            *[jax.ShapeDtypeStruct((PART, D), bf16)] * PARTS,
        ],
        compiler_params=params(),
        cost_estimate=cost(28),
        name="scores",
    )(counts, *nxt, q, dst_rows, weights)


def operator_kernel(rel_ref, gq_ref, s_ref, out_ref, acc):
    g = pl.program_id(0)

    @pl.when(g == 0)
    def _():
        acc[...] = jnp.zeros_like(acc)

    acc[rel_ref[g]] += mm(gq_ref[...], s_ref[...])

    @pl.when(g == GROUPS - 1)
    def _():
        for k in range(acc.shape[0]):
            out_ref[k] = acc[k].T.astype(bf16)


def operator_side(gq, s, rel_id, kinds):
    return pl.pallas_call(
        operator_kernel,
        grid_spec=pltpu.PrefetchScalarGridSpec(
            num_scalar_prefetch=1,
            grid=(GROUPS,),
            in_specs=[
                pl.BlockSpec((D, PAD), lambda j, rel: (0, j)),
                pl.BlockSpec((PAD, D), lambda j, rel: (j, 0)),
            ],
            out_specs=pl.BlockSpec((kinds, D, D), lambda j, rel: (0, 0, 0)),
            scratch_shapes=[pltpu.VMEM((kinds, D, D), f32)],
        ),
        out_shape=jax.ShapeDtypeStruct((kinds, D, D), bf16),
        compiler_params=params(),
        cost_estimate=cost(2),
        name="operator_grads",
    )(rel_id, gq, s)


def source_kernel(rel_ref, gq_ref, src_ref, mat_ref, *refs):
    out, acc = refs[:PARTS], refs[PARTS]
    g = pl.program_id(0)

    @pl.when(g == 0)
    def _():
        acc[...] = jnp.zeros_like(acc)

    grad = mm(mat_ref[0].astype(bf16), gq_ref[...]).astype(bf16)
    rows = lax.broadcasted_iota(jnp.int32, (BLK, PAD), 0).astype(jnp.int16)
    for b in range(NBLK):
        at = slice(b * BLK, (b + 1) * BLK)
        acc[at, :] += mm(one_hot(rows, src_ref[0], b * BLK), grad, NT)

    @pl.when(g == GROUPS - 1)
    def _():
        for p in range(PARTS):
            out[p][...] = acc[p * PART : (p + 1) * PART, :].astype(bf16)


def source_side(gq, src_rows, rel_id, relation):
    return pl.pallas_call(
        source_kernel,
        grid_spec=pltpu.PrefetchScalarGridSpec(
            num_scalar_prefetch=1,
            grid=(GROUPS,),
            in_specs=[
                pl.BlockSpec((D, PAD), lambda j, rel: (0, j)),
                pl.BlockSpec((1, 1, PAD), lambda j, rel: (j, 0, 0)),
                pl.BlockSpec((1, D, D), lambda j, rel: (rel[j], 0, 0)),
            ],
            out_specs=[pl.BlockSpec((PART, D), lambda j, rel: (0, 0))] * PARTS,
            scratch_shapes=[pltpu.VMEM((ROWS, D), f32)],
        ),
        out_shape=[jax.ShapeDtypeStruct((PART, D), bf16)] * PARTS,
        compiler_params=params(),
        cost_estimate=cost(8),
        name="source_grads",
    )(rel_id, gq, src_rows, relation)


def rowwise(param, accum, grad):
    fresh = accum + jnp.mean(grad * grad, -1)
    return (param - learn_rate * grad / jnp.sqrt(fresh)[..., None], fresh)


def shift_dom(block, by):
    size = lax.axis_size("dom")
    return lax.ppermute(block, "dom", [(i, (i + by) % size) for i in range(size)])


def swap_z(block):
    return lax.ppermute(block, "rep", [(i, i ^ 1) for i in range(8)])


def shift_x(block, by):
    return lax.ppermute(block, "rep", [(i, (i + 2 * by) % 8) for i in range(8)])


def spread_x(pair):
    return [pair] + [shift_x(pair, -k) for k in (1, 2, 3)]


def send_x(blocks):
    return [blocks[0]] + [shift_x(blocks[k], k) for k in (1, 2, 3)]


def add_up(blocks, after, dtype, copies=None):
    stacked = len(blocks) == 1
    shape = blocks[0].shape[1:] if stacked else blocks[0].shape
    whole = pl.BlockSpec(memory_space=pltpu.VMEM)

    def kernel(*refs):
        out = refs[-1]
        total = None
        if stacked:
            for i in range(blocks[0].shape[0]):
                part = refs[0][i].astype(f32)
                total = part if total is None else total + part
            total = total.astype(dtype)
        else:
            for ref in refs[: len(blocks)]:
                part = ref[...].astype(f32)
                total = part if total is None else total + part
            total = total.astype(dtype)
        if copies is None:
            out[...] = total
        else:
            for i in range(copies):
                out[i] = total

    return pl.pallas_call(
        kernel,
        in_specs=[whole] * len(blocks) + [pl.BlockSpec(memory_space=pl.ANY)],
        out_specs=whole,
        out_shape=jax.ShapeDtypeStruct(shape if copies is None else (copies,) + shape, dtype),
        compiler_params=pltpu.CompilerParams(vmem_limit_bytes=16 * MB),
        cost_estimate=cost(1),
        name="add_up",
    )(*blocks, after)


def split_sum(blocks):
    half = blocks[0].shape[0] // 2
    whole = pl.BlockSpec(memory_space=pltpu.VMEM)

    def kernel(*refs):
        for out, at in ((refs[-2], slice(0, half)), (refs[-1], slice(half, 2 * half))):
            total = None
            for ref in refs[:-2]:
                part = ref[at, :].astype(f32)
                total = part if total is None else total + part
            out[...] = total.astype(out.dtype)

    return pl.pallas_call(
        kernel,
        in_specs=[whole] * len(blocks),
        out_specs=[whole] * 2,
        out_shape=[jax.ShapeDtypeStruct((half, D), f32), jax.ShapeDtypeStruct((half, D), bf16)],
        compiler_params=pltpu.CompilerParams(vmem_limit_bytes=16 * MB),
        cost_estimate=cost(1),
        name="split_sum",
    )(*blocks)


def turned(index):
    rep = lax.axis_index("rep")
    return ((index - PART * (rep // 2)) % ROWS) ^ (256 * (rep % 2))


def spread_total(shares, kinds):
    cores = [[2 * i + c for i in range(16)] for c in range(2)]
    half = lax.all_to_all(shares, "dom", 0, 0, axis_index_groups=cores)
    other = lax.ppermute(half, "dom", [(i, i ^ 1) for i in range(32)])
    second = lax.axis_index("dom") % 2 == 1
    pairs = [jnp.where(second, other, half), jnp.where(second, half, other)]
    return jnp.stack(pairs, 1).reshape(kinds, D, D)


def pad_slots(index, fill):
    return jnp.pad(index.reshape(GROUPS, SLOTS), ((0, 0), (0, PAD - SLOTS)), constant_values=fill)


def source_stage(own, src_pad, rel_id, relation, after):
    return make_queries(own, src_pad.reshape(NCH, 1, CH), rel_id, relation, after)


def target_stage(nxt, q, s, dst_pad, weights, rel_id, counts, kinds):
    out = score_side(nxt, q, dst_pad.reshape(GROUPS, 1, PAD), weights, counts)
    return out[0], out[1:], operator_side(out[0], s, rel_id, kinds)


def back_stage(gq, src_pad, rel_id, relation):
    return source_side(gq, src_pad.reshape(GROUPS, 1, PAD), rel_id, relation)


def local_grads(own, nxt, relation, src_index, dst_index, neg_index, rel_id, counts):
    own, nxt = own.astype(bf16), nxt.astype(bf16)
    src_pad = pad_slots(src_index, -1)
    weights = neg_weights(pad_slots(neg_index, -1))
    own = [own[k * PART : (k + 1) * PART] for k in range(PARTS)]
    nxt = [nxt[k * PART : (k + 1) * PART] for k in range(PARTS)]
    s, q = source_stage(own, src_pad, rel_id, relation, nxt[0])
    gq, dst_grad, rel_grad = target_stage(
        nxt, q, s, pad_slots(dst_index, -1), weights, rel_id, counts, relation.shape[0]
    )
    src_grad = back_stage(gq, src_pad, rel_id, relation)
    return jnp.concatenate(src_grad), jnp.concatenate(dst_grad), rel_grad


def on_device(
    entity, entity_accum, relation, relation_accum, src_index, dst_index, neg_index, rel_id, counts
):
    ent_b = entity.astype(bf16)
    src_pad = pad_slots(turned(src_index), -1)
    dst_pad = pad_slots(turned(dst_index), -1)
    neg_pad = pad_slots(turned(neg_index), -1)
    other = swap_z(ent_b)
    own = spread_x(jnp.concatenate([ent_b, other]))
    nxt = [shift_dom(block, -1) for block in own]
    weights = neg_weights(neg_pad)
    s, q = source_stage(own, src_pad, rel_id, relation, nxt[0])
    gq, dst_grad, rel_grad = target_stage(
        nxt, q, s, dst_pad, weights, rel_id, counts, relation.shape[0]
    )
    kinds = relation.shape[0]
    dst_blocks = send_x(dst_grad)
    got = lax.all_to_all(rel_grad.reshape(32, -1, D), "dom", 0, 0)
    src_grad = back_stage(gq, src_pad, rel_id, relation)
    src_blocks = send_x(src_grad)
    mine = add_up([got], src_grad[0], f32)
    zsum = mine + swap_z(mine)
    dst_sum = add_up(dst_blocks, mine, bf16)
    moved = shift_dom(dst_sum, 1)
    keep, give = split_sum(src_blocks + [moved])
    shares = add_up([zsum] + [shift_x(zsum, k) for k in (1, 2, 3)], give, f32, 16)
    rel_total = spread_total(shares, kinds)
    grads = keep + swap_z(give).astype(f32)
    entity_new, entity_accum_new = rowwise(entity, entity_accum, grads)
    relation_new, relation_accum_new = rowwise(relation, relation_accum, rel_total)
    return (entity_new, entity_accum_new, relation_new, relation_accum_new)


def solution(mesh):
    placed = (
        P(("dom", "rep"), None),
        P(("dom", "rep")),
        P(),
        P(),
        P(("dom", "rep")),
        P(("dom", "rep")),
        P(("dom", "rep"), None),
        P(("dom", "rep")),
        P(("dom", "rep")),
    )
    return jax.shard_map(
        on_device,
        mesh=mesh,
        in_specs=placed,
        out_specs=(P(("dom", "rep"), None), P(("dom", "rep")), P(), P()),
        check_vma=False,
    )
```

```python
import functools
import jax
import jax.numpy as jnp
from jax import lax
from jax.experimental import pallas as pl
from jax.experimental.pallas import tpu as pltpu
from jax.sharding import PartitionSpec as P

learn_rate = 0.1
LOG2E = 1.4426950408889634
GROUPS = 4
SLOTS = 1000
PAD = 1024
ROWS = 2048
D = 256
BLK = 256
NBLK = ROWS // BLK
CH = 512
NCH = GROUPS * PAD // CH
PER = PAD // CH
bf16 = jnp.bfloat16
f32 = jnp.float32

NN = (((1,), (0,)), ((), ()))
NT = (((1,), (1,)), ((), ()))
MB = 1024 * 1024


def mm(a, b, dims=NN):
    return lax.dot_general(a, b, dims, preferred_element_type=f32)


def cost(us):
    return pl.CostEstimate(flops=int(us * 5e8), bytes_accessed=int(us * 3.5e6), transcendentals=0)


def params():
    return pltpu.CompilerParams(
        dimension_semantics=("arbitrary",), vmem_limit_bytes=48 * MB
    )


def one_hot(rows, index, first):
    return jnp.where(rows == (index - first).astype(jnp.int16), bf16(1), bf16(0))


PARTS = 4
PART = ROWS // PARTS


def block_of(parts, b):
    first = b * BLK % PART
    return parts[b * BLK // PART][first : first + BLK, :]


def count_kernel(neg_ref, out_ref):
    rows = lax.broadcasted_iota(jnp.int32, (BLK, 128), 0).astype(jnp.int16)
    for b in range(NBLK):
        hits = None
        for c in range(0, PAD, 128):
            hot = one_hot(rows, neg_ref[0, :, c : c + 128], b * BLK)
            hits = hot if hits is None else hits + hot
        count = jnp.sum(hits.astype(f32), axis=1, keepdims=True)
        lane = lax.broadcasted_iota(jnp.int32, (BLK, 8), 1)
        out_ref[0, :, b * BLK : (b + 1) * BLK] = jnp.where(lane == 0, count, count + 1.0).T
    out_ref[0] = jnp.log2(out_ref[0])


def neg_weights(neg_pad):
    return pl.pallas_call(
        count_kernel,
        grid=(GROUPS,),
        in_specs=[pl.BlockSpec((1, 1, PAD), lambda g: (g, 0, 0))],
        out_specs=pl.BlockSpec((1, 8, ROWS), lambda g: (g, 0, 0)),
        out_shape=jax.ShapeDtypeStruct((GROUPS, 8, ROWS), f32),
        compiler_params=params(),
        cost_estimate=cost(3),
        name="neg_weights",
    )(neg_pad.reshape(GROUPS, 1, PAD))


def query_kernel(rel_ref, *refs):
    own = refs[:PARTS]
    idx_ref, mat_ref, _, s_ref, q_ref = refs[PARTS:]
    column = jnp.broadcast_to(idx_ref[0].astype(f32), (128, PAD)).T
    column = column.astype(jnp.int32).astype(jnp.int16)
    cols = lax.broadcasted_iota(jnp.int32, (PAD, 128), 1).astype(jnp.int16)
    acc = None
    for b in range(NBLK):
        hot = jnp.concatenate(
            [
                jnp.where(cols + jnp.int16(first) == column, bf16(1), bf16(0))
                for first in (b * BLK, b * BLK + 128)
            ],
            axis=1,
        )
        part = mm(hot, block_of(own, b))
        acc = part if acc is None else acc + part
    rows = acc.astype(bf16)
    s_ref[...] = rows
    q_ref[...] = mm(mat_ref[0].astype(bf16).T, rows, NT).astype(bf16)


def make_queries(own, src_rows, rel_id, relation, after):
    return pl.pallas_call(
        query_kernel,
        grid_spec=pltpu.PrefetchScalarGridSpec(
            num_scalar_prefetch=1,
            grid=(GROUPS,),
            in_specs=[
                *[pl.BlockSpec((PART, D), lambda j, rel: (0, 0))] * PARTS,
                pl.BlockSpec((1, 1, PAD), lambda j, rel: (j, 0, 0)),
                pl.BlockSpec((1, D, D), lambda j, rel: (rel[j], 0, 0)),
                pl.BlockSpec(memory_space=pl.ANY),
            ],
            out_specs=[
                pl.BlockSpec((PAD, D), lambda j, rel: (j, 0)),
                pl.BlockSpec((D, PAD), lambda j, rel: (0, j)),
            ],
        ),
        out_shape=[
            jax.ShapeDtypeStruct((GROUPS * PAD, D), bf16),
            jax.ShapeDtypeStruct((D, GROUPS * PAD), bf16),
        ],
        compiler_params=params(),
        cost_estimate=cost(9),
        name="queries",
    )(rel_id, *own, src_rows, relation, after)


SUB = 32


def score_kernel(rel_ref, cnt_ref, *refs):
    nxt = refs[:PARTS]
    q_ref, s_hbm, dst_ref, wt_ref, gq_ref = refs[PARTS : PARTS + 5]
    dg = refs[PARTS + 5 : 2 * PARTS + 5]
    rg_ref, sc, nxt_t_ref, *halves, dacc, wcol, racc, s_ref, s_sem = refs[
        2 * PARTS + 5 :
    ]
    old = halves[0::2], halves[1::2]
    load_s = pltpu.make_async_copy(s_hbm, s_ref, s_sem)
    g = pl.program_id(0)
    rows = lax.broadcasted_iota(jnp.int32, (SUB, CH), 0)
    rows16 = lax.broadcasted_iota(jnp.int32, (BLK, CH), 0).astype(jnp.int16)

    @pl.when(g == 0)
    def _():
        load_s.start()
        dacc[...] = jnp.zeros_like(dacc)
        racc[...] = jnp.zeros_like(racc)
        for ref in old[1]:
            ref[...] = jnp.zeros_like(ref)
        for b in range(NBLK):
            nxt_t_ref[:, b * BLK : (b + 1) * BLK] = block_of(nxt, b).T

    def spread(b, w, qs, sl, gain, dst):
        at = slice(b * BLK, (b + 1) * BLK)
        mask = rows16 == (dst[0:1, :] - b * BLK).astype(jnp.int16)
        full = jnp.where(mask, gain[0:1, :].astype(bf16), w[at, :])
        dacc[at, :] += mm(full, qs[...], NT)
        return mm(nxt_t_ref[:, at], full)

    def finish(acc, sl, chunk):
        gq = (acc * sl[0:1, :]).astype(bf16)
        gq_ref[:, pl.ds(pl.multiple_of(chunk * CH, CH), CH)] = gq

    def stage(half, chunk_old):
        w, qs, sl, gain_ref, dst_keep = old[half]
        before = old[1 - half]
        here = slice(half * CH, (half + 1) * CH)
        chunk = 2 * g + half
        group = chunk // PER
        for b in range(NBLK):
            at = slice(b * BLK, (b + 1) * BLK)
            wcol[at, :] = wt_ref[group, :, at].T
        q = q_ref[:, here]
        dst = dst_ref[0, 0:1, here]
        acc = None
        top = jnp.full((8, CH), -jnp.inf, f32)
        hit = jnp.zeros((8, CH), f32)
        for b in range(NBLK):
            raw = mm(block_of(nxt, b), q)
            for i in range(BLK // SUB):
                at = slice(b * BLK + i * SUB, b * BLK + (i + 1) * SUB)
                mask = rows == dst - (b * BLK + i * SUB)
                val = raw[i * SUB : (i + 1) * SUB] * LOG2E + jnp.where(
                    mask, wcol[at, 1:2], wcol[at, 0:1]
                )
                sc[at, :] = val
                top = jnp.maximum(top, jnp.max(val.reshape(SUB // 8, 8, CH), axis=0))
                hit = hit + jnp.sum(jnp.where(mask, val, 0.0).reshape(SUB // 8, 8, CH), axis=0)
            part = spread(b, *before)
            acc = part if acc is None else acc + part
        finish(acc, before[2], chunk_old)
        top = jnp.max(top, axis=0, keepdims=True)
        hit = jnp.sum(hit, axis=0, keepdims=True)
        tot = jnp.zeros((8, CH), f32)
        for b in range(NBLK):
            for i in range(BLK // SUB):
                at = slice(b * BLK + i * SUB, b * BLK + (i + 1) * SUB)
                e = jnp.exp2(sc[at, :] - top)
                tot = tot + jnp.sum(e.reshape(SUB // 8, 8, CH), axis=0)
                w[at, :] = e.astype(bf16)
        tot = jnp.sum(tot, axis=0, keepdims=True)
        gain_ref[...] = jnp.broadcast_to(jnp.exp2(hit - top) - tot, (8, CH))
        dst_keep[...] = jnp.broadcast_to(dst, (8, CH))
        lane = lax.broadcasted_iota(jnp.int32, (1, CH), 1) + lax.rem(chunk, PER) * CH
        live = jnp.logical_and(lane < SLOTS, group * SLOTS + lane < cnt_ref[0])
        scale = jnp.where(live, 1.0 / tot, 0.0)
        sl[...] = jnp.broadcast_to(scale, (8, CH))
        qs[...] = (q.astype(f32) * scale).astype(bf16)

    stage(0, jnp.maximum(2 * g - 1, 0))
    stage(1, 2 * g)

    @pl.when(g == NCH // 2 - 1)
    def _():
        acc = None
        for b in range(NBLK):
            part = spread(b, *old[1])
            acc = part if acc is None else acc + part
        finish(acc, old[1][2], 2 * g + 1)
        load_s.wait()
        for k in range(GROUPS):
            at = slice(k * PAD, (k + 1) * PAD)
            racc[rel_ref[k]] += mm(gq_ref[:, at], s_ref[at, :])
        for k in range(racc.shape[0]):
            rg_ref[k] = racc[k].T.astype(bf16)
        for p in range(PARTS):
            dg[p][...] = dacc[p * PART : (p + 1) * PART, :].astype(bf16)


def score_side(nxt, q, s, dst_rows, weights, rel_id, counts, kinds):
    return pl.pallas_call(
        score_kernel,
        grid_spec=pltpu.PrefetchScalarGridSpec(
            num_scalar_prefetch=2,
            grid=(NCH // 2,),
            in_specs=[
                *[pl.BlockSpec((PART, D), lambda j, rel, cnt: (0, 0))] * PARTS,
                pl.BlockSpec((D, 2 * CH), lambda j, rel, cnt: (0, j)),
                pl.BlockSpec(memory_space=pl.ANY),
                pl.BlockSpec((1, 1, 2 * CH), lambda j, rel, cnt: (j, 0, 0)),
                pl.BlockSpec((GROUPS, 8, ROWS), lambda j, rel, cnt: (0, 0, 0)),
            ],
            out_specs=[
                pl.BlockSpec((D, GROUPS * PAD), lambda j, rel, cnt: (0, 0)),
                *[pl.BlockSpec((PART, D), lambda j, rel, cnt: (0, 0))] * PARTS,
                pl.BlockSpec((kinds, D, D), lambda j, rel, cnt: (0, 0, 0)),
            ],
            scratch_shapes=[
                pltpu.VMEM((ROWS, CH), f32),
                pltpu.VMEM((D, ROWS), bf16),
                *[pltpu.VMEM((ROWS, CH), bf16)] * 2,
                *[pltpu.VMEM((D, CH), bf16)] * 2,
                *[pltpu.VMEM((8, CH), f32)] * 4,
                *[pltpu.VMEM((8, CH), jnp.int32)] * 2,
                pltpu.VMEM((ROWS, D), f32),
                pltpu.VMEM((ROWS, 8), f32),
                pltpu.VMEM((kinds, D, D), f32),
                pltpu.VMEM((GROUPS * PAD, D), bf16),
                pltpu.SemaphoreType.DMA,
            ],
        ),
        out_shape=[
            jax.ShapeDtypeStruct((D, GROUPS * PAD), bf16),
            *[jax.ShapeDtypeStruct((PART, D), bf16)] * PARTS,
            jax.ShapeDtypeStruct((kinds, D, D), bf16),
        ],
        compiler_params=params(),
        cost_estimate=cost(28),
        name="scores",
    )(rel_id, counts, *nxt, q, s, dst_rows, weights)


def source_kernel(rel_ref, gq_ref, src_ref, mat_ref, *refs):
    out, acc = refs[:PARTS], refs[PARTS]
    g = pl.program_id(0)

    @pl.when(g == 0)
    def _():
        acc[...] = jnp.zeros_like(acc)

    grad = mm(mat_ref[0].astype(bf16), gq_ref[...]).astype(bf16)
    rows = lax.broadcasted_iota(jnp.int32, (BLK, PAD), 0).astype(jnp.int16)
    for b in range(NBLK):
        at = slice(b * BLK, (b + 1) * BLK)
        acc[at, :] += mm(one_hot(rows, src_ref[0], b * BLK), grad, NT)

    @pl.when(g == GROUPS - 1)
    def _():
        for p in range(PARTS):
            out[p][...] = acc[p * PART : (p + 1) * PART, :].astype(bf16)


def source_side(gq, src_rows, rel_id, relation):
    return pl.pallas_call(
        source_kernel,
        grid_spec=pltpu.PrefetchScalarGridSpec(
            num_scalar_prefetch=1,
            grid=(GROUPS,),
            in_specs=[
                pl.BlockSpec((D, PAD), lambda j, rel: (0, j)),
                pl.BlockSpec((1, 1, PAD), lambda j, rel: (j, 0, 0)),
                pl.BlockSpec((1, D, D), lambda j, rel: (rel[j], 0, 0)),
            ],
            out_specs=[pl.BlockSpec((PART, D), lambda j, rel: (0, 0))] * PARTS,
            scratch_shapes=[pltpu.VMEM((ROWS, D), f32)],
        ),
        out_shape=[jax.ShapeDtypeStruct((PART, D), bf16)] * PARTS,
        compiler_params=params(),
        cost_estimate=cost(8),
        name="source_grads",
    )(rel_id, gq, src_rows, relation)


def rowwise(param, accum, grad):
    fresh = accum + jnp.mean(grad * grad, -1)
    return (param - learn_rate * grad / jnp.sqrt(fresh)[..., None], fresh)


def shift_dom(block, by):
    size = lax.axis_size("dom")
    return lax.ppermute(block, "dom", [(i, (i + by) % size) for i in range(size)])


def swap_z(block):
    return lax.ppermute(block, "rep", [(i, i ^ 1) for i in range(8)])


def shift_x(block, by):
    return lax.ppermute(block, "rep", [(i, (i + 2 * by) % 8) for i in range(8)])


def spread_x(pair):
    return [pair] + [shift_x(pair, -k) for k in (1, 2, 3)]


def send_x(blocks):
    return [blocks[0]] + [shift_x(blocks[k], k) for k in (1, 2, 3)]


def add_up(blocks, after, dtype, copies=None):
    stacked = len(blocks) == 1
    shape = blocks[0].shape[1:] if stacked else blocks[0].shape
    whole = pl.BlockSpec(memory_space=pltpu.VMEM)

    def kernel(*refs):
        out = refs[-1]
        total = None
        if stacked:
            for i in range(blocks[0].shape[0]):
                part = refs[0][i].astype(f32)
                total = part if total is None else total + part
            total = total.astype(dtype)
        else:
            for ref in refs[: len(blocks)]:
                part = ref[...].astype(f32)
                total = part if total is None else total + part
            total = total.astype(dtype)
        if copies is None:
            out[...] = total
        else:
            for i in range(copies):
                out[i] = total

    return pl.pallas_call(
        kernel,
        in_specs=[whole] * len(blocks) + [pl.BlockSpec(memory_space=pl.ANY)],
        out_specs=whole,
        out_shape=jax.ShapeDtypeStruct(shape if copies is None else (copies,) + shape, dtype),
        compiler_params=pltpu.CompilerParams(vmem_limit_bytes=16 * MB),
        cost_estimate=cost(1),
        name="add_up",
    )(*blocks, after)


def split_sum(blocks):
    half = blocks[0].shape[0] // 2
    whole = pl.BlockSpec(memory_space=pltpu.VMEM)

    def kernel(*refs):
        for out, at in ((refs[-2], slice(0, half)), (refs[-1], slice(half, 2 * half))):
            total = None
            for ref in refs[:-2]:
                part = ref[at, :].astype(f32)
                total = part if total is None else total + part
            out[...] = total.astype(out.dtype)

    return pl.pallas_call(
        kernel,
        in_specs=[whole] * len(blocks),
        out_specs=[whole] * 2,
        out_shape=[jax.ShapeDtypeStruct((half, D), f32), jax.ShapeDtypeStruct((half, D), bf16)],
        compiler_params=pltpu.CompilerParams(vmem_limit_bytes=16 * MB),
        cost_estimate=cost(1),
        name="split_sum",
    )(*blocks)


def turned(index):
    rep = lax.axis_index("rep")
    return ((index - PART * (rep // 2)) % ROWS) ^ (256 * (rep % 2))


def operator_update(total, relation, accum):
    rows, width = total.shape
    mine = lax.dynamic_slice(accum.reshape(-1), (lax.axis_index("dom") * rows,), (rows,))
    fresh = mine + jnp.mean(total * total, -1)
    step = total / jnp.sqrt(fresh)[:, None]
    power = jnp.floor(jnp.log2(fresh))
    part = fresh * jnp.exp2(-power)
    high = lax.reduce_precision(part, 5, 10)
    code = jnp.pad(jnp.stack([power, high, part - high]), ((0, 5), (0, width - rows)))
    send = jnp.concatenate([step, code]).astype(jnp.float16)
    cores = [[2 * i + c for i in range(16)] for c in range(2)]
    shares = jnp.broadcast_to(send, (16,) + send.shape)
    half = lax.all_to_all(shares, "dom", 0, 0, axis_index_groups=cores)
    other = lax.ppermute(half, "dom", [(i, i ^ 1) for i in range(32)])
    second = lax.axis_index("dom") % 2 == 1
    pairs = [jnp.where(second, other, half), jnp.where(second, half, other)]
    full = jnp.stack(pairs, 1).reshape(32, rows + 8, width).astype(f32)
    steps = full[:, :rows].reshape(relation.shape)
    power, high, low = (full[:, rows + i, :rows].reshape(accum.shape) for i in range(3))
    return relation - learn_rate * steps, (high + low) * jnp.exp2(power)


def pad_slots(index, fill):
    return jnp.pad(index.reshape(GROUPS, SLOTS), ((0, 0), (0, PAD - SLOTS)), constant_values=fill)


def source_stage(own, src_pad, rel_id, relation, after):
    return make_queries(own, src_pad.reshape(GROUPS, 1, PAD), rel_id, relation, after)


def target_stage(nxt, q, s, dst_pad, weights, rel_id, counts, kinds):
    rows = dst_pad.reshape(NCH // 2, 1, 2 * CH)
    out = score_side(nxt, q, s, rows, weights, rel_id, counts, kinds)
    return out[0], out[1 : PARTS + 1], out[PARTS + 1]


def back_stage(gq, src_pad, rel_id, relation):
    return source_side(gq, src_pad.reshape(GROUPS, 1, PAD), rel_id, relation)


def local_grads(own, nxt, relation, src_index, dst_index, neg_index, rel_id, counts):
    own, nxt = own.astype(bf16), nxt.astype(bf16)
    src_pad = pad_slots(src_index, -1)
    weights = neg_weights(pad_slots(neg_index, -1))
    own = [own[k * PART : (k + 1) * PART] for k in range(PARTS)]
    nxt = [nxt[k * PART : (k + 1) * PART] for k in range(PARTS)]
    s, q = source_stage(own, src_pad, rel_id, relation, nxt[0])
    gq, dst_grad, rel_grad = target_stage(
        nxt, q, s, pad_slots(dst_index, -1), weights, rel_id, counts, relation.shape[0]
    )
    src_grad = back_stage(gq, src_pad, rel_id, relation)
    return jnp.concatenate(src_grad), jnp.concatenate(dst_grad), rel_grad


def on_device(
    entity, entity_accum, relation, relation_accum, src_index, dst_index, neg_index, rel_id, counts
):
    ent_b = entity.astype(bf16)
    src_pad = pad_slots(turned(src_index), -1)
    dst_pad = pad_slots(turned(dst_index), -1)
    neg_pad = pad_slots(turned(neg_index), -1)
    other = swap_z(ent_b)
    own = spread_x(jnp.concatenate([ent_b, other]))
    nxt = [shift_dom(block, -1) for block in own]
    weights = neg_weights(neg_pad)
    s, q = source_stage(own, src_pad, rel_id, relation, nxt[0])
    gq, dst_grad, rel_grad = target_stage(
        nxt, q, s, dst_pad, weights, rel_id, counts, relation.shape[0]
    )
    dst_blocks = send_x(dst_grad)
    got = lax.all_to_all(rel_grad.reshape(32, -1, D), "dom", 0, 0)
    src_grad = back_stage(gq, src_pad, rel_id, relation)
    src_blocks = send_x(src_grad)
    mine = add_up([got], src_grad[0], f32)
    zsum = mine + swap_z(mine)
    dst_sum = add_up(dst_blocks, zsum, bf16)
    moved = shift_dom(dst_sum, 1)
    keep, give = split_sum(src_blocks + [moved])
    rel_total = add_up([zsum] + [shift_x(zsum, k) for k in (1, 2, 3)], give, f32)
    relation_new, relation_accum_new = operator_update(rel_total, relation, relation_accum)
    grads = keep + swap_z(give).astype(f32)
    entity_new, entity_accum_new = rowwise(entity, entity_accum, grads)
    return (entity_new, entity_accum_new, relation_new, relation_accum_new)


def solution(mesh):
    placed = (
        P(("dom", "rep"), None),
        P(("dom", "rep")),
        P(),
        P(),
        P(("dom", "rep")),
        P(("dom", "rep")),
        P(("dom", "rep"), None),
        P(("dom", "rep")),
        P(("dom", "rep")),
    )
    return jax.shard_map(
        on_device,
        mesh=mesh,
        in_specs=placed,
        out_specs=(P(("dom", "rep"), None), P(("dom", "rep")), P(), P()),
        check_vma=False,
    )
```

```python
import functools
import jax
import jax.numpy as jnp
from jax import lax
from jax.experimental import pallas as pl
from jax.experimental.pallas import tpu as pltpu
from jax.sharding import PartitionSpec as P

learn_rate = 0.1
LOG2E = 1.4426950408889634
GROUPS = 4
SLOTS = 1000
PAD = 1024
ROWS = 2048
D = 256
BLK = 256
NBLK = ROWS // BLK
CH = 512
NCH = GROUPS * PAD // CH
PER = PAD // CH
bf16 = jnp.bfloat16
f32 = jnp.float32

NN = (((1,), (0,)), ((), ()))
NT = (((1,), (1,)), ((), ()))
MB = 1024 * 1024


def mm(a, b, dims=NN):
    return lax.dot_general(a, b, dims, preferred_element_type=f32)


def cost(us):
    return pl.CostEstimate(flops=int(us * 5e8), bytes_accessed=int(us * 3.5e6), transcendentals=0)


def params(size):
    return pltpu.CompilerParams(
        dimension_semantics=("arbitrary",), vmem_limit_bytes=size * MB
    )


def one_hot(rows, index, first):
    return jnp.where(rows == (index - first).astype(jnp.int16), bf16(1), bf16(0))


PARTS = 4
PART = ROWS // PARTS


def part_specs():
    spots = (0, 0, 1, 2)
    return [pl.BlockSpec((PART, D), functools.partial(lambda k, *_: (k, 0), k)) for k in spots]


def block_of(parts, b):
    first = b * BLK % PART
    return parts[b * BLK // PART][first : first + BLK, :]


def count_kernel(neg_ref, out_ref):
    rows = lax.broadcasted_iota(jnp.int32, (BLK, 128), 0).astype(jnp.int16)
    for b in range(NBLK):
        hits = None
        for c in range(0, PAD, 128):
            hot = one_hot(rows, neg_ref[0, :, c : c + 128], b * BLK)
            hits = hot if hits is None else hits + hot
        count = jnp.sum(hits.astype(f32), axis=1, keepdims=True)
        lane = lax.broadcasted_iota(jnp.int32, (BLK, 8), 1)
        out_ref[0, :, b * BLK : (b + 1) * BLK] = jnp.where(lane == 0, count, count + 1.0).T
    out_ref[0] = jnp.log2(out_ref[0])


def neg_weights(neg_pad):
    return pl.pallas_call(
        count_kernel,
        grid=(GROUPS,),
        in_specs=[pl.BlockSpec((1, 1, PAD), lambda g: (g, 0, 0))],
        out_specs=pl.BlockSpec((1, 8, ROWS), lambda g: (g, 0, 0)),
        out_shape=jax.ShapeDtypeStruct((GROUPS, 8, ROWS), f32),
        compiler_params=params(8),
        cost_estimate=cost(3),
        name="neg_weights",
    )(neg_pad.reshape(GROUPS, 1, PAD))


def query_kernel(rel_ref, *refs):
    own = refs[:PARTS]
    idx_ref, mat_ref, s_ref, q_ref = refs[PARTS:]
    column = jnp.broadcast_to(idx_ref[0].astype(f32), (128, PAD)).T
    column = column.astype(jnp.int32).astype(jnp.int16)
    cols = lax.broadcasted_iota(jnp.int32, (PAD, 128), 1).astype(jnp.int16)
    acc = None
    for b in range(NBLK):
        hot = jnp.concatenate(
            [
                jnp.where(cols + jnp.int16(first) == column, bf16(1), bf16(0))
                for first in (b * BLK, b * BLK + 128)
            ],
            axis=1,
        )
        part = mm(hot, block_of(own, b))
        acc = part if acc is None else acc + part
    rows = acc.astype(bf16)
    s_ref[...] = rows
    q_ref[...] = mm(mat_ref[0].astype(bf16).T, rows, NT).astype(bf16)


def make_queries(own, src_rows, rel_id, relation):
    return pl.pallas_call(
        query_kernel,
        grid_spec=pltpu.PrefetchScalarGridSpec(
            num_scalar_prefetch=1,
            grid=(GROUPS,),
            in_specs=[
                *part_specs(),
                pl.BlockSpec((1, 1, PAD), lambda j, rel: (j, 0, 0)),
                pl.BlockSpec((1, D, D), lambda j, rel: (rel[j], 0, 0)),
            ],
            out_specs=[
                pl.BlockSpec((PAD, D), lambda j, rel: (j, 0)),
                pl.BlockSpec((D, PAD), lambda j, rel: (0, j)),
            ],
        ),
        out_shape=[
            jax.ShapeDtypeStruct((GROUPS * PAD, D), bf16),
            jax.ShapeDtypeStruct((D, GROUPS * PAD), bf16),
        ],
        compiler_params=params(20),
        cost_estimate=cost(9),
        name="queries",
    )(rel_id, own[0], *[own[1]] * 3, src_rows, relation)


SUB = 32


def score_kernel(rel_ref, cnt_ref, *refs):
    nxt = refs[:PARTS]
    q_ref, s_ref, dst_ref, wt_ref, gq_ref = refs[PARTS : PARTS + 5]
    dg = refs[PARTS + 5 : 2 * PARTS + 5]
    rg_ref, sc, nxt_t_ref, *halves, dacc, wcol, racc = refs[
        2 * PARTS + 5 :
    ]
    old = halves[0::2], halves[1::2]
    g = pl.program_id(0)
    rows = lax.broadcasted_iota(jnp.int32, (SUB, CH), 0)
    rows16 = lax.broadcasted_iota(jnp.int32, (BLK, CH), 0).astype(jnp.int16)

    @pl.when(g == 0)
    def _():
        dacc[...] = jnp.zeros_like(dacc)
        racc[...] = jnp.zeros_like(racc)
        for ref in old[1]:
            ref[...] = jnp.zeros_like(ref)
        for b in range(NBLK):
            nxt_t_ref[:, b * BLK : (b + 1) * BLK] = block_of(nxt, b).T

    def spread(b, w, qs, sl, gain, dst):
        at = slice(b * BLK, (b + 1) * BLK)
        mask = rows16 == (dst[0:1, :] - b * BLK).astype(jnp.int16)
        full = jnp.where(mask, gain[0:1, :].astype(bf16), w[at, :])
        dacc[at, :] += mm(full, qs[...], NT)
        return mm(nxt_t_ref[:, at], full)

    def finish(acc, sl, chunk):
        gq = (acc * sl[0:1, :]).astype(bf16)
        gq_ref[:, pl.ds(pl.multiple_of(chunk * CH, CH), CH)] = gq

    def stage(half, chunk_old):
        w, qs, sl, gain_ref, dst_keep = old[half]
        before = old[1 - half]
        here = slice(half * CH, (half + 1) * CH)
        chunk = 2 * g + half
        group = chunk // PER
        for b in range(NBLK):
            at = slice(b * BLK, (b + 1) * BLK)
            wcol[at, :] = wt_ref[group, :, at].T
        q = q_ref[:, here]
        dst = dst_ref[0, 0:1, here]
        acc = None
        top = jnp.full((8, CH), -jnp.inf, f32)
        hit = jnp.zeros((8, CH), f32)
        for b in range(NBLK):
            raw = mm(block_of(nxt, b), q)
            for i in range(BLK // SUB):
                at = slice(b * BLK + i * SUB, b * BLK + (i + 1) * SUB)
                mask = rows == dst - (b * BLK + i * SUB)
                val = raw[i * SUB : (i + 1) * SUB] * LOG2E + jnp.where(
                    mask, wcol[at, 1:2], wcol[at, 0:1]
                )
                sc[at, :] = val
                top = jnp.maximum(top, jnp.max(val.reshape(SUB // 8, 8, CH), axis=0))
                hit = hit + jnp.sum(jnp.where(mask, val, 0.0).reshape(SUB // 8, 8, CH), axis=0)
            part = spread(b, *before)
            acc = part if acc is None else acc + part
        finish(acc, before[2], chunk_old)
        top = jnp.max(top, axis=0, keepdims=True)
        hit = jnp.sum(hit, axis=0, keepdims=True)
        tot = jnp.zeros((8, CH), f32)
        for b in range(NBLK):
            for i in range(BLK // SUB):
                at = slice(b * BLK + i * SUB, b * BLK + (i + 1) * SUB)
                e = jnp.exp2(sc[at, :] - top)
                tot = tot + jnp.sum(e.reshape(SUB // 8, 8, CH), axis=0)
                w[at, :] = e.astype(bf16)
        tot = jnp.sum(tot, axis=0, keepdims=True)
        gain_ref[...] = jnp.broadcast_to(jnp.exp2(hit - top) - tot, (8, CH))
        dst_keep[...] = jnp.broadcast_to(dst, (8, CH))
        lane = lax.broadcasted_iota(jnp.int32, (1, CH), 1) + lax.rem(chunk, PER) * CH
        live = jnp.logical_and(lane < SLOTS, group * SLOTS + lane < cnt_ref[0])
        scale = jnp.where(live, 1.0 / tot, 0.0)
        sl[...] = jnp.broadcast_to(scale, (8, CH))
        qs[...] = (q.astype(f32) * scale).astype(bf16)

    stage(0, jnp.maximum(2 * g - 1, 0))
    stage(1, 2 * g)

    @pl.when(g == NCH // 2 - 1)
    def _():
        acc = None
        for b in range(NBLK):
            part = spread(b, *old[1])
            acc = part if acc is None else acc + part
        finish(acc, old[1][2], 2 * g + 1)
        for k in range(GROUPS):
            at = slice(k * PAD, (k + 1) * PAD)
            racc[rel_ref[k]] += mm(gq_ref[:, at], s_ref[at, :])
        for k in range(racc.shape[0]):
            rg_ref[k] = racc[k].T.astype(bf16)
        for p in range(PARTS):
            dg[p][...] = dacc[p * PART : (p + 1) * PART, :].astype(bf16)


def score_side(nxt, q, s, dst_rows, weights, rel_id, counts, kinds):
    return pl.pallas_call(
        score_kernel,
        grid_spec=pltpu.PrefetchScalarGridSpec(
            num_scalar_prefetch=2,
            grid=(NCH // 2,),
            in_specs=[
                *part_specs(),
                pl.BlockSpec((D, 2 * CH), lambda j, rel, cnt: (0, j)),
                pl.BlockSpec((GROUPS * PAD, D), lambda j, rel, cnt: (0, 0)),
                pl.BlockSpec((1, 1, 2 * CH), lambda j, rel, cnt: (j, 0, 0)),
                pl.BlockSpec((GROUPS, 8, ROWS), lambda j, rel, cnt: (0, 0, 0)),
            ],
            out_specs=[
                pl.BlockSpec((D, GROUPS * PAD), lambda j, rel, cnt: (0, 0)),
                *[pl.BlockSpec((PART, D), lambda j, rel, cnt: (0, 0))] * PARTS,
                pl.BlockSpec((kinds, D, D), lambda j, rel, cnt: (0, 0, 0)),
            ],
            scratch_shapes=[
                pltpu.VMEM((ROWS, CH), f32),
                pltpu.VMEM((D, ROWS), bf16),
                *[pltpu.VMEM((ROWS, CH), bf16)] * 2,
                *[pltpu.VMEM((D, CH), bf16)] * 2,
                *[pltpu.VMEM((8, CH), f32)] * 4,
                *[pltpu.VMEM((8, CH), jnp.int32)] * 2,
                pltpu.VMEM((ROWS, D), f32),
                pltpu.VMEM((ROWS, 8), f32),
                pltpu.VMEM((kinds, D, D), f32),
            ],
        ),
        out_shape=[
            jax.ShapeDtypeStruct((D, GROUPS * PAD), bf16),
            *[jax.ShapeDtypeStruct((PART, D), bf16)] * PARTS,
            jax.ShapeDtypeStruct((kinds, D, D), bf16),
        ],
        compiler_params=params(34),
        cost_estimate=cost(28),
        name="scores",
    )(rel_id, counts, nxt[0], *[nxt[1]] * 3, q, s, dst_rows, weights)


def source_kernel(rel_ref, gq_ref, src_ref, mat_ref, *refs):
    out, acc = refs[:PARTS], refs[PARTS]
    g = pl.program_id(0)

    @pl.when(g == 0)
    def _():
        acc[...] = jnp.zeros_like(acc)

    grad = mm(mat_ref[0].astype(bf16), gq_ref[...]).astype(bf16)
    rows = lax.broadcasted_iota(jnp.int32, (BLK, PAD), 0).astype(jnp.int16)
    for b in range(NBLK):
        at = slice(b * BLK, (b + 1) * BLK)
        acc[at, :] += mm(one_hot(rows, src_ref[0], b * BLK), grad, NT)

    @pl.when(g == GROUPS - 1)
    def _():
        for p in range(PARTS):
            out[p][...] = acc[p * PART : (p + 1) * PART, :].astype(bf16)


def source_side(gq, src_rows, rel_id, relation):
    return pl.pallas_call(
        source_kernel,
        grid_spec=pltpu.PrefetchScalarGridSpec(
            num_scalar_prefetch=1,
            grid=(GROUPS,),
            in_specs=[
                pl.BlockSpec((D, PAD), lambda j, rel: (0, j)),
                pl.BlockSpec((1, 1, PAD), lambda j, rel: (j, 0, 0)),
                pl.BlockSpec((1, D, D), lambda j, rel: (rel[j], 0, 0)),
            ],
            out_specs=[pl.BlockSpec((PART, D), lambda j, rel: (0, 0))] * PARTS,
            scratch_shapes=[pltpu.VMEM((ROWS, D), f32)],
        ),
        out_shape=[jax.ShapeDtypeStruct((PART, D), bf16)] * PARTS,
        compiler_params=params(16),
        cost_estimate=cost(8),
        name="source_grads",
    )(rel_id, gq, src_rows, relation)


def rowwise(param, accum, grad):
    fresh = accum + jnp.mean(grad * grad, -1)
    return (param - learn_rate * grad / jnp.sqrt(fresh)[..., None], fresh)


def shift_dom(block, by):
    size = lax.axis_size("dom")
    return lax.ppermute(block, "dom", [(i, (i + by) % size) for i in range(size)])


def swap_z(block):
    return lax.ppermute(block, "rep", [(i, i ^ 1) for i in range(8)])


def shift_x(block, by):
    return lax.ppermute(block, "rep", [(i, (i + 2 * by) % 8) for i in range(8)])


def spread_x(pair):
    return [pair] + [shift_x(pair, -k) for k in (1, 2, 3)]


def send_x(blocks):
    return [blocks[0]] + [shift_x(blocks[k], k) for k in (1, 2, 3)]


def add_up(blocks, after, dtype, copies=None):
    stacked = len(blocks) == 1
    shape = blocks[0].shape[1:] if stacked else blocks[0].shape
    whole = pl.BlockSpec(memory_space=pltpu.VMEM)

    def kernel(*refs):
        out = refs[-1]
        total = None
        if stacked:
            for i in range(blocks[0].shape[0]):
                part = refs[0][i].astype(f32)
                total = part if total is None else total + part
            total = total.astype(dtype)
        else:
            for ref in refs[: len(blocks)]:
                part = ref[...].astype(f32)
                total = part if total is None else total + part
            total = total.astype(dtype)
        if copies is None:
            out[...] = total
        else:
            for i in range(copies):
                out[i] = total

    return pl.pallas_call(
        kernel,
        in_specs=[whole] * len(blocks) + [pl.BlockSpec(memory_space=pl.ANY)],
        out_specs=whole,
        out_shape=jax.ShapeDtypeStruct(shape if copies is None else (copies,) + shape, dtype),
        compiler_params=pltpu.CompilerParams(vmem_limit_bytes=16 * MB),
        cost_estimate=cost(1),
        name="add_up",
    )(*blocks, after)


def split_sum(blocks):
    half = blocks[0].shape[0] // 2
    whole = pl.BlockSpec(memory_space=pltpu.VMEM)

    def kernel(*refs):
        for out, at in ((refs[-2], slice(0, half)), (refs[-1], slice(half, 2 * half))):
            total = None
            for ref in refs[:-2]:
                part = ref[at, :].astype(f32)
                total = part if total is None else total + part
            out[...] = total.astype(out.dtype)

    return pl.pallas_call(
        kernel,
        in_specs=[whole] * len(blocks),
        out_specs=[whole] * 2,
        out_shape=[jax.ShapeDtypeStruct((half, D), f32), jax.ShapeDtypeStruct((half, D), bf16)],
        compiler_params=pltpu.CompilerParams(vmem_limit_bytes=16 * MB),
        cost_estimate=cost(1),
        name="split_sum",
    )(*blocks)


def turned(index):
    rep = lax.axis_index("rep")
    return ((index - PART * (rep // 2)) % ROWS) ^ (256 * (rep % 2))


def operator_update(total, relation, accum):
    rows, width = total.shape
    mine = lax.dynamic_slice(accum.reshape(-1), (lax.axis_index("dom") * rows,), (rows,))
    fresh = mine + jnp.mean(total * total, -1)
    step = total / jnp.sqrt(fresh)[:, None]
    power = jnp.floor(jnp.log2(fresh))
    part = fresh * jnp.exp2(-power)
    high = lax.reduce_precision(part, 5, 10)
    code = jnp.pad(jnp.stack([power, high, part - high]), ((0, 5), (0, width - rows)))
    send = jnp.concatenate([step, code]).astype(jnp.float16)
    cores = [[2 * i + c for i in range(16)] for c in range(2)]
    shares = jnp.broadcast_to(send, (16,) + send.shape)
    half = lax.all_to_all(shares, "dom", 0, 0, axis_index_groups=cores)
    other = lax.ppermute(half, "dom", [(i, i ^ 1) for i in range(32)])
    second = lax.axis_index("dom") % 2 == 1
    pairs = [jnp.where(second, other, half), jnp.where(second, half, other)]
    full = jnp.stack(pairs, 1).reshape(32, rows + 8, width).astype(f32)
    steps = full[:, :rows].reshape(relation.shape)
    power, high, low = (full[:, rows + i, :rows].reshape(accum.shape) for i in range(3))
    return relation - learn_rate * steps, (high + low) * jnp.exp2(power)


def pad_slots(index, fill):
    return jnp.pad(index.reshape(GROUPS, SLOTS), ((0, 0), (0, PAD - SLOTS)), constant_values=fill)


def source_stage(own, src_pad, rel_id, relation):
    return make_queries(own, src_pad.reshape(GROUPS, 1, PAD), rel_id, relation)


def target_stage(nxt, q, s, dst_pad, weights, rel_id, counts, kinds):
    rows = dst_pad.reshape(NCH // 2, 1, 2 * CH)
    out = score_side(nxt, q, s, rows, weights, rel_id, counts, kinds)
    return out[0], out[1 : PARTS + 1], out[PARTS + 1]


def back_stage(gq, src_pad, rel_id, relation):
    return source_side(gq, src_pad.reshape(GROUPS, 1, PAD), rel_id, relation)


def local_grads(own, nxt, relation, src_index, dst_index, neg_index, rel_id, counts):
    own, nxt = own.astype(bf16), nxt.astype(bf16)
    src_pad = pad_slots(src_index, -1)
    weights = neg_weights(pad_slots(neg_index, -1))
    own, nxt = ([rows[:PART], rows[PART:]] for rows in (own, nxt))
    s, q = source_stage(own, src_pad, rel_id, relation)
    gq, dst_grad, rel_grad = target_stage(
        nxt, q, s, pad_slots(dst_index, -1), weights, rel_id, counts, relation.shape[0]
    )
    src_grad = back_stage(gq, src_pad, rel_id, relation)
    return jnp.concatenate(src_grad), jnp.concatenate(dst_grad), rel_grad


def on_device(
    entity, entity_accum, relation, relation_accum, src_index, dst_index, neg_index, rel_id, counts
):
    ent_b = entity.astype(bf16)
    src_pad = pad_slots(turned(src_index), -1)
    dst_pad = pad_slots(turned(dst_index), -1)
    neg_pad = pad_slots(turned(neg_index), -1)
    other = swap_z(ent_b)
    pair = jnp.concatenate([ent_b, other])
    own = [pair, jnp.concatenate(spread_x(pair)[1:])]
    nxt = [shift_dom(block, -1) for block in own]
    weights = neg_weights(neg_pad)
    s, q = source_stage(own, src_pad, rel_id, relation)
    gq, dst_grad, rel_grad = target_stage(
        nxt, q, s, dst_pad, weights, rel_id, counts, relation.shape[0]
    )
    dst_blocks = send_x(dst_grad)
    got = lax.all_to_all(rel_grad.reshape(32, -1, D), "dom", 0, 0)
    src_grad = back_stage(gq, src_pad, rel_id, relation)
    src_blocks = send_x(src_grad)
    mine = add_up([got], src_grad[0], f32)
    zsum = mine + swap_z(mine)
    dst_sum = add_up(dst_blocks, zsum, bf16)
    moved = shift_dom(dst_sum, 1)
    keep, give = split_sum(src_blocks + [moved])
    rel_total = add_up([zsum] + [shift_x(zsum, k) for k in (1, 2, 3)], give, f32)
    relation_new, relation_accum_new = operator_update(rel_total, relation, relation_accum)
    grads = keep + swap_z(give).astype(f32)
    entity_new, entity_accum_new = rowwise(entity, entity_accum, grads)
    return (entity_new, entity_accum_new, relation_new, relation_accum_new)


def solution(mesh):
    placed = (
        P(("dom", "rep"), None),
        P(("dom", "rep")),
        P(),
        P(),
        P(("dom", "rep")),
        P(("dom", "rep")),
        P(("dom", "rep"), None),
        P(("dom", "rep")),
        P(("dom", "rep")),
    )
    return jax.shard_map(
        on_device,
        mesh=mesh,
        in_specs=placed,
        out_specs=(P(("dom", "rep"), None), P(("dom", "rep")), P(), P()),
        check_vma=False,
    )
```

```python
import functools
import jax
import jax.numpy as jnp
from jax import lax
from jax.experimental import pallas as pl
from jax.experimental.pallas import tpu as pltpu
from jax.sharding import PartitionSpec as P

learn_rate = 0.1
LOG2E = 1.4426950408889634
GROUPS = 4
SLOTS = 1000
PAD = 1024
ROWS = 2048
D = 256
BLK = 256
NBLK = ROWS // BLK
CH = 512
NCH = GROUPS * PAD // CH
PER = PAD // CH
bf16 = jnp.bfloat16
f32 = jnp.float32

NN = (((1,), (0,)), ((), ()))
NT = (((1,), (1,)), ((), ()))
MB = 1024 * 1024


def mm(a, b, dims=NN):
    return lax.dot_general(a, b, dims, preferred_element_type=f32)


def cost(us):
    return pl.CostEstimate(flops=int(us * 5e8), bytes_accessed=int(us * 3.5e6), transcendentals=0)


def params(size):
    return pltpu.CompilerParams(
        dimension_semantics=("arbitrary",), vmem_limit_bytes=size * MB
    )


def one_hot(rows, index, first):
    return jnp.where(rows == (index - first).astype(jnp.int16), bf16(1), bf16(0))


PARTS = 4
PART = ROWS // PARTS


def part_specs():
    return [pl.BlockSpec((PART, D), lambda *_: (0, 0))] * PARTS


def block_of(parts, b):
    first = b * BLK % PART
    return parts[b * BLK // PART][first : first + BLK, :]


def count_kernel(neg_ref, out_ref):
    rows = lax.broadcasted_iota(jnp.int32, (BLK, 128), 0).astype(jnp.int16)
    for b in range(NBLK):
        hits = None
        for c in range(0, PAD, 128):
            hot = one_hot(rows, neg_ref[0, :, c : c + 128], b * BLK)
            hits = hot if hits is None else hits + hot
        count = jnp.sum(hits.astype(f32), axis=1, keepdims=True)
        lane = lax.broadcasted_iota(jnp.int32, (BLK, 8), 1)
        out_ref[0, :, b * BLK : (b + 1) * BLK] = jnp.where(lane == 0, count, count + 1.0).T
    out_ref[0] = jnp.log2(out_ref[0])


def neg_weights(neg_pad):
    return pl.pallas_call(
        count_kernel,
        grid=(GROUPS,),
        in_specs=[pl.BlockSpec((1, 1, PAD), lambda g: (g, 0, 0))],
        out_specs=pl.BlockSpec((1, 8, ROWS), lambda g: (g, 0, 0)),
        out_shape=jax.ShapeDtypeStruct((GROUPS, 8, ROWS), f32),
        compiler_params=params(8),
        cost_estimate=cost(3),
        name="neg_weights",
    )(neg_pad.reshape(GROUPS, 1, PAD))


def query_kernel(rel_ref, *refs):
    own = refs[:PARTS]
    idx_ref, mat_ref, s_ref, q_ref = refs[PARTS:]
    column = jnp.broadcast_to(idx_ref[0].astype(f32), (128, PAD)).T
    column = column.astype(jnp.int32).astype(jnp.int16)
    cols = lax.broadcasted_iota(jnp.int32, (PAD, 128), 1).astype(jnp.int16)
    acc = None
    for b in range(NBLK):
        hot = jnp.concatenate(
            [
                jnp.where(cols + jnp.int16(first) == column, bf16(1), bf16(0))
                for first in (b * BLK, b * BLK + 128)
            ],
            axis=1,
        )
        part = mm(hot, block_of(own, b))
        acc = part if acc is None else acc + part
    rows = acc.astype(bf16)
    s_ref[...] = rows
    q_ref[...] = mm(mat_ref[0].astype(bf16).T, rows, NT).astype(bf16)


def make_queries(own, src_rows, rel_id, relation):
    return pl.pallas_call(
        query_kernel,
        grid_spec=pltpu.PrefetchScalarGridSpec(
            num_scalar_prefetch=1,
            grid=(GROUPS,),
            in_specs=[
                *part_specs(),
                pl.BlockSpec((1, 1, PAD), lambda j, rel: (j, 0, 0)),
                pl.BlockSpec((1, D, D), lambda j, rel: (rel[j], 0, 0)),
            ],
            out_specs=[
                pl.BlockSpec((PAD, D), lambda j, rel: (j, 0)),
                pl.BlockSpec((D, PAD), lambda j, rel: (0, j)),
            ],
        ),
        out_shape=[
            jax.ShapeDtypeStruct((GROUPS * PAD, D), bf16),
            jax.ShapeDtypeStruct((D, GROUPS * PAD), bf16),
        ],
        compiler_params=params(20),
        cost_estimate=cost(9),
        name="queries",
    )(rel_id, *own, src_rows, relation)


SUB = 32


def score_kernel(rel_ref, cnt_ref, *refs):
    nxt = refs[:PARTS]
    q_ref, s_ref, dst_ref, wt_ref, gq_ref = refs[PARTS : PARTS + 5]
    dg = refs[PARTS + 5 : 2 * PARTS + 5]
    rg_ref, sc, nxt_t_ref, *halves, dacc, wcol, racc = refs[
        2 * PARTS + 5 :
    ]
    old = halves[0::2], halves[1::2]
    g = pl.program_id(0)
    rows = lax.broadcasted_iota(jnp.int32, (SUB, CH), 0)
    rows16 = lax.broadcasted_iota(jnp.int32, (BLK, CH), 0).astype(jnp.int16)

    @pl.when(g == 0)
    def _():
        dacc[...] = jnp.zeros_like(dacc)
        racc[...] = jnp.zeros_like(racc)
        for ref in old[1]:
            ref[...] = jnp.zeros_like(ref)
        for b in range(NBLK):
            nxt_t_ref[:, b * BLK : (b + 1) * BLK] = block_of(nxt, b).T

    def spread(b, w, qs, sl, gain, dst):
        at = slice(b * BLK, (b + 1) * BLK)
        mask = rows16 == (dst[0:1, :] - b * BLK).astype(jnp.int16)
        full = jnp.where(mask, gain[0:1, :].astype(bf16), w[at, :])
        dacc[at, :] += mm(full, qs[...], NT)
        return mm(nxt_t_ref[:, at], full)

    def finish(acc, sl, chunk):
        gq = (acc * sl[0:1, :]).astype(bf16)
        gq_ref[:, pl.ds(pl.multiple_of(chunk * CH, CH), CH)] = gq

    def stage(half, chunk_old):
        w, qs, sl, gain_ref, dst_keep = old[half]
        before = old[1 - half]
        here = slice(half * CH, (half + 1) * CH)
        chunk = 2 * g + half
        group = chunk // PER
        for b in range(NBLK):
            at = slice(b * BLK, (b + 1) * BLK)
            wcol[at, :] = wt_ref[group, :, at].T
        q = q_ref[:, here]
        dst = dst_ref[0, 0:1, here]
        acc = None
        top = jnp.full((8, CH), -jnp.inf, f32)
        hit = jnp.zeros((8, CH), f32)
        for b in range(NBLK):
            raw = mm(block_of(nxt, b), q)
            for i in range(BLK // SUB):
                at = slice(b * BLK + i * SUB, b * BLK + (i + 1) * SUB)
                mask = rows == dst - (b * BLK + i * SUB)
                val = raw[i * SUB : (i + 1) * SUB] * LOG2E + jnp.where(
                    mask, wcol[at, 1:2], wcol[at, 0:1]
                )
                sc[at, :] = val
                top = jnp.maximum(top, jnp.max(val.reshape(SUB // 8, 8, CH), axis=0))
                hit = hit + jnp.sum(jnp.where(mask, val, 0.0).reshape(SUB // 8, 8, CH), axis=0)
            part = spread(b, *before)
            acc = part if acc is None else acc + part
        finish(acc, before[2], chunk_old)
        top = jnp.max(top, axis=0, keepdims=True)
        hit = jnp.sum(hit, axis=0, keepdims=True)
        tot = jnp.zeros((8, CH), f32)
        for b in range(NBLK):
            for i in range(BLK // SUB):
                at = slice(b * BLK + i * SUB, b * BLK + (i + 1) * SUB)
                e = jnp.exp2(sc[at, :] - top)
                tot = tot + jnp.sum(e.reshape(SUB // 8, 8, CH), axis=0)
                w[at, :] = e.astype(bf16)
        tot = jnp.sum(tot, axis=0, keepdims=True)
        gain_ref[...] = jnp.broadcast_to(jnp.exp2(hit - top) - tot, (8, CH))
        dst_keep[...] = jnp.broadcast_to(dst, (8, CH))
        lane = lax.broadcasted_iota(jnp.int32, (1, CH), 1) + lax.rem(chunk, PER) * CH
        live = jnp.logical_and(lane < SLOTS, group * SLOTS + lane < cnt_ref[0])
        scale = jnp.where(live, 1.0 / tot, 0.0)
        sl[...] = jnp.broadcast_to(scale, (8, CH))
        qs[...] = (q.astype(f32) * scale).astype(bf16)

    stage(0, jnp.maximum(2 * g - 1, 0))
    stage(1, 2 * g)

    @pl.when(g == NCH // 2 - 1)
    def _():
        acc = None
        for b in range(NBLK):
            part = spread(b, *old[1])
            acc = part if acc is None else acc + part
        finish(acc, old[1][2], 2 * g + 1)
        for k in range(GROUPS):
            at = slice(k * PAD, (k + 1) * PAD)
            racc[rel_ref[k]] += mm(gq_ref[:, at], s_ref[at, :])
        for k in range(racc.shape[0]):
            rg_ref[k] = racc[k].T.astype(bf16)
        for p in range(PARTS):
            dg[p][...] = dacc[p * PART : (p + 1) * PART, :].astype(bf16)


def score_side(nxt, q, s, dst_rows, weights, rel_id, counts, kinds):
    return pl.pallas_call(
        score_kernel,
        grid_spec=pltpu.PrefetchScalarGridSpec(
            num_scalar_prefetch=2,
            grid=(NCH // 2,),
            in_specs=[
                *part_specs(),
                pl.BlockSpec((D, 2 * CH), lambda j, rel, cnt: (0, j)),
                pl.BlockSpec((GROUPS * PAD, D), lambda j, rel, cnt: (0, 0)),
                pl.BlockSpec((1, 1, 2 * CH), lambda j, rel, cnt: (j, 0, 0)),
                pl.BlockSpec((GROUPS, 8, ROWS), lambda j, rel, cnt: (0, 0, 0)),
            ],
            out_specs=[
                pl.BlockSpec((D, GROUPS * PAD), lambda j, rel, cnt: (0, 0)),
                *[pl.BlockSpec((PART, D), lambda j, rel, cnt: (0, 0))] * PARTS,
                pl.BlockSpec((kinds, D, D), lambda j, rel, cnt: (0, 0, 0)),
            ],
            scratch_shapes=[
                pltpu.VMEM((ROWS, CH), f32),
                pltpu.VMEM((D, ROWS), bf16),
                *[pltpu.VMEM((ROWS, CH), bf16)] * 2,
                *[pltpu.VMEM((D, CH), bf16)] * 2,
                *[pltpu.VMEM((8, CH), f32)] * 4,
                *[pltpu.VMEM((8, CH), jnp.int32)] * 2,
                pltpu.VMEM((ROWS, D), f32),
                pltpu.VMEM((ROWS, 8), f32),
                pltpu.VMEM((kinds, D, D), f32),
            ],
        ),
        out_shape=[
            jax.ShapeDtypeStruct((D, GROUPS * PAD), bf16),
            *[jax.ShapeDtypeStruct((PART, D), bf16)] * PARTS,
            jax.ShapeDtypeStruct((kinds, D, D), bf16),
        ],
        compiler_params=params(34),
        cost_estimate=cost(28),
        name="scores",
    )(rel_id, counts, *nxt, q, s, dst_rows, weights)


def source_kernel(rel_ref, gq_ref, src_ref, mat_ref, *refs):
    out, acc = refs[:PARTS], refs[PARTS]
    g = pl.program_id(0)

    @pl.when(g == 0)
    def _():
        acc[...] = jnp.zeros_like(acc)

    grad = mm(mat_ref[0].astype(bf16), gq_ref[...]).astype(bf16)
    rows = lax.broadcasted_iota(jnp.int32, (BLK, PAD), 0).astype(jnp.int16)
    for b in range(NBLK):
        at = slice(b * BLK, (b + 1) * BLK)
        acc[at, :] += mm(one_hot(rows, src_ref[0], b * BLK), grad, NT)

    @pl.when(g == GROUPS - 1)
    def _():
        for p in range(PARTS):
            out[p][...] = acc[p * PART : (p + 1) * PART, :].astype(bf16)


def source_side(gq, src_rows, rel_id, relation):
    return pl.pallas_call(
        source_kernel,
        grid_spec=pltpu.PrefetchScalarGridSpec(
            num_scalar_prefetch=1,
            grid=(GROUPS,),
            in_specs=[
                pl.BlockSpec((D, PAD), lambda j, rel: (0, j)),
                pl.BlockSpec((1, 1, PAD), lambda j, rel: (j, 0, 0)),
                pl.BlockSpec((1, D, D), lambda j, rel: (rel[j], 0, 0)),
            ],
            out_specs=[pl.BlockSpec((PART, D), lambda j, rel: (0, 0))] * PARTS,
            scratch_shapes=[pltpu.VMEM((ROWS, D), f32)],
        ),
        out_shape=[jax.ShapeDtypeStruct((PART, D), bf16)] * PARTS,
        compiler_params=params(16),
        cost_estimate=cost(8),
        name="source_grads",
    )(rel_id, gq, src_rows, relation)


def rowwise(param, accum, grad):
    fresh = accum + jnp.mean(grad * grad, -1)
    return (param - learn_rate * grad / jnp.sqrt(fresh)[..., None], fresh)


def shift_dom(block, by):
    size = lax.axis_size("dom")
    return lax.ppermute(block, "dom", [(i, (i + by) % size) for i in range(size)])


def swap_z(block):
    return lax.ppermute(block, "rep", [(i, i ^ 1) for i in range(8)])


def shift_x(block, by):
    return lax.ppermute(block, "rep", [(i, (i + 2 * by) % 8) for i in range(8)])


def spread_x(pair):
    return [pair] + [shift_x(pair, -k) for k in (1, 2, 3)]


def send_x(blocks):
    return [blocks[0]] + [shift_x(blocks[k], k) for k in (1, 2, 3)]


def add_up(blocks, after, dtype, copies=None):
    stacked = len(blocks) == 1
    shape = blocks[0].shape[1:] if stacked else blocks[0].shape
    whole = pl.BlockSpec(memory_space=pltpu.VMEM)

    def kernel(*refs):
        out = refs[-1]
        total = None
        if stacked:
            for i in range(blocks[0].shape[0]):
                part = refs[0][i].astype(f32)
                total = part if total is None else total + part
            total = total.astype(dtype)
        else:
            for ref in refs[: len(blocks)]:
                part = ref[...].astype(f32)
                total = part if total is None else total + part
            total = total.astype(dtype)
        if copies is None:
            out[...] = total
        else:
            for i in range(copies):
                out[i] = total

    return pl.pallas_call(
        kernel,
        in_specs=[whole] * len(blocks) + [pl.BlockSpec(memory_space=pl.ANY)],
        out_specs=whole,
        out_shape=jax.ShapeDtypeStruct(shape if copies is None else (copies,) + shape, dtype),
        compiler_params=pltpu.CompilerParams(vmem_limit_bytes=16 * MB),
        cost_estimate=cost(1),
        name="add_up",
    )(*blocks, after)


def split_sum(blocks, after):
    half = blocks[0].shape[0] // 2
    whole = pl.BlockSpec(memory_space=pltpu.VMEM)

    def kernel(*refs):
        for out, at in ((refs[-2], slice(0, half)), (refs[-1], slice(half, 2 * half))):
            total = None
            for ref in refs[: len(blocks)]:
                part = ref[at, :].astype(f32)
                total = part if total is None else total + part
            out[...] = total.astype(out.dtype)

    return pl.pallas_call(
        kernel,
        in_specs=[whole] * len(blocks) + [pl.BlockSpec(memory_space=pl.ANY)],
        out_specs=[whole] * 2,
        out_shape=[jax.ShapeDtypeStruct((half, D), f32), jax.ShapeDtypeStruct((half, D), bf16)],
        compiler_params=pltpu.CompilerParams(vmem_limit_bytes=16 * MB),
        cost_estimate=cost(1),
        name="split_sum",
    )(*blocks, after)


def relay(blocks, after):
    whole = pl.BlockSpec(memory_space=pltpu.VMEM)

    def kernel(*refs):
        for i in range(len(blocks)):
            refs[len(blocks) + 1 + i][...] = refs[i][...]

    return pl.pallas_call(
        kernel,
        in_specs=[whole] * len(blocks) + [pl.BlockSpec(memory_space=pl.ANY)],
        out_specs=[whole] * len(blocks),
        out_shape=[jax.ShapeDtypeStruct(block.shape, block.dtype) for block in blocks],
        compiler_params=pltpu.CompilerParams(vmem_limit_bytes=16 * MB),
        cost_estimate=cost(1),
        name="relay",
    )(*blocks, after)


def turned(index):
    rep = lax.axis_index("rep")
    return ((index - PART * (rep // 2)) % ROWS) ^ (256 * (rep % 2))


def operator_step(total, accum):
    rows, width = total.shape
    mine = lax.dynamic_slice(accum.reshape(-1), (lax.axis_index("dom") * rows,), (rows,))
    fresh = mine + jnp.mean(total * total, -1)
    step = total / jnp.sqrt(fresh)[:, None]
    power = jnp.floor(jnp.log2(fresh))
    part = fresh * jnp.exp2(-power)
    high = lax.reduce_precision(part, 5, 10)
    code = jnp.pad(jnp.stack([power, high, part - high]), ((0, 5), (0, width - rows)))
    send = jnp.concatenate([step, code]).astype(jnp.float16)
    return jnp.broadcast_to(send, (16,) + send.shape)


def operator_update(shares, relation, accum):
    rows, width = shares.shape[1] - 8, shares.shape[2]
    cores = [[2 * i + c for i in range(16)] for c in range(2)]
    half = lax.all_to_all(shares, "dom", 0, 0, axis_index_groups=cores)
    other = lax.ppermute(half, "dom", [(i, i ^ 1) for i in range(32)])
    second = lax.axis_index("dom") % 2 == 1
    pairs = [jnp.where(second, other, half), jnp.where(second, half, other)]
    full = jnp.stack(pairs, 1).reshape(32, rows + 8, width).astype(f32)
    steps = full[:, :rows].reshape(relation.shape)
    power, high, low = (full[:, rows + i, :rows].reshape(accum.shape) for i in range(3))
    return relation - learn_rate * steps, (high + low) * jnp.exp2(power)


def pad_slots(index, fill):
    return jnp.pad(index.reshape(GROUPS, SLOTS), ((0, 0), (0, PAD - SLOTS)), constant_values=fill)


def source_stage(own, src_pad, rel_id, relation):
    return make_queries(own, src_pad.reshape(GROUPS, 1, PAD), rel_id, relation)


def target_stage(nxt, q, s, dst_pad, weights, rel_id, counts, kinds):
    rows = dst_pad.reshape(NCH // 2, 1, 2 * CH)
    out = score_side(nxt, q, s, rows, weights, rel_id, counts, kinds)
    return out[0], out[1 : PARTS + 1], out[PARTS + 1]


def back_stage(gq, src_pad, rel_id, relation):
    return source_side(gq, src_pad.reshape(GROUPS, 1, PAD), rel_id, relation)


def local_grads(own, nxt, relation, src_index, dst_index, neg_index, rel_id, counts):
    own, nxt = own.astype(bf16), nxt.astype(bf16)
    src_pad = pad_slots(src_index, -1)
    weights = neg_weights(pad_slots(neg_index, -1))
    own, nxt = (jnp.split(rows, PARTS) for rows in (own, nxt))
    s, q = source_stage(own, src_pad, rel_id, relation)
    gq, dst_grad, rel_grad = target_stage(
        nxt, q, s, pad_slots(dst_index, -1), weights, rel_id, counts, relation.shape[0]
    )
    src_grad = back_stage(gq, src_pad, rel_id, relation)
    return jnp.concatenate(src_grad), jnp.concatenate(dst_grad), rel_grad


def on_device(
    entity, entity_accum, relation, relation_accum, src_index, dst_index, neg_index, rel_id, counts
):
    ent_b = entity.astype(bf16)
    src_pad = pad_slots(turned(src_index), -1)
    dst_pad = pad_slots(turned(dst_index), -1)
    neg_pad = pad_slots(turned(neg_index), -1)
    other = swap_z(ent_b)
    own = spread_x(jnp.concatenate([ent_b, other]))
    nxt = [shift_dom(block, -1) for block in own]
    weights = neg_weights(neg_pad)
    s, q = source_stage(own, src_pad, rel_id, relation)
    gq, dst_grad, rel_grad = target_stage(
        nxt, q, s, dst_pad, weights, rel_id, counts, relation.shape[0]
    )
    dst_blocks = send_x(dst_grad)
    got = lax.all_to_all(rel_grad.reshape(32, -1, D), "dom", 0, 0)
    src_grad = back_stage(gq, src_pad, rel_id, relation)
    mine = add_up([got], src_grad[0], f32)
    dst_sum = add_up(dst_blocks, mine, bf16)
    xsum = add_up([mine] + [shift_x(mine, k) for k in (1, 2, 3)], dst_sum, f32)
    zsum = xsum + swap_z(xsum)
    src_blocks = send_x([src_grad[0]] + list(relay(src_grad[1:], xsum)))
    moved = shift_dom(dst_sum, 1)
    shares = operator_step(zsum, relation_accum)
    relation_new, relation_accum_new = operator_update(shares, relation, relation_accum)
    keep, give = split_sum(src_blocks + [moved], zsum)
    grads = keep + swap_z(give).astype(f32)
    entity_new, entity_accum_new = rowwise(entity, entity_accum, grads)
    return (entity_new, entity_accum_new, relation_new, relation_accum_new)


def solution(mesh):
    placed = (
        P(("dom", "rep"), None),
        P(("dom", "rep")),
        P(),
        P(),
        P(("dom", "rep")),
        P(("dom", "rep")),
        P(("dom", "rep"), None),
        P(("dom", "rep")),
        P(("dom", "rep")),
    )
    return jax.shard_map(
        on_device,
        mesh=mesh,
        in_specs=placed,
        out_specs=(P(("dom", "rep"), None), P(("dom", "rep")), P(), P()),
        check_vma=False,
    )
```

```python
import functools
import jax
import jax.numpy as jnp
from jax import lax
from jax.experimental import pallas as pl
from jax.experimental.pallas import tpu as pltpu
from jax.sharding import PartitionSpec as P

learn_rate = 0.1
LOG2E = 1.4426950408889634
GROUPS = 4
SLOTS = 1000
PAD = 1024
ROWS = 2048
D = 256
BLK = 256
NBLK = ROWS // BLK
CH = 512
NCH = GROUPS * PAD // CH
PER = PAD // CH
bf16 = jnp.bfloat16
f32 = jnp.float32

NN = (((1,), (0,)), ((), ()))
NT = (((1,), (1,)), ((), ()))
MB = 1024 * 1024


def mm(a, b, dims=NN):
    return lax.dot_general(a, b, dims, preferred_element_type=f32)


def cost(us):
    return pl.CostEstimate(flops=int(us * 5e8), bytes_accessed=int(us * 3.5e6), transcendentals=0)


def params(size):
    return pltpu.CompilerParams(
        dimension_semantics=("arbitrary",), vmem_limit_bytes=size * MB
    )


def one_hot(rows, index, first):
    return jnp.where(rows == (index - first).astype(jnp.int16), bf16(1), bf16(0))


PARTS = 4
PART = ROWS // PARTS


def part_specs():
    return [pl.BlockSpec((PART, D), lambda *_: (0, 0))] * PARTS


def send_shapes():
    return [jax.ShapeDtypeStruct((PART, D), bf16)] + [pltpu.HBM((PART, D), bf16)] * (PARTS - 1)


def block_of(parts, b):
    first = b * BLK % PART
    return parts[b * BLK // PART][first : first + BLK, :]


def count_kernel(neg_ref, out_ref):
    rows = lax.broadcasted_iota(jnp.int32, (BLK, 128), 0).astype(jnp.int16)
    for b in range(NBLK):
        hits = None
        for c in range(0, PAD, 128):
            hot = one_hot(rows, neg_ref[0, :, c : c + 128], b * BLK)
            hits = hot if hits is None else hits + hot
        count = jnp.sum(hits.astype(f32), axis=1, keepdims=True)
        lane = lax.broadcasted_iota(jnp.int32, (BLK, 8), 1)
        out_ref[0, :, b * BLK : (b + 1) * BLK] = jnp.where(lane == 0, count, count + 1.0).T
    out_ref[0] = jnp.log2(out_ref[0])


def neg_weights(neg_pad):
    return pl.pallas_call(
        count_kernel,
        grid=(GROUPS,),
        in_specs=[pl.BlockSpec((1, 1, PAD), lambda g: (g, 0, 0))],
        out_specs=pl.BlockSpec((1, 8, ROWS), lambda g: (g, 0, 0)),
        out_shape=jax.ShapeDtypeStruct((GROUPS, 8, ROWS), f32),
        compiler_params=params(8),
        cost_estimate=cost(3),
        name="neg_weights",
    )(neg_pad.reshape(GROUPS, 1, PAD))


def query_kernel(rel_ref, *refs):
    own = refs[:PARTS]
    idx_ref, mat_ref, s_ref, q_ref = refs[PARTS:]
    column = jnp.broadcast_to(idx_ref[0].astype(f32), (128, PAD)).T
    column = column.astype(jnp.int32).astype(jnp.int16)
    cols = lax.broadcasted_iota(jnp.int32, (PAD, 128), 1).astype(jnp.int16)
    acc = None
    for b in range(NBLK):
        hot = jnp.concatenate(
            [
                jnp.where(cols + jnp.int16(first) == column, bf16(1), bf16(0))
                for first in (b * BLK, b * BLK + 128)
            ],
            axis=1,
        )
        part = mm(hot, block_of(own, b))
        acc = part if acc is None else acc + part
    rows = acc.astype(bf16)
    s_ref[...] = rows
    q_ref[...] = mm(mat_ref[0].astype(bf16).T, rows, NT).astype(bf16)


def make_queries(own, src_rows, rel_id, relation):
    return pl.pallas_call(
        query_kernel,
        grid_spec=pltpu.PrefetchScalarGridSpec(
            num_scalar_prefetch=1,
            grid=(GROUPS,),
            in_specs=[
                *part_specs(),
                pl.BlockSpec((1, 1, PAD), lambda j, rel: (j, 0, 0)),
                pl.BlockSpec((1, D, D), lambda j, rel: (rel[j], 0, 0)),
            ],
            out_specs=[
                pl.BlockSpec((PAD, D), lambda j, rel: (j, 0)),
                pl.BlockSpec((D, PAD), lambda j, rel: (0, j)),
            ],
        ),
        out_shape=[
            jax.ShapeDtypeStruct((GROUPS * PAD, D), bf16),
            jax.ShapeDtypeStruct((D, GROUPS * PAD), bf16),
        ],
        compiler_params=params(20),
        cost_estimate=cost(9),
        name="queries",
    )(rel_id, *own, src_rows, relation)


SUB = 32


def score_kernel(rel_ref, cnt_ref, *refs):
    nxt = refs[:PARTS]
    q_ref, s_ref, dst_ref, wt_ref, gq_ref = refs[PARTS : PARTS + 5]
    dg = refs[PARTS + 5 : 2 * PARTS + 5]
    rg_ref, sc, nxt_t_ref, *halves, dacc, wcol, racc = refs[
        2 * PARTS + 5 :
    ]
    old = halves[0::2], halves[1::2]
    g = pl.program_id(0)
    rows = lax.broadcasted_iota(jnp.int32, (SUB, CH), 0)
    rows16 = lax.broadcasted_iota(jnp.int32, (BLK, CH), 0).astype(jnp.int16)

    @pl.when(g == 0)
    def _():
        dacc[...] = jnp.zeros_like(dacc)
        racc[...] = jnp.zeros_like(racc)
        for ref in old[1]:
            ref[...] = jnp.zeros_like(ref)
        for b in range(NBLK):
            nxt_t_ref[:, b * BLK : (b + 1) * BLK] = block_of(nxt, b).T

    def spread(b, w, qs, sl, gain, dst):
        at = slice(b * BLK, (b + 1) * BLK)
        mask = rows16 == (dst[0:1, :] - b * BLK).astype(jnp.int16)
        full = jnp.where(mask, gain[0:1, :].astype(bf16), w[at, :])
        dacc[at, :] += mm(full, qs[...], NT)
        return mm(nxt_t_ref[:, at], full)

    def finish(acc, sl, chunk):
        gq = (acc * sl[0:1, :]).astype(bf16)
        gq_ref[:, pl.ds(pl.multiple_of(chunk * CH, CH), CH)] = gq

    def stage(half, chunk_old):
        w, qs, sl, gain_ref, dst_keep = old[half]
        before = old[1 - half]
        here = slice(half * CH, (half + 1) * CH)
        chunk = 2 * g + half
        group = chunk // PER
        for b in range(NBLK):
            at = slice(b * BLK, (b + 1) * BLK)
            wcol[at, :] = wt_ref[group, :, at].T
        q = q_ref[:, here]
        dst = dst_ref[0, 0:1, here]
        acc = None
        top = jnp.full((8, CH), -jnp.inf, f32)
        hit = jnp.zeros((8, CH), f32)
        for b in range(NBLK):
            raw = mm(block_of(nxt, b), q)
            for i in range(BLK // SUB):
                at = slice(b * BLK + i * SUB, b * BLK + (i + 1) * SUB)
                mask = rows == dst - (b * BLK + i * SUB)
                val = raw[i * SUB : (i + 1) * SUB] * LOG2E + jnp.where(
                    mask, wcol[at, 1:2], wcol[at, 0:1]
                )
                sc[at, :] = val
                top = jnp.maximum(top, jnp.max(val.reshape(SUB // 8, 8, CH), axis=0))
                hit = hit + jnp.sum(jnp.where(mask, val, 0.0).reshape(SUB // 8, 8, CH), axis=0)
            part = spread(b, *before)
            acc = part if acc is None else acc + part
        finish(acc, before[2], chunk_old)
        top = jnp.max(top, axis=0, keepdims=True)
        hit = jnp.sum(hit, axis=0, keepdims=True)
        tot = jnp.zeros((8, CH), f32)
        for b in range(NBLK):
            for i in range(BLK // SUB):
                at = slice(b * BLK + i * SUB, b * BLK + (i + 1) * SUB)
                e = jnp.exp2(sc[at, :] - top)
                tot = tot + jnp.sum(e.reshape(SUB // 8, 8, CH), axis=0)
                w[at, :] = e.astype(bf16)
        tot = jnp.sum(tot, axis=0, keepdims=True)
        gain_ref[...] = jnp.broadcast_to(jnp.exp2(hit - top) - tot, (8, CH))
        dst_keep[...] = jnp.broadcast_to(dst, (8, CH))
        lane = lax.broadcasted_iota(jnp.int32, (1, CH), 1) + lax.rem(chunk, PER) * CH
        live = jnp.logical_and(lane < SLOTS, group * SLOTS + lane < cnt_ref[0])
        scale = jnp.where(live, 1.0 / tot, 0.0)
        sl[...] = jnp.broadcast_to(scale, (8, CH))
        qs[...] = (q.astype(f32) * scale).astype(bf16)

    stage(0, jnp.maximum(2 * g - 1, 0))
    stage(1, 2 * g)

    @pl.when(g == NCH // 2 - 1)
    def _():
        acc = None
        for b in range(NBLK):
            part = spread(b, *old[1])
            acc = part if acc is None else acc + part
        finish(acc, old[1][2], 2 * g + 1)
        for k in range(GROUPS):
            at = slice(k * PAD, (k + 1) * PAD)
            racc[rel_ref[k]] += mm(gq_ref[:, at], s_ref[at, :])
        for k in range(racc.shape[0]):
            rg_ref[k] = racc[k].T.astype(bf16)
        for p in range(PARTS):
            dg[p][...] = dacc[p * PART : (p + 1) * PART, :].astype(bf16)


def score_side(nxt, q, s, dst_rows, weights, rel_id, counts, kinds):
    return pl.pallas_call(
        score_kernel,
        grid_spec=pltpu.PrefetchScalarGridSpec(
            num_scalar_prefetch=2,
            grid=(NCH // 2,),
            in_specs=[
                *part_specs(),
                pl.BlockSpec((D, 2 * CH), lambda j, rel, cnt: (0, j)),
                pl.BlockSpec((GROUPS * PAD, D), lambda j, rel, cnt: (0, 0)),
                pl.BlockSpec((1, 1, 2 * CH), lambda j, rel, cnt: (j, 0, 0)),
                pl.BlockSpec((GROUPS, 8, ROWS), lambda j, rel, cnt: (0, 0, 0)),
            ],
            out_specs=[
                pl.BlockSpec((D, GROUPS * PAD), lambda j, rel, cnt: (0, 0)),
                *[pl.BlockSpec((PART, D), lambda j, rel, cnt: (0, 0))] * PARTS,
                pl.BlockSpec((kinds, D, D), lambda j, rel, cnt: (0, 0, 0)),
            ],
            scratch_shapes=[
                pltpu.VMEM((ROWS, CH), f32),
                pltpu.VMEM((D, ROWS), bf16),
                *[pltpu.VMEM((ROWS, CH), bf16)] * 2,
                *[pltpu.VMEM((D, CH), bf16)] * 2,
                *[pltpu.VMEM((8, CH), f32)] * 4,
                *[pltpu.VMEM((8, CH), jnp.int32)] * 2,
                pltpu.VMEM((ROWS, D), f32),
                pltpu.VMEM((ROWS, 8), f32),
                pltpu.VMEM((kinds, D, D), f32),
            ],
        ),
        out_shape=[
            pltpu.HBM((D, GROUPS * PAD), bf16),
            *send_shapes(),
            jax.ShapeDtypeStruct((kinds, D, D), bf16),
        ],
        compiler_params=params(34),
        cost_estimate=cost(28),
        name="scores",
    )(rel_id, counts, *nxt, q, s, dst_rows, weights)


def source_kernel(rel_ref, gq_ref, src_ref, mat_ref, *refs):
    out, acc = refs[:PARTS], refs[PARTS]
    g = pl.program_id(0)

    @pl.when(g == 0)
    def _():
        acc[...] = jnp.zeros_like(acc)

    grad = mm(mat_ref[0].astype(bf16), gq_ref[...]).astype(bf16)
    rows = lax.broadcasted_iota(jnp.int32, (BLK, PAD), 0).astype(jnp.int16)
    for b in range(NBLK):
        at = slice(b * BLK, (b + 1) * BLK)
        acc[at, :] += mm(one_hot(rows, src_ref[0], b * BLK), grad, NT)

    @pl.when(g == GROUPS - 1)
    def _():
        for p in range(PARTS):
            out[p][...] = acc[p * PART : (p + 1) * PART, :].astype(bf16)


def source_side(gq, src_rows, rel_id, relation):
    return pl.pallas_call(
        source_kernel,
        grid_spec=pltpu.PrefetchScalarGridSpec(
            num_scalar_prefetch=1,
            grid=(GROUPS,),
            in_specs=[
                pl.BlockSpec((D, PAD), lambda j, rel: (0, j)),
                pl.BlockSpec((1, 1, PAD), lambda j, rel: (j, 0, 0)),
                pl.BlockSpec((1, D, D), lambda j, rel: (rel[j], 0, 0)),
            ],
            out_specs=[pl.BlockSpec((PART, D), lambda j, rel: (0, 0))] * PARTS,
            scratch_shapes=[pltpu.VMEM((ROWS, D), f32)],
        ),
        out_shape=send_shapes(),
        compiler_params=params(16),
        cost_estimate=cost(8),
        name="source_grads",
    )(rel_id, gq, src_rows, relation)


def rowwise(param, accum, grad):
    fresh = accum + jnp.mean(grad * grad, -1)
    return (param - learn_rate * grad / jnp.sqrt(fresh)[..., None], fresh)


def shift_dom(block, by):
    size = lax.axis_size("dom")
    return lax.ppermute(block, "dom", [(i, (i + by) % size) for i in range(size)])


def swap_z(block):
    return lax.ppermute(block, "rep", [(i, i ^ 1) for i in range(8)])


def shift_x(block, by):
    return lax.ppermute(block, "rep", [(i, (i + 2 * by) % 8) for i in range(8)])


def spread_x(pair):
    return [pair] + [shift_x(pair, -k) for k in (1, 2, 3)]


def send_x(blocks):
    return [blocks[0]] + [shift_x(blocks[k], k) for k in (1, 2, 3)]


def add_up(blocks, after, dtype, copies=None):
    stacked = len(blocks) == 1
    shape = blocks[0].shape[1:] if stacked else blocks[0].shape
    whole = pl.BlockSpec(memory_space=pltpu.VMEM)

    def kernel(*refs):
        out = refs[-1]
        total = None
        if stacked:
            for i in range(blocks[0].shape[0]):
                part = refs[0][i].astype(f32)
                total = part if total is None else total + part
            total = total.astype(dtype)
        else:
            for ref in refs[: len(blocks)]:
                part = ref[...].astype(f32)
                total = part if total is None else total + part
            total = total.astype(dtype)
        if copies is None:
            out[...] = total
        else:
            for i in range(copies):
                out[i] = total

    return pl.pallas_call(
        kernel,
        in_specs=[whole] * len(blocks) + [pl.BlockSpec(memory_space=pl.ANY)],
        out_specs=whole,
        out_shape=jax.ShapeDtypeStruct(shape if copies is None else (copies,) + shape, dtype),
        compiler_params=pltpu.CompilerParams(vmem_limit_bytes=16 * MB),
        cost_estimate=cost(1),
        name="add_up",
    )(*blocks, after)


def split_sum(blocks, after):
    half = blocks[0].shape[0] // 2
    whole = pl.BlockSpec(memory_space=pltpu.VMEM)

    def kernel(*refs):
        for out, at in ((refs[-2], slice(0, half)), (refs[-1], slice(half, 2 * half))):
            total = None
            for ref in refs[: len(blocks)]:
                part = ref[at, :].astype(f32)
                total = part if total is None else total + part
            out[...] = total.astype(out.dtype)

    return pl.pallas_call(
        kernel,
        in_specs=[whole] * len(blocks) + [pl.BlockSpec(memory_space=pl.ANY)],
        out_specs=[whole] * 2,
        out_shape=[jax.ShapeDtypeStruct((half, D), f32), jax.ShapeDtypeStruct((half, D), bf16)],
        compiler_params=pltpu.CompilerParams(vmem_limit_bytes=16 * MB),
        cost_estimate=cost(1),
        name="split_sum",
    )(*blocks, after)


def turned(index):
    rep = lax.axis_index("rep")
    return ((index - PART * (rep // 2)) % ROWS) ^ (256 * (rep % 2))


def operator_step(total, accum):
    rows, width = total.shape
    mine = lax.dynamic_slice(accum.reshape(-1), (lax.axis_index("dom") * rows,), (rows,))
    fresh = mine + jnp.mean(total * total, -1)
    step = total / jnp.sqrt(fresh)[:, None]
    power = jnp.floor(jnp.log2(fresh))
    part = fresh * jnp.exp2(-power)
    high = lax.reduce_precision(part, 5, 10)
    code = jnp.pad(jnp.stack([power, high, part - high]), ((0, 5), (0, width - rows)))
    send = jnp.concatenate([step, code]).astype(jnp.float16)
    return jnp.broadcast_to(send, (16,) + send.shape)


def operator_update(shares, relation, accum):
    rows, width = shares.shape[1] - 8, shares.shape[2]
    cores = [[2 * i + c for i in range(16)] for c in range(2)]
    half = lax.all_to_all(shares, "dom", 0, 0, axis_index_groups=cores)
    other = lax.ppermute(half, "dom", [(i, i ^ 1) for i in range(32)])
    second = lax.axis_index("dom") % 2 == 1
    pairs = [jnp.where(second, other, half), jnp.where(second, half, other)]
    full = jnp.stack(pairs, 1).reshape(32, rows + 8, width).astype(f32)
    steps = full[:, :rows].reshape(relation.shape)
    power, high, low = (full[:, rows + i, :rows].reshape(accum.shape) for i in range(3))
    return relation - learn_rate * steps, (high + low) * jnp.exp2(power)


def pad_slots(index, fill):
    return jnp.pad(index.reshape(GROUPS, SLOTS), ((0, 0), (0, PAD - SLOTS)), constant_values=fill)


def source_stage(own, src_pad, rel_id, relation):
    return make_queries(own, src_pad.reshape(GROUPS, 1, PAD), rel_id, relation)


def target_stage(nxt, q, s, dst_pad, weights, rel_id, counts, kinds):
    rows = dst_pad.reshape(NCH // 2, 1, 2 * CH)
    out = score_side(nxt, q, s, rows, weights, rel_id, counts, kinds)
    return out[0], out[1 : PARTS + 1], out[PARTS + 1]


def back_stage(gq, src_pad, rel_id, relation):
    return source_side(gq, src_pad.reshape(GROUPS, 1, PAD), rel_id, relation)


def local_grads(own, nxt, relation, src_index, dst_index, neg_index, rel_id, counts):
    own, nxt = own.astype(bf16), nxt.astype(bf16)
    src_pad = pad_slots(src_index, -1)
    weights = neg_weights(pad_slots(neg_index, -1))
    own, nxt = (jnp.split(rows, PARTS) for rows in (own, nxt))
    s, q = source_stage(own, src_pad, rel_id, relation)
    gq, dst_grad, rel_grad = target_stage(
        nxt, q, s, pad_slots(dst_index, -1), weights, rel_id, counts, relation.shape[0]
    )
    src_grad = back_stage(gq, src_pad, rel_id, relation)
    return jnp.concatenate(src_grad), jnp.concatenate(dst_grad), rel_grad


def on_device(
    entity, entity_accum, relation, relation_accum, src_index, dst_index, neg_index, rel_id, counts
):
    ent_b = entity.astype(bf16)
    src_pad = pad_slots(turned(src_index), -1)
    dst_pad = pad_slots(turned(dst_index), -1)
    neg_pad = pad_slots(turned(neg_index), -1)
    other = swap_z(ent_b)
    own = spread_x(jnp.concatenate([ent_b, other]))
    nxt = [shift_dom(block, -1) for block in own]
    weights = neg_weights(neg_pad)
    s, q = source_stage(own, src_pad, rel_id, relation)
    gq, dst_grad, rel_grad = target_stage(
        nxt, q, s, dst_pad, weights, rel_id, counts, relation.shape[0]
    )
    dst_blocks = send_x(dst_grad)
    got = lax.all_to_all(rel_grad.reshape(32, -1, D), "dom", 0, 0)
    src_grad = back_stage(gq, src_pad, rel_id, relation)
    src_blocks = send_x(src_grad)
    mine = add_up([got], src_grad[0], f32)
    zsum = mine + swap_z(mine)
    dst_sum = add_up(dst_blocks, mine, bf16)
    moved = shift_dom(dst_sum, 1)
    src_sum = add_up(src_blocks, dst_sum, f32)
    total = add_up([zsum] + [shift_x(zsum, k) for k in (1, 2, 3)], src_sum, f32)
    shares = operator_step(total, relation_accum)
    relation_new, relation_accum_new = operator_update(shares, relation, relation_accum)
    keep, give = split_sum([src_sum, moved], total)
    grads = keep + swap_z(give).astype(f32)
    entity_new, entity_accum_new = rowwise(entity, entity_accum, grads)
    return (entity_new, entity_accum_new, relation_new, relation_accum_new)


def solution(mesh):
    placed = (
        P(("dom", "rep"), None),
        P(("dom", "rep")),
        P(),
        P(),
        P(("dom", "rep")),
        P(("dom", "rep")),
        P(("dom", "rep"), None),
        P(("dom", "rep")),
        P(("dom", "rep")),
    )
    return jax.shard_map(
        on_device,
        mesh=mesh,
        in_specs=placed,
        out_specs=(P(("dom", "rep"), None), P(("dom", "rep")), P(), P()),
        check_vma=False,
    )
```

```python
import functools
import jax
import jax.numpy as jnp
from jax import lax
from jax.experimental import pallas as pl
from jax.experimental.pallas import tpu as pltpu
from jax.sharding import PartitionSpec as P

learn_rate = 0.1
LOG2E = 1.4426950408889634
GROUPS = 4
SLOTS = 1000
PAD = 1024
ROWS = 2048
D = 256
BLK = 256
NBLK = ROWS // BLK
CH = 512
NCH = GROUPS * PAD // CH
PER = PAD // CH
bf16 = jnp.bfloat16
f32 = jnp.float32

NN = (((1,), (0,)), ((), ()))
NT = (((1,), (1,)), ((), ()))
MB = 1024 * 1024


def mm(a, b, dims=NN):
    return lax.dot_general(a, b, dims, preferred_element_type=f32)


def cost(us):
    return pl.CostEstimate(flops=int(us * 5e8), bytes_accessed=int(us * 3.5e6), transcendentals=0)


def params(size):
    return pltpu.CompilerParams(
        dimension_semantics=("arbitrary",), vmem_limit_bytes=size * MB
    )


def one_hot(rows, index, first):
    return jnp.where(rows == (index - first).astype(jnp.int16), bf16(1), bf16(0))


PARTS = 4
PART = ROWS // PARTS


def part_specs():
    return [pl.BlockSpec((PART, D), lambda *_: (0, 0))] * PARTS


def send_shapes():
    return [jax.ShapeDtypeStruct((PART, D), bf16)] + [pltpu.HBM((PART, D), bf16)] * (PARTS - 1)


def block_of(parts, b):
    first = b * BLK % PART
    return parts[b * BLK // PART][first : first + BLK, :]


def count_kernel(neg_ref, out_ref):
    rows = lax.broadcasted_iota(jnp.int32, (BLK, 128), 0).astype(jnp.int16)
    for b in range(NBLK):
        hits = None
        for c in range(0, PAD, 128):
            hot = one_hot(rows, neg_ref[0, :, c : c + 128], b * BLK)
            hits = hot if hits is None else hits + hot
        count = jnp.sum(hits.astype(f32), axis=1, keepdims=True)
        lane = lax.broadcasted_iota(jnp.int32, (BLK, 8), 1)
        out_ref[0, :, b * BLK : (b + 1) * BLK] = jnp.where(lane == 0, count, count + 1.0).T
    out_ref[0] = jnp.log2(out_ref[0])


def neg_weights(neg_pad):
    return pl.pallas_call(
        count_kernel,
        grid=(GROUPS,),
        in_specs=[pl.BlockSpec((1, 1, PAD), lambda g: (g, 0, 0))],
        out_specs=pl.BlockSpec((1, 8, ROWS), lambda g: (g, 0, 0)),
        out_shape=jax.ShapeDtypeStruct((GROUPS, 8, ROWS), f32),
        compiler_params=params(8),
        cost_estimate=cost(3),
        name="neg_weights",
    )(neg_pad.reshape(GROUPS, 1, PAD))


def query_kernel(rel_ref, *refs):
    own = refs[:PARTS]
    idx_ref, mat_ref, s_ref, q_ref = refs[PARTS:]
    column = jnp.broadcast_to(idx_ref[0].astype(f32), (128, PAD)).T
    column = column.astype(jnp.int32).astype(jnp.int16)
    cols = lax.broadcasted_iota(jnp.int32, (PAD, 128), 1).astype(jnp.int16)
    acc = None
    for b in range(NBLK):
        hot = jnp.concatenate(
            [
                jnp.where(cols + jnp.int16(first) == column, bf16(1), bf16(0))
                for first in (b * BLK, b * BLK + 128)
            ],
            axis=1,
        )
        part = mm(hot, block_of(own, b))
        acc = part if acc is None else acc + part
    rows = acc.astype(bf16)
    s_ref[...] = rows
    q_ref[...] = mm(mat_ref[0].astype(bf16).T, rows, NT).astype(bf16)


def make_queries(own, src_rows, rel_id, relation):
    return pl.pallas_call(
        query_kernel,
        grid_spec=pltpu.PrefetchScalarGridSpec(
            num_scalar_prefetch=1,
            grid=(GROUPS,),
            in_specs=[
                *part_specs(),
                pl.BlockSpec((1, 1, PAD), lambda j, rel: (j, 0, 0)),
                pl.BlockSpec((1, D, D), lambda j, rel: (rel[j], 0, 0)),
            ],
            out_specs=[
                pl.BlockSpec((PAD, D), lambda j, rel: (j, 0)),
                pl.BlockSpec((D, PAD), lambda j, rel: (0, j)),
            ],
        ),
        out_shape=[
            jax.ShapeDtypeStruct((GROUPS * PAD, D), bf16),
            jax.ShapeDtypeStruct((D, GROUPS * PAD), bf16),
        ],
        compiler_params=params(20),
        cost_estimate=cost(9),
        name="queries",
    )(rel_id, *own, src_rows, relation)


SUB = 32


def score_kernel(rel_ref, cnt_ref, *refs):
    nxt = refs[:PARTS]
    q_ref, s_ref, dst_ref, wt_ref, gq_ref = refs[PARTS : PARTS + 5]
    dg = refs[PARTS + 5 : 2 * PARTS + 5]
    rg_ref, sc, nxt_t_ref, *halves, dacc, wcol, racc = refs[
        2 * PARTS + 5 :
    ]
    old = halves[0::2], halves[1::2]
    g = pl.program_id(0)
    rows = lax.broadcasted_iota(jnp.int32, (SUB, CH), 0)
    rows16 = lax.broadcasted_iota(jnp.int32, (BLK, CH), 0).astype(jnp.int16)

    @pl.when(g == 0)
    def _():
        dacc[...] = jnp.zeros_like(dacc)
        racc[...] = jnp.zeros_like(racc)
        for ref in old[1]:
            ref[...] = jnp.zeros_like(ref)
        for b in range(NBLK):
            nxt_t_ref[:, b * BLK : (b + 1) * BLK] = block_of(nxt, b).T

    def spread(b, w, qs, sl, gain, dst):
        at = slice(b * BLK, (b + 1) * BLK)
        mask = rows16 == (dst[0:1, :] - b * BLK).astype(jnp.int16)
        full = jnp.where(mask, gain[0:1, :].astype(bf16), w[at, :])
        dacc[at, :] += mm(full, qs[...], NT)
        return mm(nxt_t_ref[:, at], full)

    def finish(acc, sl, chunk):
        gq = (acc * sl[0:1, :]).astype(bf16)
        gq_ref[:, pl.ds(pl.multiple_of(chunk * CH, CH), CH)] = gq

    def stage(half, chunk_old):
        w, qs, sl, gain_ref, dst_keep = old[half]
        before = old[1 - half]
        here = slice(half * CH, (half + 1) * CH)
        chunk = 2 * g + half
        group = chunk // PER
        for b in range(NBLK):
            at = slice(b * BLK, (b + 1) * BLK)
            wcol[at, :] = wt_ref[group, :, at].T
        q = q_ref[:, here]
        dst = dst_ref[0, 0:1, here]
        acc = None
        top = jnp.full((8, CH), -jnp.inf, f32)
        hit = jnp.zeros((8, CH), f32)
        for b in range(NBLK):
            raw = mm(block_of(nxt, b), q)
            for i in range(BLK // SUB):
                at = slice(b * BLK + i * SUB, b * BLK + (i + 1) * SUB)
                mask = rows == dst - (b * BLK + i * SUB)
                val = raw[i * SUB : (i + 1) * SUB] * LOG2E + jnp.where(
                    mask, wcol[at, 1:2], wcol[at, 0:1]
                )
                sc[at, :] = val
                top = jnp.maximum(top, jnp.max(val.reshape(SUB // 8, 8, CH), axis=0))
                hit = hit + jnp.sum(jnp.where(mask, val, 0.0).reshape(SUB // 8, 8, CH), axis=0)
            part = spread(b, *before)
            acc = part if acc is None else acc + part
        finish(acc, before[2], chunk_old)
        top = jnp.max(top, axis=0, keepdims=True)
        hit = jnp.sum(hit, axis=0, keepdims=True)
        tot = jnp.zeros((8, CH), f32)
        for b in range(NBLK):
            for i in range(BLK // SUB):
                at = slice(b * BLK + i * SUB, b * BLK + (i + 1) * SUB)
                e = jnp.exp2(sc[at, :] - top)
                tot = tot + jnp.sum(e.reshape(SUB // 8, 8, CH), axis=0)
                w[at, :] = e.astype(bf16)
        tot = jnp.sum(tot, axis=0, keepdims=True)
        gain_ref[...] = jnp.broadcast_to(jnp.exp2(hit - top) - tot, (8, CH))
        dst_keep[...] = jnp.broadcast_to(dst, (8, CH))
        lane = lax.broadcasted_iota(jnp.int32, (1, CH), 1) + lax.rem(chunk, PER) * CH
        live = jnp.logical_and(lane < SLOTS, group * SLOTS + lane < cnt_ref[0])
        scale = jnp.where(live, 1.0 / tot, 0.0)
        sl[...] = jnp.broadcast_to(scale, (8, CH))
        qs[...] = (q.astype(f32) * scale).astype(bf16)

    stage(0, jnp.maximum(2 * g - 1, 0))
    stage(1, 2 * g)

    @pl.when(g == NCH // 2 - 1)
    def _():
        acc = None
        for b in range(NBLK):
            part = spread(b, *old[1])
            acc = part if acc is None else acc + part
        finish(acc, old[1][2], 2 * g + 1)
        for k in range(GROUPS):
            at = slice(k * PAD, (k + 1) * PAD)
            racc[rel_ref[k]] += mm(gq_ref[:, at], s_ref[at, :])
        for k in range(racc.shape[0]):
            rg_ref[k] = racc[k].T.astype(bf16)
        for p in range(PARTS):
            dg[p][...] = dacc[p * PART : (p + 1) * PART, :].astype(bf16)


def score_side(nxt, q, s, dst_rows, weights, rel_id, counts, kinds):
    return pl.pallas_call(
        score_kernel,
        grid_spec=pltpu.PrefetchScalarGridSpec(
            num_scalar_prefetch=2,
            grid=(NCH // 2,),
            in_specs=[
                *part_specs(),
                pl.BlockSpec((D, 2 * CH), lambda j, rel, cnt: (0, j)),
                pl.BlockSpec((GROUPS * PAD, D), lambda j, rel, cnt: (0, 0)),
                pl.BlockSpec((1, 1, 2 * CH), lambda j, rel, cnt: (j, 0, 0)),
                pl.BlockSpec((GROUPS, 8, ROWS), lambda j, rel, cnt: (0, 0, 0)),
            ],
            out_specs=[
                pl.BlockSpec((D, GROUPS * PAD), lambda j, rel, cnt: (0, 0)),
                *[pl.BlockSpec((PART, D), lambda j, rel, cnt: (0, 0))] * PARTS,
                pl.BlockSpec((kinds, D, D), lambda j, rel, cnt: (0, 0, 0)),
            ],
            scratch_shapes=[
                pltpu.VMEM((ROWS, CH), f32),
                pltpu.VMEM((D, ROWS), bf16),
                *[pltpu.VMEM((ROWS, CH), bf16)] * 2,
                *[pltpu.VMEM((D, CH), bf16)] * 2,
                *[pltpu.VMEM((8, CH), f32)] * 4,
                *[pltpu.VMEM((8, CH), jnp.int32)] * 2,
                pltpu.VMEM((ROWS, D), f32),
                pltpu.VMEM((ROWS, 8), f32),
                pltpu.VMEM((kinds, D, D), f32),
            ],
        ),
        out_shape=[
            pltpu.HBM((D, GROUPS * PAD), bf16),
            *send_shapes(),
            jax.ShapeDtypeStruct((kinds, D, D), bf16),
        ],
        compiler_params=params(34),
        cost_estimate=cost(28),
        name="scores",
    )(rel_id, counts, *nxt, q, s, dst_rows, weights)


def source_kernel(rel_ref, gq_ref, src_ref, mat_ref, *refs):
    out, acc = refs[:PARTS], refs[PARTS]
    g = pl.program_id(0)

    @pl.when(g == 0)
    def _():
        acc[...] = jnp.zeros_like(acc)

    grad = mm(mat_ref[0].astype(bf16), gq_ref[...]).astype(bf16)
    rows = lax.broadcasted_iota(jnp.int32, (BLK, PAD), 0).astype(jnp.int16)
    for b in range(NBLK):
        at = slice(b * BLK, (b + 1) * BLK)
        acc[at, :] += mm(one_hot(rows, src_ref[0], b * BLK), grad, NT)

    @pl.when(g == GROUPS - 1)
    def _():
        for p in range(PARTS):
            out[p][...] = acc[p * PART : (p + 1) * PART, :].astype(bf16)


def source_side(gq, src_rows, rel_id, relation):
    return pl.pallas_call(
        source_kernel,
        grid_spec=pltpu.PrefetchScalarGridSpec(
            num_scalar_prefetch=1,
            grid=(GROUPS,),
            in_specs=[
                pl.BlockSpec((D, PAD), lambda j, rel: (0, j)),
                pl.BlockSpec((1, 1, PAD), lambda j, rel: (j, 0, 0)),
                pl.BlockSpec((1, D, D), lambda j, rel: (rel[j], 0, 0)),
            ],
            out_specs=[pl.BlockSpec((PART, D), lambda j, rel: (0, 0))] * PARTS,
            scratch_shapes=[pltpu.VMEM((ROWS, D), f32)],
        ),
        out_shape=send_shapes(),
        compiler_params=params(16),
        cost_estimate=cost(8),
        name="source_grads",
    )(rel_id, gq, src_rows, relation)


def rowwise(param, accum, grad):
    fresh = accum + jnp.mean(grad * grad, -1)
    return (param - learn_rate * grad / jnp.sqrt(fresh)[..., None], fresh)


def shift_dom(block, by):
    size = lax.axis_size("dom")
    return lax.ppermute(block, "dom", [(i, (i + by) % size) for i in range(size)])


def swap_z(block):
    return lax.ppermute(block, "rep", [(i, i ^ 1) for i in range(8)])


def shift_x(block, by):
    return lax.ppermute(block, "rep", [(i, (i + 2 * by) % 8) for i in range(8)])


def spread_x(pair):
    return [pair] + [shift_x(pair, -k) for k in (1, 2, 3)]


def send_x(blocks):
    return [blocks[0]] + [shift_x(blocks[k], k) for k in (1, 2, 3)]


def add_up(blocks, after, dtype, copies=None):
    stacked = len(blocks) == 1
    shape = blocks[0].shape[1:] if stacked else blocks[0].shape
    whole = pl.BlockSpec(memory_space=pltpu.VMEM)

    def kernel(*refs):
        out = refs[-1]
        total = None
        if stacked:
            for i in range(blocks[0].shape[0]):
                part = refs[0][i].astype(f32)
                total = part if total is None else total + part
            total = total.astype(dtype)
        else:
            for ref in refs[: len(blocks)]:
                part = ref[...].astype(f32)
                total = part if total is None else total + part
            total = total.astype(dtype)
        if copies is None:
            out[...] = total
        else:
            for i in range(copies):
                out[i] = total

    return pl.pallas_call(
        kernel,
        in_specs=[whole] * len(blocks) + [pl.BlockSpec(memory_space=pl.ANY)],
        out_specs=whole,
        out_shape=jax.ShapeDtypeStruct(shape if copies is None else (copies,) + shape, dtype),
        compiler_params=pltpu.CompilerParams(vmem_limit_bytes=16 * MB),
        cost_estimate=cost(1),
        name="add_up",
    )(*blocks, after)


def split_sum(blocks, after):
    half = blocks[0].shape[0] // 2
    whole = pl.BlockSpec(memory_space=pltpu.VMEM)

    def kernel(*refs):
        for out, at in ((refs[-2], slice(0, half)), (refs[-1], slice(half, 2 * half))):
            total = None
            for ref in refs[: len(blocks)]:
                part = ref[at, :].astype(f32)
                total = part if total is None else total + part
            out[...] = total.astype(out.dtype)

    return pl.pallas_call(
        kernel,
        in_specs=[whole] * len(blocks) + [pl.BlockSpec(memory_space=pl.ANY)],
        out_specs=[whole] * 2,
        out_shape=[jax.ShapeDtypeStruct((half, D), f32), jax.ShapeDtypeStruct((half, D), bf16)],
        compiler_params=pltpu.CompilerParams(vmem_limit_bytes=16 * MB),
        cost_estimate=cost(1),
        name="split_sum",
    )(*blocks, after)


def turned(index):
    rep = lax.axis_index("rep")
    return ((index - PART * (rep // 2)) % ROWS) ^ (256 * (rep % 2))


def operator_step(total, accum):
    rows, width = total.shape
    mine = lax.dynamic_slice(accum.reshape(-1), (lax.axis_index("dom") * rows,), (rows,))
    fresh = mine + jnp.mean(total * total, -1)
    step = total / jnp.sqrt(fresh)[:, None]
    power = jnp.floor(jnp.log2(fresh))
    part = fresh * jnp.exp2(-power)
    high = lax.reduce_precision(part, 5, 10)
    code = jnp.pad(jnp.stack([power, high, part - high]), ((0, 5), (0, width - rows)))
    send = jnp.concatenate([step, code]).astype(jnp.float16)
    return jnp.broadcast_to(send, (16,) + send.shape)


def operator_update(shares, relation, accum):
    rows, width = shares.shape[1] - 8, shares.shape[2]
    cores = [[2 * i + c for i in range(16)] for c in range(2)]
    half = lax.all_to_all(shares, "dom", 0, 0, axis_index_groups=cores)
    other = lax.ppermute(half, "dom", [(i, i ^ 1) for i in range(32)])
    second = lax.axis_index("dom") % 2 == 1
    pairs = [jnp.where(second, other, half), jnp.where(second, half, other)]
    full = jnp.stack(pairs, 1).reshape(32, rows + 8, width).astype(f32)
    steps = full[:, :rows].reshape(relation.shape)
    power, high, low = (full[:, rows + i, :rows].reshape(accum.shape) for i in range(3))
    return relation - learn_rate * steps, (high + low) * jnp.exp2(power)


def pad_slots(index, fill):
    return jnp.pad(index.reshape(GROUPS, SLOTS), ((0, 0), (0, PAD - SLOTS)), constant_values=fill)


def source_stage(own, src_pad, rel_id, relation):
    return make_queries(own, src_pad.reshape(GROUPS, 1, PAD), rel_id, relation)


def target_stage(nxt, q, s, dst_pad, weights, rel_id, counts, kinds):
    rows = dst_pad.reshape(NCH // 2, 1, 2 * CH)
    out = score_side(nxt, q, s, rows, weights, rel_id, counts, kinds)
    return out[0], out[1 : PARTS + 1], out[PARTS + 1]


def back_stage(gq, src_pad, rel_id, relation):
    return source_side(gq, src_pad.reshape(GROUPS, 1, PAD), rel_id, relation)


def local_grads(own, nxt, relation, src_index, dst_index, neg_index, rel_id, counts):
    own, nxt = own.astype(bf16), nxt.astype(bf16)
    src_pad = pad_slots(src_index, -1)
    weights = neg_weights(pad_slots(neg_index, -1))
    own, nxt = (jnp.split(rows, PARTS) for rows in (own, nxt))
    s, q = source_stage(own, src_pad, rel_id, relation)
    gq, dst_grad, rel_grad = target_stage(
        nxt, q, s, pad_slots(dst_index, -1), weights, rel_id, counts, relation.shape[0]
    )
    src_grad = back_stage(gq, src_pad, rel_id, relation)
    return jnp.concatenate(src_grad), jnp.concatenate(dst_grad), rel_grad


def on_device(
    entity, entity_accum, relation, relation_accum, src_index, dst_index, neg_index, rel_id, counts
):
    ent_b = entity.astype(bf16)
    src_pad = pad_slots(turned(src_index), -1)
    dst_pad = pad_slots(turned(dst_index), -1)
    neg_pad = pad_slots(turned(neg_index), -1)
    other = swap_z(ent_b)
    own = spread_x(jnp.concatenate([ent_b, other]))
    nxt = [shift_dom(block, -1) for block in own]
    weights = neg_weights(neg_pad)
    s, q = source_stage(own, src_pad, rel_id, relation)
    gq, dst_grad, rel_grad = target_stage(
        nxt, q, s, dst_pad, weights, rel_id, counts, relation.shape[0]
    )
    dst_blocks = send_x(dst_grad)
    got = lax.all_to_all(rel_grad.reshape(32, -1, D), "dom", 0, 0)
    src_grad = back_stage(gq, src_pad, rel_id, relation)
    src_blocks = send_x(src_grad)
    mine = add_up([got], src_grad[0], f32)
    zsum = mine + swap_z(mine)
    dst_sum = add_up(dst_blocks, mine, bf16)
    moved = shift_dom(dst_sum, 1)
    src_sum = add_up(src_blocks + [moved], dst_sum, f32)
    total = add_up([zsum] + [shift_x(zsum, k) for k in (1, 2, 3)], src_sum, f32)
    shares = operator_step(total, relation_accum)
    relation_new, relation_accum_new = operator_update(shares, relation, relation_accum)
    keep, give = split_sum([src_sum], total)
    grads = keep + swap_z(give).astype(f32)
    entity_new, entity_accum_new = rowwise(entity, entity_accum, grads)
    return (entity_new, entity_accum_new, relation_new, relation_accum_new)


def solution(mesh):
    placed = (
        P(("dom", "rep"), None),
        P(("dom", "rep")),
        P(),
        P(),
        P(("dom", "rep")),
        P(("dom", "rep")),
        P(("dom", "rep"), None),
        P(("dom", "rep")),
        P(("dom", "rep")),
    )
    return jax.shard_map(
        on_device,
        mesh=mesh,
        in_specs=placed,
        out_specs=(P(("dom", "rep"), None), P(("dom", "rep")), P(), P()),
        check_vma=False,
    )
```

```python
import functools
import jax
import jax.numpy as jnp
from jax import lax
from jax.experimental import pallas as pl
from jax.experimental.pallas import tpu as pltpu
from jax.sharding import PartitionSpec as P

learn_rate = 0.1
LOG2E = 1.4426950408889634
GROUPS = 4
SLOTS = 1000
PAD = 1024
ROWS = 2048
D = 256
BLK = 256
NBLK = ROWS // BLK
CH = 512
NCH = GROUPS * PAD // CH
PER = PAD // CH
bf16 = jnp.bfloat16
f32 = jnp.float32

NN = (((1,), (0,)), ((), ()))
NT = (((1,), (1,)), ((), ()))
MB = 1024 * 1024


def mm(a, b, dims=NN):
    return lax.dot_general(a, b, dims, preferred_element_type=f32)


def cost(us):
    return pl.CostEstimate(flops=int(us * 5e8), bytes_accessed=int(us * 3.5e6), transcendentals=0)


def params(size):
    return pltpu.CompilerParams(
        dimension_semantics=("arbitrary",), vmem_limit_bytes=size * MB
    )


def one_hot(rows, index, first):
    return jnp.where(rows == (index - first).astype(jnp.int16), bf16(1), bf16(0))


PARTS = 4
PART = ROWS // PARTS


def part_specs():
    return [pl.BlockSpec((PART, D), lambda *_: (0, 0))] * PARTS


def send_shapes():
    return [jax.ShapeDtypeStruct((PART, D), bf16)] + [pltpu.HBM((PART, D), bf16)] * (PARTS - 1)


def block_of(parts, b):
    first = b * BLK % PART
    return parts[b * BLK // PART][first : first + BLK, :]


def count_kernel(neg_ref, out_ref):
    rows = lax.broadcasted_iota(jnp.int32, (BLK, 128), 0).astype(jnp.int16)
    for b in range(NBLK):
        hits = None
        for c in range(0, PAD, 128):
            hot = one_hot(rows, neg_ref[0, :, c : c + 128], b * BLK)
            hits = hot if hits is None else hits + hot
        count = jnp.sum(hits.astype(f32), axis=1, keepdims=True)
        lane = lax.broadcasted_iota(jnp.int32, (BLK, 8), 1)
        out_ref[0, :, b * BLK : (b + 1) * BLK] = jnp.where(lane == 0, count, count + 1.0).T
    out_ref[0] = jnp.log2(out_ref[0])


def neg_weights(neg_pad):
    return pl.pallas_call(
        count_kernel,
        grid=(GROUPS,),
        in_specs=[pl.BlockSpec((1, 1, PAD), lambda g: (g, 0, 0))],
        out_specs=pl.BlockSpec((1, 8, ROWS), lambda g: (g, 0, 0)),
        out_shape=jax.ShapeDtypeStruct((GROUPS, 8, ROWS), f32),
        compiler_params=params(8),
        cost_estimate=cost(3),
        name="neg_weights",
    )(neg_pad.reshape(GROUPS, 1, PAD))


def query_kernel(rel_ref, *refs):
    own = refs[:PARTS]
    idx_ref, mat_ref, s_ref, q_ref = refs[PARTS:]
    column = jnp.broadcast_to(idx_ref[0].astype(f32), (128, PAD)).T
    column = column.astype(jnp.int32).astype(jnp.int16)
    cols = lax.broadcasted_iota(jnp.int32, (PAD, 128), 1).astype(jnp.int16)
    acc = None
    for b in range(NBLK):
        hot = jnp.concatenate(
            [
                jnp.where(cols + jnp.int16(first) == column, bf16(1), bf16(0))
                for first in (b * BLK, b * BLK + 128)
            ],
            axis=1,
        )
        part = mm(hot, block_of(own, b))
        acc = part if acc is None else acc + part
    rows = acc.astype(bf16)
    s_ref[...] = rows
    q_ref[...] = mm(mat_ref[0].astype(bf16).T, rows, NT).astype(bf16)


def make_queries(own, src_rows, rel_id, relation):
    return pl.pallas_call(
        query_kernel,
        grid_spec=pltpu.PrefetchScalarGridSpec(
            num_scalar_prefetch=1,
            grid=(GROUPS,),
            in_specs=[
                *part_specs(),
                pl.BlockSpec((1, 1, PAD), lambda j, rel: (j, 0, 0)),
                pl.BlockSpec((1, D, D), lambda j, rel: (rel[j], 0, 0)),
            ],
            out_specs=[
                pl.BlockSpec((PAD, D), lambda j, rel: (j, 0)),
                pl.BlockSpec((D, PAD), lambda j, rel: (0, j)),
            ],
        ),
        out_shape=[
            jax.ShapeDtypeStruct((GROUPS * PAD, D), bf16),
            jax.ShapeDtypeStruct((D, GROUPS * PAD), bf16),
        ],
        compiler_params=params(20),
        cost_estimate=cost(9),
        name="queries",
    )(rel_id, *own, src_rows, relation)


SUB = 32


def score_kernel(rel_ref, cnt_ref, *refs):
    nxt = refs[:PARTS]
    q_ref, s_ref, dst_ref, wt_ref, gq_ref = refs[PARTS : PARTS + 5]
    dg = refs[PARTS + 5 : 2 * PARTS + 5]
    rg_ref, sc, nxt_t_ref, *halves, dacc, wcol, racc = refs[
        2 * PARTS + 5 :
    ]
    old = halves[0::2], halves[1::2]
    g = pl.program_id(0)
    rows = lax.broadcasted_iota(jnp.int32, (SUB, CH), 0)
    rows16 = lax.broadcasted_iota(jnp.int32, (BLK, CH), 0).astype(jnp.int16)

    @pl.when(g == 0)
    def _():
        dacc[...] = jnp.zeros_like(dacc)
        racc[...] = jnp.zeros_like(racc)
        for ref in old[1]:
            ref[...] = jnp.zeros_like(ref)
        for b in range(NBLK):
            nxt_t_ref[:, b * BLK : (b + 1) * BLK] = block_of(nxt, b).T

    def spread(b, w, qs, sl, gain, dst):
        at = slice(b * BLK, (b + 1) * BLK)
        mask = rows16 == (dst[0:1, :] - b * BLK).astype(jnp.int16)
        full = jnp.where(mask, gain[0:1, :].astype(bf16), w[at, :])
        dacc[at, :] += mm(full, qs[...], NT)
        return mm(nxt_t_ref[:, at], full)

    def finish(acc, sl, chunk):
        gq = (acc * sl[0:1, :]).astype(bf16)
        gq_ref[:, pl.ds(pl.multiple_of(chunk * CH, CH), CH)] = gq

    def stage(half, chunk_old):
        w, qs, sl, gain_ref, dst_keep = old[half]
        before = old[1 - half]
        here = slice(half * CH, (half + 1) * CH)
        chunk = 2 * g + half
        group = chunk // PER
        for b in range(NBLK):
            at = slice(b * BLK, (b + 1) * BLK)
            wcol[at, :] = wt_ref[group, :, at].T
        q = q_ref[:, here]
        dst = dst_ref[0, 0:1, here]
        acc = None
        top = jnp.full((8, CH), -jnp.inf, f32)
        hit = jnp.zeros((8, CH), f32)
        for b in range(NBLK):
            raw = mm(block_of(nxt, b), q)
            for i in range(BLK // SUB):
                at = slice(b * BLK + i * SUB, b * BLK + (i + 1) * SUB)
                mask = rows == dst - (b * BLK + i * SUB)
                val = raw[i * SUB : (i + 1) * SUB] * LOG2E + jnp.where(
                    mask, wcol[at, 1:2], wcol[at, 0:1]
                )
                sc[at, :] = val
                top = jnp.maximum(top, jnp.max(val.reshape(SUB // 8, 8, CH), axis=0))
                hit = hit + jnp.sum(jnp.where(mask, val, 0.0).reshape(SUB // 8, 8, CH), axis=0)
            part = spread(b, *before)
            acc = part if acc is None else acc + part
        finish(acc, before[2], chunk_old)
        top = jnp.max(top, axis=0, keepdims=True)
        hit = jnp.sum(hit, axis=0, keepdims=True)
        tot = jnp.zeros((8, CH), f32)
        for b in range(NBLK):
            for i in range(BLK // SUB):
                at = slice(b * BLK + i * SUB, b * BLK + (i + 1) * SUB)
                e = jnp.exp2(sc[at, :] - top)
                tot = tot + jnp.sum(e.reshape(SUB // 8, 8, CH), axis=0)
                w[at, :] = e.astype(bf16)
        tot = jnp.sum(tot, axis=0, keepdims=True)
        gain_ref[...] = jnp.broadcast_to(jnp.exp2(hit - top) - tot, (8, CH))
        dst_keep[...] = jnp.broadcast_to(dst, (8, CH))
        lane = lax.broadcasted_iota(jnp.int32, (1, CH), 1) + lax.rem(chunk, PER) * CH
        live = jnp.logical_and(lane < SLOTS, group * SLOTS + lane < cnt_ref[0])
        scale = jnp.where(live, 1.0 / tot, 0.0)
        sl[...] = jnp.broadcast_to(scale, (8, CH))
        qs[...] = (q.astype(f32) * scale).astype(bf16)

    stage(0, jnp.maximum(2 * g - 1, 0))
    stage(1, 2 * g)

    @pl.when(g == NCH // 2 - 1)
    def _():
        acc = None
        for b in range(NBLK):
            part = spread(b, *old[1])
            acc = part if acc is None else acc + part
        finish(acc, old[1][2], 2 * g + 1)
        for k in range(GROUPS):
            at = slice(k * PAD, (k + 1) * PAD)
            racc[rel_ref[k]] += mm(gq_ref[:, at], s_ref[at, :])
        for k in range(racc.shape[0]):
            rg_ref[k] = racc[k].T.astype(bf16)
        for p in range(PARTS):
            dg[p][...] = dacc[p * PART : (p + 1) * PART, :].astype(bf16)


def score_side(nxt, q, s, dst_rows, weights, rel_id, counts, kinds):
    return pl.pallas_call(
        score_kernel,
        grid_spec=pltpu.PrefetchScalarGridSpec(
            num_scalar_prefetch=2,
            grid=(NCH // 2,),
            in_specs=[
                *part_specs(),
                pl.BlockSpec((D, 2 * CH), lambda j, rel, cnt: (0, j)),
                pl.BlockSpec((GROUPS * PAD, D), lambda j, rel, cnt: (0, 0)),
                pl.BlockSpec((1, 1, 2 * CH), lambda j, rel, cnt: (j, 0, 0)),
                pl.BlockSpec((GROUPS, 8, ROWS), lambda j, rel, cnt: (0, 0, 0)),
            ],
            out_specs=[
                pl.BlockSpec((D, GROUPS * PAD), lambda j, rel, cnt: (0, 0)),
                *[pl.BlockSpec((PART, D), lambda j, rel, cnt: (0, 0))] * PARTS,
                pl.BlockSpec((kinds, D, D), lambda j, rel, cnt: (0, 0, 0)),
            ],
            scratch_shapes=[
                pltpu.VMEM((ROWS, CH), f32),
                pltpu.VMEM((D, ROWS), bf16),
                *[pltpu.VMEM((ROWS, CH), bf16)] * 2,
                *[pltpu.VMEM((D, CH), bf16)] * 2,
                *[pltpu.VMEM((8, CH), f32)] * 4,
                *[pltpu.VMEM((8, CH), jnp.int32)] * 2,
                pltpu.VMEM((ROWS, D), f32),
                pltpu.VMEM((ROWS, 8), f32),
                pltpu.VMEM((kinds, D, D), f32),
            ],
        ),
        out_shape=[
            pltpu.HBM((D, GROUPS * PAD), bf16),
            *send_shapes(),
            jax.ShapeDtypeStruct((kinds, D, D), bf16),
        ],
        compiler_params=params(34),
        cost_estimate=cost(28),
        name="scores",
    )(rel_id, counts, *nxt, q, s, dst_rows, weights)


def source_kernel(rel_ref, gq_ref, src_ref, mat_ref, *refs):
    out, acc = refs[:PARTS], refs[PARTS]
    g = pl.program_id(0)

    @pl.when(g == 0)
    def _():
        acc[...] = jnp.zeros_like(acc)

    grad = mm(mat_ref[0].astype(bf16), gq_ref[...]).astype(bf16)
    rows = lax.broadcasted_iota(jnp.int32, (BLK, PAD), 0).astype(jnp.int16)
    for b in range(NBLK):
        at = slice(b * BLK, (b + 1) * BLK)
        acc[at, :] += mm(one_hot(rows, src_ref[0], b * BLK), grad, NT)

    @pl.when(g == GROUPS - 1)
    def _():
        for p in range(PARTS):
            out[p][...] = acc[p * PART : (p + 1) * PART, :].astype(bf16)


def source_side(gq, src_rows, rel_id, relation):
    return pl.pallas_call(
        source_kernel,
        grid_spec=pltpu.PrefetchScalarGridSpec(
            num_scalar_prefetch=1,
            grid=(GROUPS,),
            in_specs=[
                pl.BlockSpec((D, PAD), lambda j, rel: (0, j)),
                pl.BlockSpec((1, 1, PAD), lambda j, rel: (j, 0, 0)),
                pl.BlockSpec((1, D, D), lambda j, rel: (rel[j], 0, 0)),
            ],
            out_specs=[pl.BlockSpec((PART, D), lambda j, rel: (0, 0))] * PARTS,
            scratch_shapes=[pltpu.VMEM((ROWS, D), f32)],
        ),
        out_shape=send_shapes(),
        compiler_params=params(48),
        cost_estimate=cost(8),
        name="source_grads",
    )(rel_id, gq, src_rows, relation)


def rowwise(param, accum, grad):
    fresh = accum + jnp.mean(grad * grad, -1)
    return (param - learn_rate * grad / jnp.sqrt(fresh)[..., None], fresh)


def shift_dom(block, by):
    size = lax.axis_size("dom")
    return lax.ppermute(block, "dom", [(i, (i + by) % size) for i in range(size)])


def swap_z(block):
    return lax.ppermute(block, "rep", [(i, i ^ 1) for i in range(8)])


def shift_x(block, by):
    return lax.ppermute(block, "rep", [(i, (i + 2 * by) % 8) for i in range(8)])


def spread_x(pair):
    return [pair] + [shift_x(pair, -k) for k in (1, 2, 3)]


def send_x(blocks):
    return [blocks[0]] + [shift_x(blocks[k], k) for k in (1, 2, 3)]


def whole_of(shape):
    return pl.BlockSpec(shape, lambda: (0,) * len(shape))


def add_up(blocks, after, dtype):
    stacked = len(blocks) == 1
    shape = blocks[0].shape[1:] if stacked else blocks[0].shape

    def kernel(*refs):
        out = refs[-1]
        total = None
        if stacked:
            for i in range(blocks[0].shape[0]):
                part = refs[0][i].astype(f32)
                total = part if total is None else total + part
            total = total.astype(dtype)
        else:
            for ref in refs[: len(blocks)]:
                part = ref[...].astype(f32)
                total = part if total is None else total + part
            total = total.astype(dtype)
        out[...] = total

    return pl.pallas_call(
        kernel,
        in_specs=[whole_of(block.shape) for block in blocks] + [pl.BlockSpec(memory_space=pl.ANY)],
        out_specs=whole_of(shape),
        out_shape=jax.ShapeDtypeStruct(shape, dtype),
        compiler_params=pltpu.CompilerParams(vmem_limit_bytes=16 * MB),
        cost_estimate=cost(1),
        name="add_up",
    )(*blocks, after)


def split_sum(blocks, after):
    half = blocks[0].shape[0] // 2

    def kernel(*refs):
        for out, at in ((refs[-2], slice(0, half)), (refs[-1], slice(half, 2 * half))):
            total = None
            for ref in refs[: len(blocks)]:
                part = ref[at, :].astype(f32)
                total = part if total is None else total + part
            out[...] = total.astype(out.dtype)

    return pl.pallas_call(
        kernel,
        in_specs=[whole_of(block.shape) for block in blocks] + [pl.BlockSpec(memory_space=pl.ANY)],
        out_specs=[whole_of((half, D))] * 2,
        out_shape=[jax.ShapeDtypeStruct((half, D), f32), jax.ShapeDtypeStruct((half, D), bf16)],
        compiler_params=pltpu.CompilerParams(vmem_limit_bytes=16 * MB),
        cost_estimate=cost(1),
        name="split_sum",
    )(*blocks, after)


def turned(index):
    rep = lax.axis_index("rep")
    return ((index - PART * (rep // 2)) % ROWS) ^ (256 * (rep % 2))


def operator_step(total, accum):
    rows, width = total.shape
    mine = lax.dynamic_slice(accum.reshape(-1), (lax.axis_index("dom") * rows,), (rows,))
    fresh = mine + jnp.mean(total * total, -1)
    step = total / jnp.sqrt(fresh)[:, None]
    power = jnp.floor(jnp.log2(fresh))
    part = fresh * jnp.exp2(-power)
    high = lax.reduce_precision(part, 5, 10)
    code = jnp.pad(jnp.stack([power, high, part - high]), ((0, 5), (0, width - rows)))
    send = jnp.concatenate([step, code]).astype(jnp.float16)
    return jnp.broadcast_to(send, (16,) + send.shape)


def operator_update(shares, relation, accum):
    rows, width = shares.shape[1] - 8, shares.shape[2]
    cores = [[2 * i + c for i in range(16)] for c in range(2)]
    half = lax.all_to_all(shares, "dom", 0, 0, axis_index_groups=cores)
    other = lax.ppermute(half, "dom", [(i, i ^ 1) for i in range(32)])
    second = lax.axis_index("dom") % 2 == 1
    pairs = [jnp.where(second, other, half), jnp.where(second, half, other)]
    full = jnp.stack(pairs, 1).reshape(32, rows + 8, width).astype(f32)
    steps = full[:, :rows].reshape(relation.shape)
    power, high, low = (full[:, rows + i, :rows].reshape(accum.shape) for i in range(3))
    return relation - learn_rate * steps, (high + low) * jnp.exp2(power)


def pad_slots(index, fill):
    return jnp.pad(index.reshape(GROUPS, SLOTS), ((0, 0), (0, PAD - SLOTS)), constant_values=fill)


def source_stage(own, src_pad, rel_id, relation):
    return make_queries(own, src_pad.reshape(GROUPS, 1, PAD), rel_id, relation)


def target_stage(nxt, q, s, dst_pad, weights, rel_id, counts, kinds):
    rows = dst_pad.reshape(NCH // 2, 1, 2 * CH)
    out = score_side(nxt, q, s, rows, weights, rel_id, counts, kinds)
    return out[0], out[1 : PARTS + 1], out[PARTS + 1]


def back_stage(gq, src_pad, rel_id, relation):
    return source_side(gq, src_pad.reshape(GROUPS, 1, PAD), rel_id, relation)


def local_grads(own, nxt, relation, src_index, dst_index, neg_index, rel_id, counts):
    own, nxt = own.astype(bf16), nxt.astype(bf16)
    src_pad = pad_slots(src_index, -1)
    weights = neg_weights(pad_slots(neg_index, -1))
    own, nxt = (jnp.split(rows, PARTS) for rows in (own, nxt))
    s, q = source_stage(own, src_pad, rel_id, relation)
    gq, dst_grad, rel_grad = target_stage(
        nxt, q, s, pad_slots(dst_index, -1), weights, rel_id, counts, relation.shape[0]
    )
    src_grad = back_stage(gq, src_pad, rel_id, relation)
    return jnp.concatenate(src_grad), jnp.concatenate(dst_grad), rel_grad


def on_device(
    entity, entity_accum, relation, relation_accum, src_index, dst_index, neg_index, rel_id, counts
):
    ent_b = entity.astype(bf16)
    src_pad = pad_slots(turned(src_index), -1)
    dst_pad = pad_slots(turned(dst_index), -1)
    neg_pad = pad_slots(turned(neg_index), -1)
    other = swap_z(ent_b)
    own = spread_x(jnp.concatenate([ent_b, other]))
    nxt = [shift_dom(block, -1) for block in own]
    weights = neg_weights(neg_pad)
    s, q = source_stage(own, src_pad, rel_id, relation)
    gq, dst_grad, rel_grad = target_stage(
        nxt, q, s, dst_pad, weights, rel_id, counts, relation.shape[0]
    )
    dst_blocks = send_x(dst_grad)
    got = lax.all_to_all(rel_grad.reshape(32, -1, D), "dom", 0, 0)
    src_grad = back_stage(gq, src_pad, rel_id, relation)
    src_blocks = send_x(src_grad)
    mine = add_up([got], src_grad[0], f32)
    zsum = mine + swap_z(mine)
    dst_sum = add_up(dst_blocks, mine, bf16)
    moved = shift_dom(dst_sum, 1)
    src_sum = add_up(src_blocks + [moved], dst_sum, f32)
    total = add_up([zsum] + [shift_x(zsum, k) for k in (1, 2, 3)], src_sum, f32)
    shares = operator_step(total, relation_accum)
    relation_new, relation_accum_new = operator_update(shares, relation, relation_accum)
    keep, give = split_sum([src_sum], total)
    grads = keep + swap_z(give).astype(f32)
    entity_new, entity_accum_new = rowwise(entity, entity_accum, grads)
    return (entity_new, entity_accum_new, relation_new, relation_accum_new)


def solution(mesh):
    placed = (
        P(("dom", "rep"), None),
        P(("dom", "rep")),
        P(),
        P(),
        P(("dom", "rep")),
        P(("dom", "rep")),
        P(("dom", "rep"), None),
        P(("dom", "rep")),
        P(("dom", "rep")),
    )
    return jax.shard_map(
        on_device,
        mesh=mesh,
        in_specs=placed,
        out_specs=(P(("dom", "rep"), None), P(("dom", "rep")), P(), P()),
        check_vma=False,
    )
```

```python
import functools
import jax
import jax.numpy as jnp
from jax import lax
from jax.experimental import pallas as pl
from jax.experimental.pallas import tpu as pltpu
from jax.sharding import PartitionSpec as P

learn_rate = 0.1
LOG2E = 1.4426950408889634
GROUPS = 4
SLOTS = 1000
PAD = 1024
ROWS = 2048
D = 256
BLK = 256
NBLK = ROWS // BLK
CH = 512
NCH = GROUPS * PAD // CH
PER = PAD // CH
bf16 = jnp.bfloat16
f32 = jnp.float32

NN = (((1,), (0,)), ((), ()))
NT = (((1,), (1,)), ((), ()))
MB = 1024 * 1024


def mm(a, b, dims=NN):
    return lax.dot_general(a, b, dims, preferred_element_type=f32)


def cost(us):
    return pl.CostEstimate(flops=int(us * 5e8), bytes_accessed=int(us * 3.5e6), transcendentals=0)


def params(size):
    return pltpu.CompilerParams(
        dimension_semantics=("arbitrary",), vmem_limit_bytes=size * MB
    )


def one_hot(rows, index, first):
    return jnp.where(rows == (index - first).astype(jnp.int16), bf16(1), bf16(0))


PARTS = 4
PART = ROWS // PARTS


def part_specs():
    return [pl.BlockSpec((PART, D), lambda *_: (0, 0))] * PARTS


def send_shapes():
    return [pltpu.HBM((PART, D), bf16)] * PARTS


def block_of(parts, b):
    first = b * BLK % PART
    return parts[b * BLK // PART][first : first + BLK, :]


def count_kernel(neg_ref, out_ref):
    rows = lax.broadcasted_iota(jnp.int32, (BLK, 128), 0).astype(jnp.int16)
    for b in range(NBLK):
        hits = None
        for c in range(0, PAD, 128):
            hot = one_hot(rows, neg_ref[0, :, c : c + 128], b * BLK)
            hits = hot if hits is None else hits + hot
        count = jnp.sum(hits.astype(f32), axis=1, keepdims=True)
        lane = lax.broadcasted_iota(jnp.int32, (BLK, 8), 1)
        out_ref[0, :, b * BLK : (b + 1) * BLK] = jnp.where(lane == 0, count, count + 1.0).T
    out_ref[0] = jnp.log2(out_ref[0])


def neg_weights(neg_pad):
    return pl.pallas_call(
        count_kernel,
        grid=(GROUPS,),
        in_specs=[pl.BlockSpec((1, 1, PAD), lambda g: (g, 0, 0))],
        out_specs=pl.BlockSpec((1, 8, ROWS), lambda g: (g, 0, 0)),
        out_shape=jax.ShapeDtypeStruct((GROUPS, 8, ROWS), f32),
        compiler_params=params(8),
        cost_estimate=cost(3),
        name="neg_weights",
    )(neg_pad.reshape(GROUPS, 1, PAD))


def query_kernel(rel_ref, *refs):
    own = refs[:PARTS]
    idx_ref, mat_ref, s_ref, q_ref = refs[PARTS:]
    column = jnp.broadcast_to(idx_ref[0].astype(f32), (128, PAD)).T
    column = column.astype(jnp.int32).astype(jnp.int16)
    cols = lax.broadcasted_iota(jnp.int32, (PAD, 128), 1).astype(jnp.int16)
    acc = None
    for b in range(NBLK):
        hot = jnp.concatenate(
            [
                jnp.where(cols + jnp.int16(first) == column, bf16(1), bf16(0))
                for first in (b * BLK, b * BLK + 128)
            ],
            axis=1,
        )
        part = mm(hot, block_of(own, b))
        acc = part if acc is None else acc + part
    rows = acc.astype(bf16)
    s_ref[...] = rows
    q_ref[...] = mm(mat_ref[0].astype(bf16).T, rows, NT).astype(bf16)


def make_queries(own, src_rows, rel_id, relation):
    return pl.pallas_call(
        query_kernel,
        grid_spec=pltpu.PrefetchScalarGridSpec(
            num_scalar_prefetch=1,
            grid=(GROUPS,),
            in_specs=[
                *part_specs(),
                pl.BlockSpec((1, 1, PAD), lambda j, rel: (j, 0, 0)),
                pl.BlockSpec((1, D, D), lambda j, rel: (rel[j], 0, 0)),
            ],
            out_specs=[
                pl.BlockSpec((PAD, D), lambda j, rel: (j, 0)),
                pl.BlockSpec((D, PAD), lambda j, rel: (0, j)),
            ],
        ),
        out_shape=[
            jax.ShapeDtypeStruct((GROUPS * PAD, D), bf16),
            jax.ShapeDtypeStruct((D, GROUPS * PAD), bf16),
        ],
        compiler_params=params(20),
        cost_estimate=cost(9),
        name="queries",
    )(rel_id, *own, src_rows, relation)


SUB = 32


def score_kernel(rel_ref, cnt_ref, *refs):
    nxt = refs[:PARTS]
    q_ref, s_ref, dst_ref, wt_ref, gq_ref = refs[PARTS : PARTS + 5]
    dg = refs[PARTS + 5 : 2 * PARTS + 5]
    rg_ref, sc, nxt_t_ref, *halves, dacc, wcol, racc = refs[
        2 * PARTS + 5 :
    ]
    old = halves[0::2], halves[1::2]
    g = pl.program_id(0)
    rows = lax.broadcasted_iota(jnp.int32, (SUB, CH), 0)
    rows16 = lax.broadcasted_iota(jnp.int32, (BLK, CH), 0).astype(jnp.int16)

    @pl.when(g == 0)
    def _():
        dacc[...] = jnp.zeros_like(dacc)
        racc[...] = jnp.zeros_like(racc)
        for ref in old[1]:
            ref[...] = jnp.zeros_like(ref)
        for b in range(NBLK):
            nxt_t_ref[:, b * BLK : (b + 1) * BLK] = block_of(nxt, b).T

    def spread(b, w, qs, sl, gain, dst):
        at = slice(b * BLK, (b + 1) * BLK)
        mask = rows16 == (dst[0:1, :] - b * BLK).astype(jnp.int16)
        full = jnp.where(mask, gain[0:1, :].astype(bf16), w[at, :])
        dacc[at, :] += mm(full, qs[...], NT)
        return mm(nxt_t_ref[:, at], full)

    def finish(acc, sl, chunk):
        gq = (acc * sl[0:1, :]).astype(bf16)
        gq_ref[:, pl.ds(pl.multiple_of(chunk * CH, CH), CH)] = gq

    def stage(half, chunk_old):
        w, qs, sl, gain_ref, dst_keep = old[half]
        before = old[1 - half]
        here = slice(half * CH, (half + 1) * CH)
        chunk = 2 * g + half
        group = chunk // PER
        for b in range(NBLK):
            at = slice(b * BLK, (b + 1) * BLK)
            wcol[at, :] = wt_ref[group, :, at].T
        q = q_ref[:, here]
        dst = dst_ref[0, 0:1, here]
        acc = None
        top = jnp.full((8, CH), -jnp.inf, f32)
        hit = jnp.zeros((8, CH), f32)
        for b in range(NBLK):
            raw = mm(block_of(nxt, b), q)
            for i in range(BLK // SUB):
                at = slice(b * BLK + i * SUB, b * BLK + (i + 1) * SUB)
                mask = rows == dst - (b * BLK + i * SUB)
                val = raw[i * SUB : (i + 1) * SUB] * LOG2E + jnp.where(
                    mask, wcol[at, 1:2], wcol[at, 0:1]
                )
                sc[at, :] = val
                top = jnp.maximum(top, jnp.max(val.reshape(SUB // 8, 8, CH), axis=0))
                hit = hit + jnp.sum(jnp.where(mask, val, 0.0).reshape(SUB // 8, 8, CH), axis=0)
            part = spread(b, *before)
            acc = part if acc is None else acc + part
        finish(acc, before[2], chunk_old)
        top = jnp.max(top, axis=0, keepdims=True)
        hit = jnp.sum(hit, axis=0, keepdims=True)
        tot = jnp.zeros((8, CH), f32)
        for b in range(NBLK):
            for i in range(BLK // SUB):
                at = slice(b * BLK + i * SUB, b * BLK + (i + 1) * SUB)
                e = jnp.exp2(sc[at, :] - top)
                tot = tot + jnp.sum(e.reshape(SUB // 8, 8, CH), axis=0)
                w[at, :] = e.astype(bf16)
        tot = jnp.sum(tot, axis=0, keepdims=True)
        gain_ref[...] = jnp.broadcast_to(jnp.exp2(hit - top) - tot, (8, CH))
        dst_keep[...] = jnp.broadcast_to(dst, (8, CH))
        lane = lax.broadcasted_iota(jnp.int32, (1, CH), 1) + lax.rem(chunk, PER) * CH
        live = jnp.logical_and(lane < SLOTS, group * SLOTS + lane < cnt_ref[0])
        scale = jnp.where(live, 1.0 / tot, 0.0)
        sl[...] = jnp.broadcast_to(scale, (8, CH))
        qs[...] = (q.astype(f32) * scale).astype(bf16)

    stage(0, jnp.maximum(2 * g - 1, 0))
    stage(1, 2 * g)

    @pl.when(g == NCH // 2 - 1)
    def _():
        acc = None
        for b in range(NBLK):
            part = spread(b, *old[1])
            acc = part if acc is None else acc + part
        finish(acc, old[1][2], 2 * g + 1)
        for k in range(GROUPS):
            at = slice(k * PAD, (k + 1) * PAD)
            racc[rel_ref[k]] += mm(gq_ref[:, at], s_ref[at, :])
        for k in range(racc.shape[0]):
            rg_ref[k] = racc[k].T.astype(bf16)
        for p in range(PARTS):
            dg[p][...] = dacc[p * PART : (p + 1) * PART, :].astype(bf16)


def score_side(nxt, q, s, dst_rows, weights, rel_id, counts, kinds):
    return pl.pallas_call(
        score_kernel,
        grid_spec=pltpu.PrefetchScalarGridSpec(
            num_scalar_prefetch=2,
            grid=(NCH // 2,),
            in_specs=[
                *part_specs(),
                pl.BlockSpec((D, 2 * CH), lambda j, rel, cnt: (0, j)),
                pl.BlockSpec((GROUPS * PAD, D), lambda j, rel, cnt: (0, 0)),
                pl.BlockSpec((1, 1, 2 * CH), lambda j, rel, cnt: (j, 0, 0)),
                pl.BlockSpec((GROUPS, 8, ROWS), lambda j, rel, cnt: (0, 0, 0)),
            ],
            out_specs=[
                pl.BlockSpec((D, GROUPS * PAD), lambda j, rel, cnt: (0, 0)),
                *[pl.BlockSpec((PART, D), lambda j, rel, cnt: (0, 0))] * PARTS,
                pl.BlockSpec((kinds, D, D), lambda j, rel, cnt: (0, 0, 0)),
            ],
            scratch_shapes=[
                pltpu.VMEM((ROWS, CH), f32),
                pltpu.VMEM((D, ROWS), bf16),
                *[pltpu.VMEM((ROWS, CH), bf16)] * 2,
                *[pltpu.VMEM((D, CH), bf16)] * 2,
                *[pltpu.VMEM((8, CH), f32)] * 4,
                *[pltpu.VMEM((8, CH), jnp.int32)] * 2,
                pltpu.VMEM((ROWS, D), f32),
                pltpu.VMEM((ROWS, 8), f32),
                pltpu.VMEM((kinds, D, D), f32),
            ],
        ),
        out_shape=[
            pltpu.HBM((D, GROUPS * PAD), bf16),
            *send_shapes(),
            jax.ShapeDtypeStruct((kinds, D, D), bf16),
        ],
        compiler_params=params(34),
        cost_estimate=cost(28),
        name="scores",
    )(rel_id, counts, *nxt, q, s, dst_rows, weights)


def source_kernel(rel_ref, gq_ref, src_ref, mat_ref, *refs):
    out, acc = refs[:PARTS], refs[PARTS]
    g = pl.program_id(0)

    @pl.when(g == 0)
    def _():
        acc[...] = jnp.zeros_like(acc)

    grad = mm(mat_ref[0].astype(bf16), gq_ref[...]).astype(bf16)
    rows = lax.broadcasted_iota(jnp.int32, (BLK, PAD), 0).astype(jnp.int16)
    for b in range(NBLK):
        at = slice(b * BLK, (b + 1) * BLK)
        acc[at, :] += mm(one_hot(rows, src_ref[0], b * BLK), grad, NT)

    @pl.when(g == GROUPS - 1)
    def _():
        for p in range(PARTS):
            out[p][...] = acc[p * PART : (p + 1) * PART, :].astype(bf16)


def source_side(gq, src_rows, rel_id, relation):
    return pl.pallas_call(
        source_kernel,
        grid_spec=pltpu.PrefetchScalarGridSpec(
            num_scalar_prefetch=1,
            grid=(GROUPS,),
            in_specs=[
                pl.BlockSpec((D, PAD), lambda j, rel: (0, j)),
                pl.BlockSpec((1, 1, PAD), lambda j, rel: (j, 0, 0)),
                pl.BlockSpec((1, D, D), lambda j, rel: (rel[j], 0, 0)),
            ],
            out_specs=[pl.BlockSpec((PART, D), lambda j, rel: (0, 0))] * PARTS,
            scratch_shapes=[pltpu.VMEM((ROWS, D), f32)],
        ),
        out_shape=send_shapes(),
        compiler_params=params(16),
        cost_estimate=cost(8),
        name="source_grads",
    )(rel_id, gq, src_rows, relation)


def rowwise(param, accum, grad):
    fresh = accum + jnp.mean(grad * grad, -1)
    return (param - learn_rate * grad / jnp.sqrt(fresh)[..., None], fresh)


def shift_dom(block, by):
    size = lax.axis_size("dom")
    return lax.ppermute(block, "dom", [(i, (i + by) % size) for i in range(size)])


def swap_z(block):
    return lax.ppermute(block, "rep", [(i, i ^ 1) for i in range(8)])


def shift_x(block, by):
    return lax.ppermute(block, "rep", [(i, (i + 2 * by) % 8) for i in range(8)])


def spread_x(pair):
    return [pair] + [shift_x(pair, -k) for k in (1, 2, 3)]


def send_x(blocks):
    return [blocks[0]] + [shift_x(blocks[k], k) for k in (1, 2, 3)]


def add_up(blocks, after, dtype, copies=None):
    stacked = len(blocks) == 1
    shape = blocks[0].shape[1:] if stacked else blocks[0].shape
    whole = pl.BlockSpec(memory_space=pltpu.VMEM)

    def kernel(*refs):
        out = refs[-1]
        total = None
        if stacked:
            for i in range(blocks[0].shape[0]):
                part = refs[0][i].astype(f32)
                total = part if total is None else total + part
            total = total.astype(dtype)
        else:
            for ref in refs[: len(blocks)]:
                part = ref[...].astype(f32)
                total = part if total is None else total + part
            total = total.astype(dtype)
        if copies is None:
            out[...] = total
        else:
            for i in range(copies):
                out[i] = total

    return pl.pallas_call(
        kernel,
        in_specs=[whole] * len(blocks) + [pl.BlockSpec(memory_space=pl.ANY)],
        out_specs=whole,
        out_shape=jax.ShapeDtypeStruct(shape if copies is None else (copies,) + shape, dtype),
        compiler_params=pltpu.CompilerParams(vmem_limit_bytes=16 * MB),
        cost_estimate=cost(1),
        name="add_up",
    )(*blocks, after)


def split_sum(blocks, after):
    half = blocks[0].shape[0] // 2
    whole = pl.BlockSpec(memory_space=pltpu.VMEM)

    def kernel(*refs):
        for out, at in ((refs[-2], slice(0, half)), (refs[-1], slice(half, 2 * half))):
            total = None
            for ref in refs[: len(blocks)]:
                part = ref[at, :].astype(f32)
                total = part if total is None else total + part
            out[...] = total.astype(out.dtype)

    return pl.pallas_call(
        kernel,
        in_specs=[whole] * len(blocks) + [pl.BlockSpec(memory_space=pl.ANY)],
        out_specs=[whole] * 2,
        out_shape=[jax.ShapeDtypeStruct((half, D), f32), jax.ShapeDtypeStruct((half, D), bf16)],
        compiler_params=pltpu.CompilerParams(vmem_limit_bytes=16 * MB),
        cost_estimate=cost(1),
        name="split_sum",
    )(*blocks, after)


def turned(index):
    rep = lax.axis_index("rep")
    return ((index - PART * (rep // 2)) % ROWS) ^ (256 * (rep % 2))


def operator_step(total, accum):
    rows, width = total.shape
    mine = lax.dynamic_slice(accum.reshape(-1), (lax.axis_index("dom") * rows,), (rows,))
    fresh = mine + jnp.mean(total * total, -1)
    step = total / jnp.sqrt(fresh)[:, None]
    power = jnp.floor(jnp.log2(fresh))
    part = fresh * jnp.exp2(-power)
    high = lax.reduce_precision(part, 5, 10)
    code = jnp.pad(jnp.stack([power, high, part - high]), ((0, 5), (0, width - rows)))
    send = jnp.concatenate([step, code]).astype(jnp.float16)
    return jnp.broadcast_to(send, (16,) + send.shape)


def operator_update(shares, relation, accum):
    rows, width = shares.shape[1] - 8, shares.shape[2]
    cores = [[2 * i + c for i in range(16)] for c in range(2)]
    half = lax.all_to_all(shares, "dom", 0, 0, axis_index_groups=cores)
    other = lax.ppermute(half, "dom", [(i, i ^ 1) for i in range(32)])
    second = lax.axis_index("dom") % 2 == 1
    pairs = [jnp.where(second, other, half), jnp.where(second, half, other)]
    full = jnp.stack(pairs, 1).reshape(32, rows + 8, width).astype(f32)
    steps = full[:, :rows].reshape(relation.shape)
    power, high, low = (full[:, rows + i, :rows].reshape(accum.shape) for i in range(3))
    return relation - learn_rate * steps, (high + low) * jnp.exp2(power)


def pad_slots(index, fill):
    return jnp.pad(index.reshape(GROUPS, SLOTS), ((0, 0), (0, PAD - SLOTS)), constant_values=fill)


def source_stage(own, src_pad, rel_id, relation):
    return make_queries(own, src_pad.reshape(GROUPS, 1, PAD), rel_id, relation)


def target_stage(nxt, q, s, dst_pad, weights, rel_id, counts, kinds):
    rows = dst_pad.reshape(NCH // 2, 1, 2 * CH)
    out = score_side(nxt, q, s, rows, weights, rel_id, counts, kinds)
    return out[0], out[1 : PARTS + 1], out[PARTS + 1]


def back_stage(gq, src_pad, rel_id, relation):
    return source_side(gq, src_pad.reshape(GROUPS, 1, PAD), rel_id, relation)


def local_grads(own, nxt, relation, src_index, dst_index, neg_index, rel_id, counts):
    own, nxt = own.astype(bf16), nxt.astype(bf16)
    src_pad = pad_slots(src_index, -1)
    weights = neg_weights(pad_slots(neg_index, -1))
    own, nxt = (jnp.split(rows, PARTS) for rows in (own, nxt))
    s, q = source_stage(own, src_pad, rel_id, relation)
    gq, dst_grad, rel_grad = target_stage(
        nxt, q, s, pad_slots(dst_index, -1), weights, rel_id, counts, relation.shape[0]
    )
    src_grad = back_stage(gq, src_pad, rel_id, relation)
    return jnp.concatenate(src_grad), jnp.concatenate(dst_grad), rel_grad


def on_device(
    entity, entity_accum, relation, relation_accum, src_index, dst_index, neg_index, rel_id, counts
):
    ent_b = entity.astype(bf16)
    src_pad = pad_slots(turned(src_index), -1)
    dst_pad = pad_slots(turned(dst_index), -1)
    neg_pad = pad_slots(turned(neg_index), -1)
    other = swap_z(ent_b)
    own = spread_x(jnp.concatenate([ent_b, other]))
    nxt = [shift_dom(block, -1) for block in own]
    weights = neg_weights(neg_pad)
    s, q = source_stage(own, src_pad, rel_id, relation)
    gq, dst_grad, rel_grad = target_stage(
        nxt, q, s, dst_pad, weights, rel_id, counts, relation.shape[0]
    )
    dst_blocks = send_x(dst_grad)
    got = lax.all_to_all(rel_grad.reshape(32, -1, D), "dom", 0, 0)
    src_grad = back_stage(gq, src_pad, rel_id, relation)
    src_blocks = send_x(src_grad)
    mine = add_up([got], src_grad[0], f32)
    zsum = mine + swap_z(mine)
    dst_sum = add_up(dst_blocks, mine, bf16)
    moved = shift_dom(dst_sum, 1)
    src_sum = add_up(src_blocks + [moved], dst_sum, f32)
    total = add_up([zsum] + [shift_x(zsum, k) for k in (1, 2, 3)], src_sum, f32)
    shares = operator_step(total, relation_accum)
    relation_new, relation_accum_new = operator_update(shares, relation, relation_accum)
    keep, give = split_sum([src_sum], total)
    grads = keep + swap_z(give).astype(f32)
    entity_new, entity_accum_new = rowwise(entity, entity_accum, grads)
    return (entity_new, entity_accum_new, relation_new, relation_accum_new)


def solution(mesh):
    placed = (
        P(("dom", "rep"), None),
        P(("dom", "rep")),
        P(),
        P(),
        P(("dom", "rep")),
        P(("dom", "rep")),
        P(("dom", "rep"), None),
        P(("dom", "rep")),
        P(("dom", "rep")),
    )
    return jax.shard_map(
        on_device,
        mesh=mesh,
        in_specs=placed,
        out_specs=(P(("dom", "rep"), None), P(("dom", "rep")), P(), P()),
        check_vma=False,
    )
```

```python
import functools
import jax
import jax.numpy as jnp
from jax import lax
from jax.experimental import pallas as pl
from jax.experimental.pallas import tpu as pltpu
from jax.sharding import PartitionSpec as P

learn_rate = 0.1
LOG2E = 1.4426950408889634
GROUPS = 4
SLOTS = 1000
PAD = 1024
ROWS = 2048
D = 256
BLK = 256
NBLK = ROWS // BLK
CH = 512
NCH = GROUPS * PAD // CH
PER = PAD // CH
bf16 = jnp.bfloat16
f32 = jnp.float32

NN = (((1,), (0,)), ((), ()))
NT = (((1,), (1,)), ((), ()))
MB = 1024 * 1024


def mm(a, b, dims=NN):
    return lax.dot_general(a, b, dims, preferred_element_type=f32)


def cost(us):
    return pl.CostEstimate(flops=int(us * 5e8), bytes_accessed=int(us * 3.5e6), transcendentals=0)


def params(size):
    return pltpu.CompilerParams(
        dimension_semantics=("arbitrary",), vmem_limit_bytes=size * MB
    )


def one_hot(rows, index, first):
    return jnp.where(rows == (index - first).astype(jnp.int16), bf16(1), bf16(0))


PARTS = 4
PART = ROWS // PARTS


def part_specs():
    return [pl.BlockSpec((PART, D), lambda *_: (0, 0))] * PARTS


def send_shapes():
    return [jax.ShapeDtypeStruct((PART, D), bf16)] + [pltpu.HBM((PART, D), bf16)] * (PARTS - 1)


def block_of(parts, b):
    first = b * BLK % PART
    return parts[b * BLK // PART][first : first + BLK, :]


def count_kernel(neg_ref, out_ref):
    rows = lax.broadcasted_iota(jnp.int32, (BLK, 128), 0).astype(jnp.int16)
    for b in range(NBLK):
        hits = None
        for c in range(0, PAD, 128):
            hot = one_hot(rows, neg_ref[0, :, c : c + 128], b * BLK)
            hits = hot if hits is None else hits + hot
        count = jnp.sum(hits.astype(f32), axis=1, keepdims=True)
        lane = lax.broadcasted_iota(jnp.int32, (BLK, 8), 1)
        out_ref[0, :, b * BLK : (b + 1) * BLK] = jnp.where(lane == 0, count, count + 1.0).T
    out_ref[0] = jnp.log2(out_ref[0])


def neg_weights(neg_pad):
    return pl.pallas_call(
        count_kernel,
        grid=(GROUPS,),
        in_specs=[pl.BlockSpec((1, 1, PAD), lambda g: (g, 0, 0))],
        out_specs=pl.BlockSpec((1, 8, ROWS), lambda g: (g, 0, 0)),
        out_shape=jax.ShapeDtypeStruct((GROUPS, 8, ROWS), f32),
        compiler_params=params(8),
        cost_estimate=cost(3),
        name="neg_weights",
    )(neg_pad.reshape(GROUPS, 1, PAD))


def query_kernel(rel_ref, *refs):
    own = refs[:PARTS]
    idx_ref, mat_ref, s_ref, q_ref = refs[PARTS:]
    column = jnp.broadcast_to(idx_ref[0].astype(f32), (128, PAD)).T
    column = column.astype(jnp.int32).astype(jnp.int16)
    cols = lax.broadcasted_iota(jnp.int32, (PAD, 128), 1).astype(jnp.int16)
    acc = None
    for b in range(NBLK):
        hot = jnp.concatenate(
            [
                jnp.where(cols + jnp.int16(first) == column, bf16(1), bf16(0))
                for first in (b * BLK, b * BLK + 128)
            ],
            axis=1,
        )
        part = mm(hot, block_of(own, b))
        acc = part if acc is None else acc + part
    rows = acc.astype(bf16)
    s_ref[...] = rows
    q_ref[...] = mm(mat_ref[0].astype(bf16).T, rows, NT).astype(bf16)


def make_queries(own, src_rows, rel_id, relation):
    return pl.pallas_call(
        query_kernel,
        grid_spec=pltpu.PrefetchScalarGridSpec(
            num_scalar_prefetch=1,
            grid=(GROUPS,),
            in_specs=[
                *part_specs(),
                pl.BlockSpec((1, 1, PAD), lambda j, rel: (j, 0, 0)),
                pl.BlockSpec((1, D, D), lambda j, rel: (rel[j], 0, 0)),
            ],
            out_specs=[
                pl.BlockSpec((PAD, D), lambda j, rel: (j, 0)),
                pl.BlockSpec((D, PAD), lambda j, rel: (0, j)),
            ],
        ),
        out_shape=[
            jax.ShapeDtypeStruct((GROUPS * PAD, D), bf16),
            jax.ShapeDtypeStruct((D, GROUPS * PAD), bf16),
        ],
        compiler_params=params(20),
        cost_estimate=cost(9),
        name="queries",
    )(rel_id, *own, src_rows, relation)


SUB = 32


def score_kernel(rel_ref, cnt_ref, *refs):
    nxt = refs[:PARTS]
    q_ref, s_ref, dst_ref, wt_ref, gq_ref = refs[PARTS : PARTS + 5]
    dg = refs[PARTS + 5 : 2 * PARTS + 5]
    rg_ref, sc, nxt_t_ref, *halves, dacc, wcol, racc = refs[
        2 * PARTS + 5 :
    ]
    old = halves[0::2], halves[1::2]
    g = pl.program_id(0)
    rows = lax.broadcasted_iota(jnp.int32, (SUB, CH), 0)
    rows16 = lax.broadcasted_iota(jnp.int32, (BLK, CH), 0).astype(jnp.int16)

    @pl.when(g == 0)
    def _():
        dacc[...] = jnp.zeros_like(dacc)
        racc[...] = jnp.zeros_like(racc)
        for ref in old[1]:
            ref[...] = jnp.zeros_like(ref)
        for b in range(NBLK):
            nxt_t_ref[:, b * BLK : (b + 1) * BLK] = block_of(nxt, b).T

    def spread(b, w, qs, sl, gain, dst):
        at = slice(b * BLK, (b + 1) * BLK)
        mask = rows16 == (dst[0:1, :] - b * BLK).astype(jnp.int16)
        full = jnp.where(mask, gain[0:1, :].astype(bf16), w[at, :])
        dacc[at, :] += mm(full, qs[...], NT)
        return mm(nxt_t_ref[:, at], full)

    def finish(acc, sl, chunk):
        gq = (acc * sl[0:1, :]).astype(bf16)
        gq_ref[:, pl.ds(pl.multiple_of(chunk * CH, CH), CH)] = gq

    def stage(half, chunk_old):
        w, qs, sl, gain_ref, dst_keep = old[half]
        before = old[1 - half]
        here = slice(half * CH, (half + 1) * CH)
        chunk = 2 * g + half
        group = chunk // PER
        for b in range(NBLK):
            at = slice(b * BLK, (b + 1) * BLK)
            wcol[at, :] = wt_ref[group, :, at].T
        q = q_ref[:, here]
        dst = dst_ref[0, 0:1, here]
        acc = None
        top = jnp.full((8, CH), -jnp.inf, f32)
        hit = jnp.zeros((8, CH), f32)
        for b in range(NBLK):
            raw = mm(block_of(nxt, b), q)
            for i in range(BLK // SUB):
                at = slice(b * BLK + i * SUB, b * BLK + (i + 1) * SUB)
                mask = rows == dst - (b * BLK + i * SUB)
                val = raw[i * SUB : (i + 1) * SUB] * LOG2E + jnp.where(
                    mask, wcol[at, 1:2], wcol[at, 0:1]
                )
                sc[at, :] = val
                top = jnp.maximum(top, jnp.max(val.reshape(SUB // 8, 8, CH), axis=0))
                hit = hit + jnp.sum(jnp.where(mask, val, 0.0).reshape(SUB // 8, 8, CH), axis=0)
            part = spread(b, *before)
            acc = part if acc is None else acc + part
        finish(acc, before[2], chunk_old)
        top = jnp.max(top, axis=0, keepdims=True)
        hit = jnp.sum(hit, axis=0, keepdims=True)
        tot = jnp.zeros((8, CH), f32)
        for b in range(NBLK):
            for i in range(BLK // SUB):
                at = slice(b * BLK + i * SUB, b * BLK + (i + 1) * SUB)
                e = jnp.exp2(sc[at, :] - top)
                tot = tot + jnp.sum(e.reshape(SUB // 8, 8, CH), axis=0)
                w[at, :] = e.astype(bf16)
        tot = jnp.sum(tot, axis=0, keepdims=True)
        gain_ref[...] = jnp.broadcast_to(jnp.exp2(hit - top) - tot, (8, CH))
        dst_keep[...] = jnp.broadcast_to(dst, (8, CH))
        lane = lax.broadcasted_iota(jnp.int32, (1, CH), 1) + lax.rem(chunk, PER) * CH
        live = jnp.logical_and(lane < SLOTS, group * SLOTS + lane < cnt_ref[0])
        scale = jnp.where(live, 1.0 / tot, 0.0)
        sl[...] = jnp.broadcast_to(scale, (8, CH))
        qs[...] = (q.astype(f32) * scale).astype(bf16)

    stage(0, jnp.maximum(2 * g - 1, 0))
    stage(1, 2 * g)

    @pl.when(g == NCH // 2 - 1)
    def _():
        acc = None
        for b in range(NBLK):
            part = spread(b, *old[1])
            acc = part if acc is None else acc + part
        finish(acc, old[1][2], 2 * g + 1)
        for k in range(GROUPS):
            at = slice(k * PAD, (k + 1) * PAD)
            racc[rel_ref[k]] += mm(gq_ref[:, at], s_ref[at, :])
        for k in range(racc.shape[0]):
            rg_ref[k] = racc[k].T.astype(bf16)
        for p in range(PARTS):
            dg[p][...] = dacc[p * PART : (p + 1) * PART, :].astype(bf16)


def score_side(nxt, q, s, dst_rows, weights, rel_id, counts, kinds):
    return pl.pallas_call(
        score_kernel,
        grid_spec=pltpu.PrefetchScalarGridSpec(
            num_scalar_prefetch=2,
            grid=(NCH // 2,),
            in_specs=[
                *part_specs(),
                pl.BlockSpec((D, 2 * CH), lambda j, rel, cnt: (0, j)),
                pl.BlockSpec((GROUPS * PAD, D), lambda j, rel, cnt: (0, 0)),
                pl.BlockSpec((1, 1, 2 * CH), lambda j, rel, cnt: (j, 0, 0)),
                pl.BlockSpec((GROUPS, 8, ROWS), lambda j, rel, cnt: (0, 0, 0)),
            ],
            out_specs=[
                pl.BlockSpec((D, GROUPS * PAD), lambda j, rel, cnt: (0, 0)),
                *[pl.BlockSpec((PART, D), lambda j, rel, cnt: (0, 0))] * PARTS,
                pl.BlockSpec((kinds, D, D), lambda j, rel, cnt: (0, 0, 0)),
            ],
            scratch_shapes=[
                pltpu.VMEM((ROWS, CH), f32),
                pltpu.VMEM((D, ROWS), bf16),
                *[pltpu.VMEM((ROWS, CH), bf16)] * 2,
                *[pltpu.VMEM((D, CH), bf16)] * 2,
                *[pltpu.VMEM((8, CH), f32)] * 4,
                *[pltpu.VMEM((8, CH), jnp.int32)] * 2,
                pltpu.VMEM((ROWS, D), f32),
                pltpu.VMEM((ROWS, 8), f32),
                pltpu.VMEM((kinds, D, D), f32),
            ],
        ),
        out_shape=[
            pltpu.HBM((D, GROUPS * PAD), bf16),
            *send_shapes(),
            jax.ShapeDtypeStruct((kinds, D, D), bf16),
        ],
        compiler_params=params(34),
        cost_estimate=cost(28),
        name="scores",
    )(rel_id, counts, *nxt, q, s, dst_rows, weights)


def source_kernel(rel_ref, gq_ref, src_ref, mat_ref, *refs):
    out, acc = refs[:PARTS], refs[PARTS]
    g = pl.program_id(0)

    @pl.when(g == 0)
    def _():
        acc[...] = jnp.zeros_like(acc)

    grad = mm(mat_ref[0].astype(bf16), gq_ref[...]).astype(bf16)
    rows = lax.broadcasted_iota(jnp.int32, (BLK, PAD), 0).astype(jnp.int16)
    for b in range(NBLK):
        at = slice(b * BLK, (b + 1) * BLK)
        acc[at, :] += mm(one_hot(rows, src_ref[0], b * BLK), grad, NT)

    @pl.when(g == GROUPS - 1)
    def _():
        for p in range(PARTS):
            out[p][...] = acc[p * PART : (p + 1) * PART, :].astype(bf16)


def source_side(gq, src_rows, rel_id, relation):
    return pl.pallas_call(
        source_kernel,
        grid_spec=pltpu.PrefetchScalarGridSpec(
            num_scalar_prefetch=1,
            grid=(GROUPS,),
            in_specs=[
                pl.BlockSpec((D, PAD), lambda j, rel: (0, j)),
                pl.BlockSpec((1, 1, PAD), lambda j, rel: (j, 0, 0)),
                pl.BlockSpec((1, D, D), lambda j, rel: (rel[j], 0, 0)),
            ],
            out_specs=[pl.BlockSpec((PART, D), lambda j, rel: (0, 0))] * PARTS,
            scratch_shapes=[pltpu.VMEM((ROWS, D), f32)],
        ),
        out_shape=send_shapes(),
        compiler_params=params(16),
        cost_estimate=cost(8),
        name="source_grads",
    )(rel_id, gq, src_rows, relation)


def rowwise(param, accum, grad):
    fresh = accum + jnp.mean(grad * grad, -1)
    return (param - learn_rate * grad / jnp.sqrt(fresh)[..., None], fresh)


def shift_dom(block, by):
    size = lax.axis_size("dom")
    return lax.ppermute(block, "dom", [(i, (i + by) % size) for i in range(size)])


def swap_z(block):
    return lax.ppermute(block, "rep", [(i, i ^ 1) for i in range(8)])


def shift_x(block, by):
    return lax.ppermute(block, "rep", [(i, (i + 2 * by) % 8) for i in range(8)])


def spread_x(pair):
    return [pair] + [shift_x(pair, -k) for k in (1, 2, 3)]


def send_x(blocks):
    return [blocks[0]] + [shift_x(blocks[k], k) for k in (1, 2, 3)]


def add_up(blocks, after, dtype, copies=None):
    stacked = len(blocks) == 1
    shape = blocks[0].shape[1:] if stacked else blocks[0].shape
    whole = pl.BlockSpec(memory_space=pltpu.VMEM)

    def kernel(*refs):
        out = refs[-1]
        total = None
        if stacked:
            for i in range(blocks[0].shape[0]):
                part = refs[0][i].astype(f32)
                total = part if total is None else total + part
            total = total.astype(dtype)
        else:
            for ref in refs[: len(blocks)]:
                part = ref[...].astype(f32)
                total = part if total is None else total + part
            total = total.astype(dtype)
        if copies is None:
            out[...] = total
        else:
            for i in range(copies):
                out[i] = total

    return pl.pallas_call(
        kernel,
        in_specs=[whole] * len(blocks) + [pl.BlockSpec(memory_space=pl.ANY)],
        out_specs=whole,
        out_shape=jax.ShapeDtypeStruct(shape if copies is None else (copies,) + shape, dtype),
        compiler_params=pltpu.CompilerParams(vmem_limit_bytes=16 * MB),
        cost_estimate=cost(1),
        name="add_up",
    )(*blocks, after)


def split_sum(blocks, after):
    half = blocks[0].shape[0] // 2
    whole = pl.BlockSpec(memory_space=pltpu.VMEM)

    def kernel(*refs):
        for out, at in ((refs[-2], slice(0, half)), (refs[-1], slice(half, 2 * half))):
            total = None
            for ref in refs[: len(blocks)]:
                part = ref[at, :].astype(f32)
                total = part if total is None else total + part
            out[...] = total.astype(out.dtype)

    return pl.pallas_call(
        kernel,
        in_specs=[whole] * len(blocks) + [pl.BlockSpec(memory_space=pl.ANY)],
        out_specs=[whole] * 2,
        out_shape=[jax.ShapeDtypeStruct((half, D), f32), jax.ShapeDtypeStruct((half, D), bf16)],
        compiler_params=pltpu.CompilerParams(vmem_limit_bytes=16 * MB),
        cost_estimate=cost(1),
        name="split_sum",
    )(*blocks, after)


def turned(index):
    rep = lax.axis_index("rep")
    return ((index - PART * (rep // 2)) % ROWS) ^ (256 * (rep % 2))


def operator_step(total, accum):
    rows, width = total.shape
    mine = lax.dynamic_slice(accum.reshape(-1), (lax.axis_index("dom") * rows,), (rows,))
    fresh = mine + jnp.mean(total * total, -1)
    step = total / jnp.sqrt(fresh)[:, None]
    power = jnp.floor(jnp.log2(fresh))
    part = fresh * jnp.exp2(-power)
    high = lax.reduce_precision(part, 5, 10)
    code = jnp.pad(jnp.stack([power, high, part - high]), ((0, 5), (0, width - rows)))
    send = jnp.concatenate([step, code]).astype(jnp.float16)
    return jnp.broadcast_to(send, (16,) + send.shape)


def operator_update(shares, relation, accum):
    rows, width = shares.shape[1] - 8, shares.shape[2]
    cores = [[2 * i + c for i in range(16)] for c in range(2)]
    half = lax.all_to_all(shares, "dom", 0, 0, axis_index_groups=cores)
    other = lax.ppermute(half, "dom", [(i, i ^ 1) for i in range(32)])
    second = lax.axis_index("dom") % 2 == 1
    pairs = [jnp.where(second, other, half), jnp.where(second, half, other)]
    full = jnp.stack(pairs, 1).reshape(32, rows + 8, width).astype(f32)
    steps = full[:, :rows].reshape(relation.shape)
    power, high, low = (full[:, rows + i, :rows].reshape(accum.shape) for i in range(3))
    return relation - learn_rate * steps, (high + low) * jnp.exp2(power)


def pad_slots(index, fill):
    return jnp.pad(index.reshape(GROUPS, SLOTS), ((0, 0), (0, PAD - SLOTS)), constant_values=fill)


def source_stage(own, src_pad, rel_id, relation):
    return make_queries(own, src_pad.reshape(GROUPS, 1, PAD), rel_id, relation)


def target_stage(nxt, q, s, dst_pad, weights, rel_id, counts, kinds):
    rows = dst_pad.reshape(NCH // 2, 1, 2 * CH)
    out = score_side(nxt, q, s, rows, weights, rel_id, counts, kinds)
    return out[0], out[1 : PARTS + 1], out[PARTS + 1]


def back_stage(gq, src_pad, rel_id, relation):
    return source_side(gq, src_pad.reshape(GROUPS, 1, PAD), rel_id, relation)


def local_grads(own, nxt, relation, src_index, dst_index, neg_index, rel_id, counts):
    own, nxt = own.astype(bf16), nxt.astype(bf16)
    src_pad = pad_slots(src_index, -1)
    weights = neg_weights(pad_slots(neg_index, -1))
    own, nxt = (jnp.split(rows, PARTS) for rows in (own, nxt))
    s, q = source_stage(own, src_pad, rel_id, relation)
    gq, dst_grad, rel_grad = target_stage(
        nxt, q, s, pad_slots(dst_index, -1), weights, rel_id, counts, relation.shape[0]
    )
    src_grad = back_stage(gq, src_pad, rel_id, relation)
    return jnp.concatenate(src_grad), jnp.concatenate(dst_grad), rel_grad


def on_device(
    entity, entity_accum, relation, relation_accum, src_index, dst_index, neg_index, rel_id, counts
):
    ent_b = entity.astype(bf16)
    src_pad = pad_slots(turned(src_index), -1)
    dst_pad = pad_slots(turned(dst_index), -1)
    neg_pad = pad_slots(turned(neg_index), -1)
    other = swap_z(ent_b)
    own = spread_x(jnp.concatenate([ent_b, other]))
    nxt = [shift_dom(block, -1) for block in own]
    weights = neg_weights(neg_pad)
    s, q = source_stage(own, src_pad, rel_id, relation)
    gq, dst_grad, rel_grad = target_stage(
        nxt, q, s, dst_pad, weights, rel_id, counts, relation.shape[0]
    )
    dst_blocks = send_x(dst_grad)
    got = lax.all_to_all(rel_grad.reshape(32, -1, D), "dom", 0, 0)
    src_grad = back_stage(gq, src_pad, rel_id, relation)
    src_blocks = send_x(src_grad)
    mine = add_up([got], src_grad[0], f32)
    zsum = mine + swap_z(mine)
    dst_sum = add_up(dst_blocks, mine, bf16)
    moved = shift_dom(dst_sum, 1)
    src_sum = add_up(src_blocks + [moved], dst_sum, f32)
    total = add_up([zsum] + [shift_x(zsum, k) for k in (1, 2, 3)], src_sum, f32)
    shares = operator_step(total, relation_accum)
    relation_new, relation_accum_new = operator_update(shares, relation, relation_accum)
    keep, give = split_sum([src_sum], total)
    grads = add_up([keep, swap_z(give)], relation_new, f32)
    entity_new, entity_accum_new = rowwise(entity, entity_accum, grads)
    return (entity_new, entity_accum_new, relation_new, relation_accum_new)


def solution(mesh):
    placed = (
        P(("dom", "rep"), None),
        P(("dom", "rep")),
        P(),
        P(),
        P(("dom", "rep")),
        P(("dom", "rep")),
        P(("dom", "rep"), None),
        P(("dom", "rep")),
        P(("dom", "rep")),
    )
    return jax.shard_map(
        on_device,
        mesh=mesh,
        in_specs=placed,
        out_specs=(P(("dom", "rep"), None), P(("dom", "rep")), P(), P()),
        check_vma=False,
    )
```
